128 devices in a mesh: region: 16 (over z, x), dom: 8 (over y, core).
Axes of the slice: x: 4, y: 4, z: 4, core: 2. Of those that a mesh axis runs over, the one named last changes fastest.
Arguments:
- slave_disp: float32 [12, 2097152], P(None, ('region', 'dom')), may hold values from -4 to 4
- slave_normal: float32 [3, 2097152], P(None, ('region', 'dom')), may hold values from -6 to 6
- gap_zero: float32 [4, 2097152], P(None, ('region', 'dom')), may hold values from -6 to 6
- quad_weight: float32 [4, 2097152], P(None, ('region', 'dom')), may hold values from 0.1 to 1
- proj_coord: float32 [8, 2097152], P(None, ('region', 'dom')), may hold values from -1 to 1
- multiplier: float32 [4, 2097152], P(None, ('region', 'dom')), may hold values from 0 to 2
- active: int32 [4, 2097152], P(None, ('region', 'dom')), may hold values 0 or 1
- pair_owner: int32 [2097152, 1], P(('region', 'dom')), may hold values from 0 to 127; in each aligned block of 16384 rows (0 to 16383, 16384 to 32767, ...) at most 256 rows name the same one
- pair_slot: int32 [2097152], P(('region', 'dom')), may hold values from 0 to 4095
- master_vol: float32 [12, 524288], P(None, ('region', 'dom')), may hold values from -4 to 4
- surf_pick: int32 [128, 4096], P(('region', 'dom')), may hold values from 0 to 4095, each once within a row
Outputs:
- weighted_gap: float32 [4, 2097152], P(None, ('region', 'dom'))
- multiplier_new: float32 [4, 2097152], P(None, ('region', 'dom'))
- master_force: float32 [12, 524288], P(None, ('region', 'dom'))
The draws below stay inside these ranges and needn't reach their ends.
Inputs may be any that keep to these rules, and one draw needn't show every extreme that they name: `pair_owner`: among the 16384 rows of one device no owner is named more than 256 times, a bound that some block reaches. `surf_pick`: each row is a permutation of 0 to 4095.
All inputs are finite; a program needn't handle non-finite values. No bound on the sum of `active` on one device may be relied on, other than what follows from the above.
Results may differ from the reference program's by a relative error of at most 0.0003.
Values sent between devices are 32-bit elements; how exact they have to be, the bound alone decides.
No kernel may reach another device: no remote copies, remote signals or barrier semaphores. Data moves between devices by JAX's collectives and lax.ppermute only.
A program may use at most 128 MiB of HBM per device.

```python
import math
import jax
import jax.numpy as jnp
import numpy as np

S_DEV = 16384
M_DEV = 4096
OWNERS = 128
CAP = 256
SLAVES = 2097152
MASTERS = 524288
N_REGION = 16
N_DOM = 8


def with_ends(values, key, smallest, high):
    shape = values.shape
    spot = [jax.random.randint(jax.random.fold_in(key, axis), (), 0, shape[axis]) for axis in range(len(shape))]
    values = values.at[tuple(spot)].set(smallest)
    longest = shape.index(max(shape))
    spot[longest] = (spot[longest] + 1) % shape[longest]
    return values.at[tuple(spot)].set(high)


def levels(key, dims, cuts, least, top_value):
    gain = 1.0
    for axis_at, blocks in cuts:
        draws = jax.random.uniform(jax.random.fold_in(jax.random.fold_in(key, 6), axis_at), (blocks,), jnp.float32, least / len(cuts), top_value / len(cuts))
        gain = gain * jnp.repeat(jnp.exp(draws), dims[axis_at] // blocks).reshape((-1,) + (1,) * (len(dims) - 1 - axis_at))
    return gain


def routed_block(rng, own, number, rows, count, top, bound, lean):
    order = jax.random.permutation(rng, count)
    packed, ordinary = portions_of(count, rows * top, bound, lean, True), portions_of(count, rows * top, bound, lean, False)
    places = jnp.arange(count)

    def named(sizes, turn):
        used = int((sizes > 0).sum())
        fixed = max(1, used // 4)
        shifted = fixed + (places - fixed + turn * (used - fixed)) % max(1, count - fixed)
        return jnp.zeros((count,), jnp.int32).at[order[jnp.where(places < fixed, places, shifted)]].set(jnp.asarray(sizes, jnp.int32))

    sizes = jnp.where(number % 4 == 0, named(packed, number // 4), named(ordinary, number - number // 4 - 1))
    mixed = jax.random.permutation(jax.random.fold_in(own, 3), count)
    donor, receiver = mixed[0:count // 2 * 2:2], mixed[1:count // 2 * 2:2]
    room = jnp.minimum(sizes[donor] - 1, bound - sizes[receiver]) // 2
    room = jnp.where((donor == order[0]) | (receiver == order[0]) | (sizes[receiver] == 0), 0, jnp.maximum(room, 0))
    shifted = jax.random.randint(jax.random.fold_in(own, 4), (count // 2,), 0, 1 << 20) % (room + 1)
    sizes = sizes.at[donor].add(-shifted).at[receiver].add(shifted)
    members = jnp.searchsorted(jnp.cumsum(sizes), jnp.arange(rows * top), side="right").astype(jnp.int32)
    grid = members.reshape(top, rows).T
    grid = grid[jax.random.permutation(jax.random.fold_in(own, 1), rows)]
    turn = jax.random.randint(jax.random.fold_in(own, 2), (rows, 1), 0, top)
    return jnp.take_along_axis(grid, (jnp.arange(top)[None, :] + turn) % top, axis=1)


def portions_of(amount, total, most, lean, full):
    weights = [(1 << 20) // math.isqrt(standing ** lean) + 1 for standing in range(1, amount + 1)]
    largest = most if full else min(most, max(-(-total // amount), total * weights[0] // sum(weights)))
    least = 1 if total - largest >= amount - 1 else 0
    counts, surplus = [largest] + [least] * (amount - 1), total - largest - least * (amount - 1)
    while surplus > 0:
        movable = [i for i in range(1, amount) if counts[i] < largest] or [i for i in range(1, amount) if counts[i] < most]
        pool, left = sum([weights[i] for i in movable]), surplus
        for i in movable:
            addition = min(most - counts[i], max(1, left * weights[i] // pool), surplus)
            counts[i] = counts[i] + addition
            surplus = surplus - addition
    return np.array(counts)


def noise(stream_key, dims, scale, limit, shards=(), held_as=jnp.bfloat16):
    values = scale * jax.random.normal(stream_key, dims, jnp.float32)
    if shards:
        values = values * levels(stream_key, dims, shards, -0.22, 0.18)
    return jnp.clip(values, -limit, limit).astype(held_as)


def setup_inputs(seed: int = 0) -> dict:
    seeds = jax.random.split(jax.random.key(seed), 12)
    slave_disp = noise(seeds[0], (12, SLAVES), 0.5, 4.0, ((1, 128),), jnp.float32)
    slave_normal = noise(seeds[1], (3, SLAVES), 1.0, 6.0, ((1, 128),), jnp.float32)
    gap_zero = noise(seeds[2], (4, SLAVES), 1.0, 6.0, ((1, 128),), jnp.float32)
    quad_weight = jnp.clip(jnp.exp(math.log(1.0) - 2.3025851 * jax.random.uniform(seeds[3], (4, SLAVES), jnp.float32) ** levels(seeds[3], (4, SLAVES), ((1, 128),), -0.2, 0.2)), 0.1, 1.0)
    proj_coord = jnp.clip(jax.random.uniform(seeds[4], (8, SLAVES), jnp.float32, -1.0, 1.0) * levels(seeds[4], (8, SLAVES), ((1, 128),), -0.4, 0.0), -1.0, 1.0)
    multiplier = jnp.clip(2.0 * jax.random.uniform(seeds[5], (4, SLAVES), jnp.float32) ** levels(seeds[5], (4, SLAVES), ((1, 128),), -0.2, 0.2), 0.0, 2.0)
    active = with_ends((jax.random.randint(seeds[6], (4, SLAVES), 0, 4) < 3).astype(jnp.int32), jax.random.fold_in(seeds[6], 1), 0, 1)
    pair_owner_keys = jax.random.split(jax.random.fold_in(seeds[7], 1), SLAVES // S_DEV)
    pair_owner_turns = jax.random.permutation(jax.random.fold_in(seeds[7], 3), SLAVES // S_DEV)
    pair_owner = jax.vmap(lambda own, number: routed_block(jax.random.fold_in(seeds[7], 2), own, number, S_DEV, OWNERS, 1, CAP, 2))(pair_owner_keys, pair_owner_turns).reshape((SLAVES, 1))
    pair_slot = with_ends(jax.random.randint(seeds[8], (SLAVES,), 0, M_DEV), jax.random.fold_in(seeds[8], 1), 0, M_DEV - 1).astype(jnp.int32)
    master_vol = noise(seeds[9], (12, MASTERS), 0.5, 4.0, ((1, 128),), jnp.float32)
    surf_pick = jax.vmap(lambda own: jax.random.permutation(own, M_DEV))(jax.random.split(seeds[10], OWNERS)).reshape((OWNERS, M_DEV)).astype(jnp.int32)
    return dict(slave_disp=slave_disp, slave_normal=slave_normal, gap_zero=gap_zero, quad_weight=quad_weight, proj_coord=proj_coord, multiplier=multiplier, active=active, pair_owner=pair_owner, pair_slot=pair_slot, master_vol=master_vol, surf_pick=surf_pick)


gauss_point = 1.0 / math.sqrt(3.0)
node_xs = [-1.0, 1.0, 1.0, -1.0]
node_ys = [-1.0, -1.0, 1.0, 1.0]
point_xs = [-gauss_point, gauss_point, gauss_point, -gauss_point]
point_ys = [-gauss_point, -gauss_point, gauss_point, gauss_point]
slave_table = [[(1.0 + node_xs[c] * point_xs[q]) * (1.0 + node_ys[c] * point_ys[q]) * 0.25 for q in range(4)] for c in range(4)]

def master_shapes(proj_coord):
    result = []
    for q in range(4):
        first = proj_coord[2 * q]
        second = proj_coord[2 * q + 1]
        result.append([(1.0 + node_xs[c] * first) * (1.0 + node_ys[c] * second) * 0.25 for c in range(4)])
    return result

def normal_part(normal, displace):
    return [normal[0] * displace[3 * c] + normal[1] * displace[3 * c + 1] + normal[2] * displace[3 * c + 2] for c in range(4)]

def mortar_term(proj_coord, normal, weight, master_disp):
    shapes = master_shapes(proj_coord)
    along = normal_part(normal, master_disp)
    points = []
    for q in range(4):
        total = shapes[q][0] * along[0]
        for c in range(1, 4):
            total = total + shapes[q][c] * along[c]
        points.append(weight[q] * total)
    result = []
    for a in range(4):
        total = slave_table[a][0] * points[0]
        for q in range(1, 4):
            total = total + slave_table[a][q] * points[q]
        result.append(total)
    return jnp.stack(result)

def slave_term(slave_disp, normal, gap_zero, weight):
    along = normal_part(normal, slave_disp)
    points = []
    for q in range(4):
        total = gap_zero[q]
        for b in range(4):
            total = total + slave_table[b][q] * along[b]
        points.append(weight[q] * total)
    result = []
    for a in range(4):
        total = slave_table[a][0] * points[0]
        for q in range(1, 4):
            total = total + slave_table[a][q] * points[q]
        result.append(total)
    return jnp.stack(result)

def force_term(proj_coord, normal, weight, lagrange):
    shapes = master_shapes(proj_coord)
    coeff = []
    for q in range(4):
        total = slave_table[0][q] * lagrange[0]
        for a in range(1, 4):
            total = total + slave_table[a][q] * lagrange[a]
        coeff.append(weight[q] * total)
    result = []
    for c in range(4):
        total = shapes[0][c] * coeff[0]
        for q in range(1, 4):
            total = total + shapes[q][c] * coeff[q]
        for j in range(3):
            result.append(total * normal[j])
    return jnp.stack(result)

def reference(slave_disp, slave_normal, gap_zero, quad_weight, proj_coord, multiplier, active, pair_owner, pair_slot, master_vol, surf_pick):
    volume = master_vol.reshape(12, OWNERS, M_DEV)
    local = jnp.take_along_axis(volume, surf_pick[None, :, :], axis=2)
    blocks = local.reshape(12, N_REGION, N_DOM, N_DOM, M_DEV // N_DOM)
    master_surf = jnp.swapaxes(blocks, 2, 3).reshape(12, OWNERS * M_DEV)
    target_row = (pair_owner[:, 0] * M_DEV + pair_slot).astype(jnp.int32)
    master_disp = jnp.take(master_surf, target_row, axis=1)
    mortar = mortar_term(proj_coord, slave_normal, quad_weight, master_disp)
    slave_part = slave_term(slave_disp, slave_normal, gap_zero, quad_weight)
    weighted_gap = slave_part - mortar
    multiplier_new = jnp.where(active == 1, jnp.maximum(multiplier - weighted_gap, 0.0), 0.0).astype(jnp.float32)
    force = force_term(proj_coord, slave_normal, quad_weight, multiplier_new)
    surf_force = jnp.zeros((12, OWNERS * M_DEV), jnp.float32).at[:, target_row].add(force)
    back_blocks = surf_force.reshape(12, N_REGION, N_DOM, N_DOM, M_DEV // N_DOM)
    back_local = jnp.swapaxes(back_blocks, 2, 3).reshape(12, OWNERS, M_DEV)
    owner_index = jnp.broadcast_to(jnp.arange(OWNERS, dtype=jnp.int32)[:, None], (OWNERS, M_DEV))
    master_force = jnp.zeros((12, OWNERS, M_DEV), jnp.float32).at[:, owner_index, surf_pick].set(back_local)
    return (weighted_gap, multiplier_new, master_force.reshape(12, OWNERS * M_DEV))
```

```python
import functools
import math

import jax
import jax.numpy as jnp
from jax import lax
from jax.experimental import pallas as pl
from jax.experimental.pallas import tpu as pltpu
from jax.sharding import PartitionSpec as P

gauss_point = 1.0 / math.sqrt(3.0)
node_xs = [-1.0, 1.0, 1.0, -1.0]
node_ys = [-1.0, -1.0, 1.0, 1.0]
point_xs = [-gauss_point, gauss_point, gauss_point, -gauss_point]
point_ys = [-gauss_point, -gauss_point, gauss_point, gauss_point]
slave_table = [
    [(1.0 + node_xs[c] * point_xs[q]) * (1.0 + node_ys[c] * point_ys[q]) * 0.25 for q in range(4)]
    for c in range(4)
]

BF = jnp.bfloat16
F32 = jnp.float32
LANE = 256

NN = (((1,), (0,)), ((), ()))
NT = (((1,), (1,)), ((), ()))


def sub_iota(rows, cols):
    return lax.broadcasted_iota(jnp.int32, (rows, cols), 0)


def split(values):
    high = values.astype(BF)
    return high, (values - high.astype(F32)).astype(BF)


def onehot(index, size):
    n = index.shape[1]
    base = (jnp.broadcast_to(index, (16, n)) - sub_iota(16, n)).astype(F32).astype(BF)
    one, zero = jnp.ones((16, n), BF), jnp.zeros((16, n), BF)
    return jnp.concatenate(
        [jnp.where(base == jnp.asarray(16 * g, BF), one, zero) for g in range(size // 16)], axis=0
    )


def spread(index, values, group, count):
    n = index.shape[1]
    base = (jnp.broadcast_to(index, (16, n)) - sub_iota(16, n) // (16 // group)).astype(F32).astype(BF)
    zero = jnp.zeros((16, n), BF)
    return [
        [jnp.where(base == jnp.asarray(group * g, BF), v, zero) for g in range(count // group)]
        for v in values
    ]


def fill_table(rows, table):
    lows = rows.shape[1] // LANE
    parts = [rows[0:8, l * LANE : (l + 1) * LANE] for l in range(lows)]
    parts += [rows[8:12, l * LANE : (l + 1) * LANE] for l in range(lows)]
    high, low = split(jnp.concatenate(parts, axis=0))
    table[0 : 12 * lows, :] = high
    table[12 * lows :, :] = low


def pick_table(table, index, lows):
    n = index.shape[1]
    grabbed = lax.dot_general(table, onehot(index % LANE, LANE), NN, preferred_element_type=F32)
    total = 12 * lows
    low = jnp.broadcast_to(index // LANE, (8, n))
    pair = low - sub_iota(8, n) // 4
    first = jnp.zeros((8, n), F32)
    for l in range(lows):
        at = 8 * l
        value = grabbed[at : at + 8] + grabbed[total + at : total + at + 8]
        first = jnp.where(low == l, value, first)
    second = jnp.zeros((8, n), F32)
    for l in range(lows // 2):
        at = 8 * lows + 8 * l
        value = grabbed[at : at + 8] + grabbed[total + at : total + at + 8]
        second = jnp.where(pair == 2 * l, value, second)
    return first, second[0:4] + second[4:8]


def add_table(first, second, index, lows):
    high, low = split(first)
    group = jnp.concatenate([high.astype(F32), low.astype(F32)], axis=0).astype(BF)
    wide = spread(index // LANE, [group], 1, lows)[0]
    high, low = split(second)
    high, low = high.astype(F32), low.astype(F32)
    group = jnp.concatenate([high, low, high, low], axis=0).astype(BF)
    narrow = spread(index // LANE, [group], 2, lows)[0]
    stacked = jnp.concatenate(wide + narrow, axis=0)
    return lax.dot_general(
        stacked, onehot(index % LANE, LANE), NT, preferred_element_type=F32
    )


def table_part(total, lows, l):
    first = total[16 * l : 16 * l + 8] + total[16 * l + 8 : 16 * l + 16]
    at = 16 * lows + 8 * l
    return first, total[at : at + 4] + total[at + 4 : at + 8]


def pick_kernel(vol, pick, out, table):
    width = vol.shape[1]
    lows = width // LANE
    rows = vol[...]
    fill_table(
        jnp.concatenate([rows[3 * c + j : 3 * c + j + 1] for j in range(3) for c in range(4)], axis=0),
        table,
    )
    count, _, part = out.shape
    for k in range(count):
        first, second = pick_table(table[...], pick[:, k * part : (k + 1) * part], lows)
        out[k, 0:8, :] = first
        out[k, 8:12, :] = second


def owner_pairs(values):
    left = values[:, 0:128].reshape(-1, 8, 128)
    right = values[:, 128:256].reshape(-1, 8, 128)
    sub = lax.broadcasted_iota(jnp.int32, left.shape, 1)
    even = jnp.where(sub < 4, left, pltpu.roll(right, 4, 1))
    odd = jnp.where(sub < 4, pltpu.roll(left, 4, 1), right)
    return even, odd


def owner_rows(even, odd):
    sub = lax.broadcasted_iota(jnp.int32, even.shape, 1)
    left = jnp.where(sub < 4, even, pltpu.roll(odd, 4, 1)).reshape(-1, 128)
    right = jnp.where(sub < 4, pltpu.roll(even, 4, 1), odd).reshape(-1, 128)
    return jnp.concatenate([left, right], axis=1)


def slot_terms(values, owner, rank, owners):
    high, low = split(jnp.concatenate([values] * 4, axis=0))
    first, second = spread(owner, [high, low], 4, owners)
    stacked = jnp.concatenate(first + second, axis=0)
    return lax.dot_general(stacked, onehot(rank, LANE), NT, preferred_element_type=F32)


def store_slots(total, out):
    half = total.shape[0] // 2
    even, odd = owner_pairs(total[0:half, :] + total[half:, :])
    out[:, 0] = even
    out[:, 1] = odd


def request_kernel(step, owner, slot, normal, out, rank, total):
    count = owner.shape[1]
    owners = 2 * out.shape[0]
    row = sub_iota(256, 512)
    col = lax.broadcasted_iota(jnp.int32, (256, 512), 1)
    upper = ((row <= col) | (col >= 256)).astype(F32).astype(BF)

    def ranks(i, base):
        for u in range(4):
            lanes = pl.ds(pl.multiple_of(i * 1024 + u * 256, 256), 256)
            named = onehot(owner[:, lanes], owners)
            sums = lax.dot_general(named, upper, NN, preferred_element_type=F32)
            seen = named.astype(F32) * (sums[:, 0:256] + base)
            rank[:, lanes] = (jnp.sum(seen, axis=0, keepdims=True) - 1.0).astype(jnp.int32)
            base = base + sums[:, 256:512]
        return base

    lax.fori_loop(0, count // 1024, ranks, jnp.zeros((owners, 256), F32))
    total[...] = jnp.zeros_like(total)

    def slots(i, _):
        lanes = pl.ds(pl.multiple_of(i * step, step), step)
        values = jnp.concatenate([slot[:, lanes].astype(F32), normal[:, lanes]], axis=0)
        total[...] += slot_terms(values, owner[:, lanes], rank[:, lanes], owners)
        return 0

    lax.fori_loop(0, count // step, slots, 0)
    store_slots(total[...], out)


def along_kernel(group, surf, recv, out, table):
    lows = surf.shape[0] * surf.shape[2] // LANE
    fill_table(jnp.concatenate([surf[s] for s in range(surf.shape[0])], axis=1), table)

    def step(i, _):
        parts = [recv[i * group + u] for u in range(group)]
        block = jnp.concatenate([p[4 * h : 4 * h + 4] for p in parts for h in range(2)], axis=1)
        index = block[0:1].astype(jnp.int32)
        first, second = pick_table(table[...], index, lows)
        along = first[0:4] * block[1:2] + first[4:8] * block[2:3] + second * block[3:4]
        for u in range(group):
            for h in range(2):
                at = (2 * u + h) * 128
                out[i * group + u, 4 * h : 4 * h + 4, :] = along[:, at : at + 128]
        return 0

    lax.fori_loop(0, recv.shape[0] // group, step, 0)


def signs(xs, inner):
    sub = sub_iota(8, 1)

    def column(number):
        value = jnp.full((8, 1), xs[3], F32)
        for c in range(3):
            value = jnp.where(number == c, xs[c], value)
        return value

    return [column(sub % 4)] * 2 if inner else [column(sub // 4), column(sub // 4 + 2)]


def local_kernel(step, disp, normal, gap, weight, proj, toward, back, part):
    count = disp.shape[1]
    sub4 = sub_iota(4, 1)

    def column(xs):
        value = jnp.full((4, 1), xs[3], F32)
        for a in range(3):
            value = jnp.where(sub4 == a, xs[a], value)
        return value

    def body(i, _):
        lanes = pl.ds(pl.multiple_of(i * step, step), step)
        p, w, d, n, g = proj[:, lanes], weight[:, lanes], disp[:, lanes], normal[:, lanes], gap[:, lanes]
        for inner, out in ((False, toward), (True, back)):
            node_x, node_y = signs(node_xs, inner), signs(node_ys, inner)
            sums = [None, None]
            for q in range(4):
                table = signs([slave_table[a][q] * 0.25 for a in range(4)], not inner)
                first = jnp.broadcast_to(p[2 * q : 2 * q + 1], (8, step))
                second = jnp.broadcast_to(p[2 * q + 1 : 2 * q + 2], (8, step))
                along = jnp.broadcast_to(w[q : q + 1], (8, step))
                for h in range(2):
                    term = (1.0 + node_x[h] * first) * (1.0 + node_y[h] * second) * (along * table[h])
                    sums[h] = term if q == 0 else sums[h] + term
            out[0:8, lanes] = sums[0]
            out[8:16, lanes] = sums[1]
        total = g
        for b in range(4):
            along = n[0:1] * d[3 * b : 3 * b + 1] + n[1:2] * d[3 * b + 1 : 3 * b + 2] + n[2:3] * d[3 * b + 2 : 3 * b + 3]
            total = total + column(slave_table[b]) * along
        points = w * total
        result = column([slave_table[a][0] for a in range(4)]) * points[0:1]
        for q in range(1, 4):
            result = result + column([slave_table[a][q] for a in range(4)]) * points[q : q + 1]
        part[:, lanes] = result
        return 0

    lax.fori_loop(0, count // step, body, 0)


def doubled(values):
    n = values.shape[1]
    rows = [jnp.broadcast_to(values[c : c + 1], (4, n)) for c in range(4)]
    return jnp.concatenate(rows[0:2], axis=0), jnp.concatenate(rows[2:4], axis=0)


def combine(factors, values):
    one, two = doubled(values)
    both = factors[0:8] * one + factors[8:16] * two
    return both[0:4] + both[4:8]


def update_kernel(step, owner, rank, recv, toward, back, part, multiplier, active, gap_out, new_out, out, table, total):
    count = owner.shape[1]
    owners = 2 * out.shape[0]
    half = owners * 4
    high, low = split(owner_rows(recv[:, 0], recv[:, 1]))
    table[0:half, :] = high
    table[half:, :] = low
    total[...] = jnp.zeros_like(total)

    def body(i, _):
        lanes = pl.ds(pl.multiple_of(i * step, step), step)
        names, places = owner[:, lanes], rank[:, lanes]
        grabbed = lax.dot_general(table[...], onehot(places, LANE), NN, preferred_element_type=F32)
        base = jnp.broadcast_to(names, (8, step)) - sub_iota(8, step) // 4
        along = jnp.zeros((8, step), F32)
        for g in range(owners // 2):
            value = grabbed[8 * g : 8 * g + 8] + grabbed[half + 8 * g : half + 8 * g + 8]
            along = jnp.where(base == 2 * g, value, along)
        mortar = combine(toward[:, lanes], along[0:4] + along[4:8])
        weighted = part[:, lanes] - mortar
        lagrange = jnp.where(active[:, lanes] == 1, jnp.maximum(multiplier[:, lanes] - weighted, 0.0), 0.0)
        gap_out[:, lanes] = weighted
        new_out[:, lanes] = lagrange
        total[...] += slot_terms(combine(back[:, lanes], lagrange), names, places, owners)
        return 0

    lax.fori_loop(0, count // step, body, 0)
    store_slots(total[...], out)


def force_kernel(group, recv, factor, out, total):
    lows = out.shape[0] * out.shape[2] // LANE
    total[...] = jnp.zeros_like(total)

    def step(i, _):
        parts = [recv[i * group + u] for u in range(group)]
        block = jnp.concatenate([p[4 * h : 4 * h + 4] for p in parts for h in range(2)], axis=1)
        parts = [factor[i * group + u] for u in range(group)]
        node = jnp.concatenate([p[4 * h : 4 * h + 4] for p in parts for h in range(2)], axis=1)
        index = block[0:1].astype(jnp.int32)
        first = jnp.concatenate([node * block[1:2], node * block[2:3]], axis=0)
        total[...] += add_table(first, node * block[3:4], index, lows)
        return 0

    lax.fori_loop(0, recv.shape[0] // group, step, 0)
    sums = total[...]
    per = out.shape[2] // LANE
    for l in range(lows):
        first, second = table_part(sums, lows, l)
        lanes = slice(l % per * LANE, (l % per + 1) * LANE)
        out[l // per, 0:8, lanes] = first
        out[l // per, 8:12, lanes] = second


def place_kernel(moved, pick, out):
    lows = out.shape[1] // LANE
    rows = jnp.concatenate([moved[k] for k in range(moved.shape[0])], axis=1)
    sums = add_table(rows[0:8], rows[8:12], pick[...], lows)
    for l in range(lows):
        first, second = table_part(sums, lows, l)
        both = jnp.concatenate([first, second], axis=0)
        ordered = jnp.concatenate(
            [both[4 * j + c : 4 * j + c + 1] for c in range(4) for j in range(3)], axis=0
        )
        out[:, l * LANE : (l + 1) * LANE] = ordered


def call(kernel, outs, scratch, cycles, *args):
    vmem = pl.BlockSpec(memory_space=pltpu.VMEM)
    size = sum(a.size * 4 for a in args) + sum(math.prod(o[0]) * 4 for o in outs)
    result = pl.pallas_call(
        kernel,
        out_shape=[jax.ShapeDtypeStruct(*o) for o in outs],
        in_specs=[vmem] * len(args),
        out_specs=[vmem] * len(outs),
        scratch_shapes=[pltpu.VMEM(*s) for s in scratch],
        compiler_params=pltpu.CompilerParams(vmem_limit_bytes=48 * 2**20),
        cost_estimate=pl.CostEstimate(flops=cycles, bytes_accessed=size, transcendentals=0),
    )(*args)
    return result[0] if len(outs) == 1 else result


def on_device(
    slave_disp,
    slave_normal,
    gap_zero,
    quad_weight,
    proj_coord,
    multiplier,
    active,
    pair_owner,
    pair_slot,
    master_vol,
    surf_pick,
):
    region_count = lax.axis_size("region")
    dom_count = lax.axis_size("dom")
    owners = region_count * dom_count
    count = slave_disp.shape[1]
    width = master_vol.shape[1]
    lows = width // LANE
    part = width // dom_count
    step = 1024
    exchange = functools.partial(lax.all_to_all, split_axis=0, concat_axis=0, tiled=True)
    owner = pair_owner.reshape(1, count)
    slots = (owners // 2, 2, 8, 128)
    flat = (owners, 8, 128)
    everyone = ("region", "dom")

    picked = call(
        pick_kernel, [((dom_count, 12, part), F32)], [((24 * lows, LANE), BF)], 4 * 10**9, master_vol, surf_pick
    )
    surf = exchange(picked, "dom")
    request, rank = call(
        functools.partial(request_kernel, step),
        [(slots, F32), ((1, count), jnp.int32)],
        [((8 * owners, LANE), F32)],
        10**10,
        owner,
        pair_slot.reshape(1, count),
        slave_normal,
    )
    recv = exchange(request.reshape(flat), everyone)
    toward, back, slave_part = call(
        functools.partial(local_kernel, 512),
        [((16, count), F32), ((16, count), F32), ((4, count), F32)],
        [],
        10**9,
        slave_disp,
        slave_normal,
        gap_zero,
        quad_weight,
        proj_coord,
    )
    along = call(
        functools.partial(along_kernel, 4), [(flat, F32)], [((24 * lows, LANE), BF)], 10**10, surf, recv
    )
    returned = exchange(along, everyone)
    weighted_gap, multiplier_new, terms = call(
        functools.partial(update_kernel, step),
        [((4, count), F32), ((4, count), F32), (slots, F32)],
        [((8 * owners, LANE), BF), ((8 * owners, LANE), F32)],
        2 * 10**10,
        owner,
        rank,
        returned.reshape(slots),
        toward,
        back,
        slave_part,
        multiplier,
        active,
    )
    factor = exchange(terms.reshape(flat), everyone)
    forces = call(
        functools.partial(force_kernel, 4),
        [((dom_count, 12, part), F32)],
        [((24 * lows, LANE), F32)],
        10**10,
        recv,
        factor,
    )
    moved = exchange(forces, "dom")
    master_force = call(place_kernel, [((12, width), F32)], [], 10**9, moved, surf_pick)
    return (weighted_gap, multiplier_new, master_force)


def solution(mesh):
    both = ("region", "dom")
    return jax.shard_map(
        on_device,
        mesh=mesh,
        in_specs=(P(None, both),) * 7 + (P(both, None), P(both), P(None, both), P(both, None)),
        out_specs=(P(None, both),) * 3,
        check_vma=False,
    )
```

```python
import functools
import math

import jax
import jax.numpy as jnp
from jax import lax
from jax.experimental import pallas as pl
from jax.experimental.pallas import tpu as pltpu
from jax.sharding import PartitionSpec as P

gauss_point = 1.0 / math.sqrt(3.0)
node_xs = [-1.0, 1.0, 1.0, -1.0]
node_ys = [-1.0, -1.0, 1.0, 1.0]
point_xs = [-gauss_point, gauss_point, gauss_point, -gauss_point]
point_ys = [-gauss_point, -gauss_point, gauss_point, gauss_point]
slave_table = [
    [(1.0 + node_xs[c] * point_xs[q]) * (1.0 + node_ys[c] * point_ys[q]) * 0.25 for q in range(4)]
    for c in range(4)
]

BF = jnp.bfloat16
F32 = jnp.float32
LANE = 256

NN = (((1,), (0,)), ((), ()))
NT = (((1,), (1,)), ((), ()))


def sub_iota(rows, cols):
    return lax.broadcasted_iota(jnp.int32, (rows, cols), 0)


def split(values):
    high = values.astype(BF)
    return high, (values - high.astype(F32)).astype(BF)


def onehot(index, size):
    n = index.shape[1]
    base = (jnp.broadcast_to(index, (16, n)) - sub_iota(16, n)).astype(F32).astype(BF)
    one, zero = jnp.ones((16, n), BF), jnp.zeros((16, n), BF)
    return jnp.concatenate(
        [jnp.where(base == jnp.asarray(16 * g, BF), one, zero) for g in range(size // 16)], axis=0
    )


def spread(index, values, group, count):
    n = index.shape[1]
    base = (jnp.broadcast_to(index, (16, n)) - sub_iota(16, n) // (16 // group)).astype(F32).astype(BF)
    zero = jnp.zeros((16, n), BF)
    return [
        [jnp.where(base == jnp.asarray(group * g, BF), v, zero) for g in range(count // group)]
        for v in values
    ]


def fill_table(rows, table):
    lows = rows.shape[1] // LANE
    parts = [rows[0:8, l * LANE : (l + 1) * LANE] for l in range(lows)]
    parts += [rows[8:12, l * LANE : (l + 1) * LANE] for l in range(lows)]
    high, low = split(jnp.concatenate(parts, axis=0))
    table[0 : 12 * lows, :] = high
    table[12 * lows :, :] = low


def pick_table(table, index, lows):
    n = index.shape[1]
    grabbed = lax.dot_general(table, onehot(index % LANE, LANE), NN, preferred_element_type=F32)
    total = 12 * lows
    low = jnp.broadcast_to(index // LANE, (8, n))
    pair = low - sub_iota(8, n) // 4
    first = jnp.zeros((8, n), F32)
    for l in range(lows):
        at = 8 * l
        value = grabbed[at : at + 8] + grabbed[total + at : total + at + 8]
        first = jnp.where(low == l, value, first)
    second = jnp.zeros((8, n), F32)
    for l in range(lows // 2):
        at = 8 * lows + 8 * l
        value = grabbed[at : at + 8] + grabbed[total + at : total + at + 8]
        second = jnp.where(pair == 2 * l, value, second)
    return first, second[0:4] + second[4:8]


def add_table(first, second, index, lows):
    high, low = split(first)
    group = jnp.concatenate([high.astype(F32), low.astype(F32)], axis=0).astype(BF)
    wide = spread(index // LANE, [group], 1, lows)[0]
    high, low = split(second)
    high, low = high.astype(F32), low.astype(F32)
    group = jnp.concatenate([high, low, high, low], axis=0).astype(BF)
    narrow = spread(index // LANE, [group], 2, lows)[0]
    stacked = jnp.concatenate(wide + narrow, axis=0)
    return lax.dot_general(
        stacked, onehot(index % LANE, LANE), NT, preferred_element_type=F32
    )


def table_part(total, lows, l):
    first = total[16 * l : 16 * l + 8] + total[16 * l + 8 : 16 * l + 16]
    at = 16 * lows + 8 * l
    return first, total[at : at + 4] + total[at + 4 : at + 8]


def pick_kernel(vol, pick, out, table):
    width = vol.shape[1]
    lows = width // LANE
    rows = vol[...]
    fill_table(
        jnp.concatenate([rows[3 * c + j : 3 * c + j + 1] for j in range(3) for c in range(4)], axis=0),
        table,
    )
    count, _, part = out.shape
    for k in range(count):
        first, second = pick_table(table[...], pick[:, k * part : (k + 1) * part], lows)
        out[k, 0:8, :] = first
        out[k, 8:12, :] = second


def lane_iota(rows, cols):
    return lax.broadcasted_iota(jnp.int32, (rows, cols), 1)


def sort_terms(values, place, lows):
    high, low = split(jnp.concatenate([values] * 4, axis=0))
    first, second = spread(place // LANE, [high, low], 4, lows)
    stacked = jnp.concatenate(first + second, axis=0)
    return lax.dot_general(stacked, onehot(place % LANE, LANE), NT, preferred_element_type=F32)


def cut_windows(total, offsets, ordered, out, masked):
    half = total.shape[0] // 2
    sums = total[0:half, :] + total[half:, :]
    top = sub_iota(8, 128) < 4
    groups = half // 8
    left = [sums[8 * g : 8 * g + 8, 0:128] for g in range(groups)]
    right = [sums[8 * g : 8 * g + 8, 128:256] for g in range(groups)]
    turned_left = [pltpu.roll(v, 4, 0) for v in left] + [jnp.zeros((8, 128), F32)]
    turned_right = [pltpu.roll(v, 4, 0) for v in right]
    for g in range(groups):
        ordered[4 * g] = jnp.where(top, left[g], turned_right[g])
        ordered[4 * g + 1] = jnp.where(top, right[g], left[g])
        ordered[4 * g + 2] = jnp.where(top, turned_left[g], right[g])
        ordered[4 * g + 3] = jnp.where(top, turned_right[g], turned_left[g + 1])
    for g in range(4 * groups, ordered.shape[0]):
        ordered[g] = jnp.zeros((8, 128), F32)
    lane = lane_iota(8, 128)
    number = lane + jnp.where(top, 0, 128)

    def window(i, _):
        for u in range(8):
            o = i * 8 + u
            start = offsets[0, o]
            block, shift = start // 128, start % 128
            joined = jnp.where(lane >= shift, ordered[block], ordered[block + 1])
            joined = pltpu.roll(joined, (128 - shift) % 128, 1)
            if masked:
                joined = jnp.where(number < offsets[0, o + 1] - start, joined, 0.0)
            out[o] = joined
        return 0

    lax.fori_loop(0, out.shape[0] // 8, window, 0)


def merge_windows(windows, offsets, merged, table):
    lane = lane_iota(8, 128)
    top = sub_iota(8, 128) < 4

    def window(i, carry):
        for u in range(8):
            o = i * 8 + u
            start, later = offsets[0, o], offsets[0, o + 1]
            block, shift = start // 128, start % 128
            value = pltpu.roll(windows[o], shift, 1)
            turned = pltpu.roll(value, 4, 0)
            one, two = jnp.where(top, value, turned), jnp.where(top, turned, value)
            first = jnp.where(lane >= shift, one, carry)
            second = jnp.where(lane >= shift, two, one)
            merged[block] = first
            merged[block + 1] = second
            merged[block + 2] = two
            ahead = later // 128 - block
            carry = jnp.where(ahead == 0, first, jnp.where(ahead == 1, second, two))
        return carry

    lax.fori_loop(0, windows.shape[0] // 8, window, jnp.zeros((8, 128), F32))
    half = table.shape[0] // 2
    left, right = [], []
    for g in range(half // 8):
        left.append(jnp.where(top, merged[4 * g], merged[4 * g + 2]))
        right.append(jnp.where(top, merged[4 * g + 1], merged[4 * g + 3]))
    both = jnp.concatenate([jnp.concatenate(left, axis=0), jnp.concatenate(right, axis=0)], axis=1)
    high, low = split(both)
    table[0:half, :] = high
    table[half:, :] = low


def request_kernel(step, owner_hbm, slot_hbm, normal_hbm, out, place, offset, owner, slot, normal, total, named, ordered, scalars, sems):
    copies = [
        pltpu.make_async_copy(a, b, sems.at[i])
        for i, (a, b) in enumerate(((owner_hbm, owner), (slot_hbm, slot), (normal_hbm, normal)))
    ]
    for copy in copies:
        copy.start()
    count = owner.shape[1]
    owners = out.shape[0]
    lows = count // LANE
    total[...] = jnp.zeros_like(total)
    copies[0].wait()

    def tally(i, sums):
        for u in range(step // 256):
            lanes = pl.ds(pl.multiple_of(i * step + u * 256, 256), 256)
            value = onehot(owner[:, lanes], owners)
            named[:, lanes] = value
            sums = sums + value
        return sums

    sums = lax.fori_loop(0, count // step, tally, jnp.zeros((owners, 256), BF))
    counts = lax.dot_general(sums, jnp.ones((256, 256), BF), NN, preferred_element_type=F32).astype(BF)
    before = (sub_iota(owners, owners) > lane_iota(owners, owners)).astype(F32).astype(BF)
    base = lax.dot_general(before, counts, NN, preferred_element_type=F32) - 1.0
    counts = lax.dot_general(jnp.ones((16, 256), BF), sums, NT, preferred_element_type=F32).astype(BF)
    before = (sub_iota(owners, 2 * owners) < lane_iota(owners, 2 * owners)).astype(F32).astype(BF)
    offset[...] = lax.dot_general(counts, before, NN, preferred_element_type=F32)[0:8].astype(jnp.int32)
    save = pltpu.make_async_copy(offset, scalars, sems.at[3])
    save.start()
    row, col = sub_iota(256, 512), lane_iota(256, 512)
    upper = ((row <= col) | (col >= 256)).astype(F32).astype(BF)

    def ranks(i, base):
        chunks = []
        for u in range(step // 256):
            chunks.append(named[:, pl.ds(pl.multiple_of(i * step + u * 256, 256), 256)])
        sums = lax.dot_general(jnp.concatenate(chunks, axis=0), upper, NN, preferred_element_type=F32)
        for u in range(step // 256):
            part = sums[u * owners : (u + 1) * owners]
            seen = chunks[u].astype(F32) * (part[:, 0:256] + base)
            lanes = pl.ds(pl.multiple_of(i * step + u * 256, 256), 256)
            place[:, lanes] = jnp.sum(seen, axis=0, keepdims=True).astype(jnp.int32)
            base = base + part[:, 256:512]
        return base

    lax.fori_loop(0, count // step, ranks, base)
    copies[1].wait()
    copies[2].wait()

    def slots(i, _):
        lanes = pl.ds(pl.multiple_of(i * step, step), step)
        values = jnp.concatenate([slot[:, lanes].astype(F32), normal[:, lanes]], axis=0)
        total[...] += sort_terms(values, place[:, lanes], lows)
        return 0

    lax.fori_loop(0, count // step, slots, 0)
    save.wait()
    cut_windows(total, scalars, ordered, out, True)


def along_kernel(group, surf, recv, out, table):
    lows = surf.shape[0] * surf.shape[2] // LANE
    fill_table(jnp.concatenate([surf[s] for s in range(surf.shape[0])], axis=1), table)

    def step(i, _):
        parts = [recv[i * group + u] for u in range(group)]
        block = jnp.concatenate([p[4 * h : 4 * h + 4] for p in parts for h in range(2)], axis=1)
        index = block[0:1].astype(jnp.int32)
        first, second = pick_table(table[...], index, lows)
        along = first[0:4] * block[1:2] + first[4:8] * block[2:3] + second * block[3:4]
        for u in range(group):
            for h in range(2):
                at = (2 * u + h) * 128
                out[i * group + u, 4 * h : 4 * h + 4, :] = along[:, at : at + 128]
        return 0

    lax.fori_loop(0, recv.shape[0] // group, step, 0)


def signs(xs, inner):
    sub = sub_iota(8, 1)

    def column(number):
        value = jnp.full((8, 1), xs[3], F32)
        for c in range(3):
            value = jnp.where(number == c, xs[c], value)
        return value

    return [column(sub % 4)] * 2 if inner else [column(sub // 4), column(sub // 4 + 2)]


def local_kernel(step, disp, normal, gap, weight, proj, toward, back, part):
    count = disp.shape[1]
    sub4 = sub_iota(4, 1)

    def column(xs):
        value = jnp.full((4, 1), xs[3], F32)
        for a in range(3):
            value = jnp.where(sub4 == a, xs[a], value)
        return value

    def body(i, _):
        lanes = pl.ds(pl.multiple_of(i * step, step), step)
        p, w, d, n, g = proj[:, lanes], weight[:, lanes], disp[:, lanes], normal[:, lanes], gap[:, lanes]
        for inner, out in ((False, toward), (True, back)):
            node_x, node_y = signs(node_xs, inner), signs(node_ys, inner)
            sums = [None, None]
            for q in range(4):
                table = signs([slave_table[a][q] * 0.25 for a in range(4)], not inner)
                first = jnp.broadcast_to(p[2 * q : 2 * q + 1], (8, step))
                second = jnp.broadcast_to(p[2 * q + 1 : 2 * q + 2], (8, step))
                along = jnp.broadcast_to(w[q : q + 1], (8, step))
                for h in range(2):
                    term = (1.0 + node_x[h] * first) * (1.0 + node_y[h] * second) * (along * table[h])
                    sums[h] = term if q == 0 else sums[h] + term
            out[0:8, lanes] = sums[0]
            out[8:16, lanes] = sums[1]
        total = g
        for b in range(4):
            along = n[0:1] * d[3 * b : 3 * b + 1] + n[1:2] * d[3 * b + 1 : 3 * b + 2] + n[2:3] * d[3 * b + 2 : 3 * b + 3]
            total = total + column(slave_table[b]) * along
        points = w * total
        result = column([slave_table[a][0] for a in range(4)]) * points[0:1]
        for q in range(1, 4):
            result = result + column([slave_table[a][q] for a in range(4)]) * points[q : q + 1]
        part[:, lanes] = result
        return 0

    lax.fori_loop(0, count // step, body, 0)


def doubled(values):
    n = values.shape[1]
    rows = [jnp.broadcast_to(values[c : c + 1], (4, n)) for c in range(4)]
    return jnp.concatenate(rows[0:2], axis=0), jnp.concatenate(rows[2:4], axis=0)


def combine(factors, values):
    one, two = doubled(values)
    both = factors[0:8] * one + factors[8:16] * two
    return both[0:4] + both[4:8]


def update_kernel(step, recv, *refs):
    inputs, outputs, out = refs[0:7], refs[7:9], refs[9]
    buffers, results = refs[10:17], refs[17:19]
    table, total, ordered, sems = refs[19:23]
    copies = [pltpu.make_async_copy(inputs[i], buffers[i], sems.at[i]) for i in range(7)]
    for copy in copies:
        copy.start()
    offsets, place, toward, back, part, multiplier, active = buffers
    gap_out, new_out = results
    count = place.shape[1]
    lows = count // LANE
    half = lows * 4
    total[...] = jnp.zeros_like(total)
    copies[0].wait()
    merge_windows(recv, offsets, ordered, table)
    for copy in copies[1:]:
        copy.wait()

    def body(i, _):
        lanes = pl.ds(pl.multiple_of(i * step, step), step)
        places = place[:, lanes]
        grabbed = lax.dot_general(table[...], onehot(places % LANE, LANE), NN, preferred_element_type=F32)
        base = jnp.broadcast_to(places // LANE, (8, step)) - sub_iota(8, step) // 4
        along = jnp.zeros((8, step), F32)
        for g in range(lows // 2):
            value = grabbed[8 * g : 8 * g + 8] + grabbed[half + 8 * g : half + 8 * g + 8]
            along = jnp.where(base == 2 * g, value, along)
        mortar = combine(toward[:, lanes], along[0:4] + along[4:8])
        weighted = part[:, lanes] - mortar
        lagrange = jnp.where(active[:, lanes] == 1, jnp.maximum(multiplier[:, lanes] - weighted, 0.0), 0.0)
        gap_out[:, lanes] = weighted
        new_out[:, lanes] = lagrange
        total[...] += sort_terms(combine(back[:, lanes], lagrange), places, lows)
        return 0

    lax.fori_loop(0, count // step, body, 0)
    saves = [pltpu.make_async_copy(results[i], outputs[i], sems.at[7 + i]) for i in range(2)]
    for save in saves:
        save.start()
    cut_windows(total, offsets, ordered, out, False)
    for save in saves:
        save.wait()


def force_kernel(group, recv, factor, out, total):
    lows = out.shape[0] * out.shape[2] // LANE
    total[...] = jnp.zeros_like(total)

    def step(i, _):
        parts = [recv[i * group + u] for u in range(group)]
        block = jnp.concatenate([p[4 * h : 4 * h + 4] for p in parts for h in range(2)], axis=1)
        parts = [factor[i * group + u] for u in range(group)]
        node = jnp.concatenate([p[4 * h : 4 * h + 4] for p in parts for h in range(2)], axis=1)
        index = block[0:1].astype(jnp.int32)
        first = jnp.concatenate([node * block[1:2], node * block[2:3]], axis=0)
        total[...] += add_table(first, node * block[3:4], index, lows)
        return 0

    lax.fori_loop(0, recv.shape[0] // group, step, 0)
    sums = total[...]
    per = out.shape[2] // LANE
    for l in range(lows):
        first, second = table_part(sums, lows, l)
        lanes = slice(l % per * LANE, (l % per + 1) * LANE)
        out[l // per, 0:8, lanes] = first
        out[l // per, 8:12, lanes] = second


def place_kernel(moved, pick, out):
    lows = out.shape[1] // LANE
    rows = jnp.concatenate([moved[k] for k in range(moved.shape[0])], axis=1)
    sums = add_table(rows[0:8], rows[8:12], pick[...], lows)
    for l in range(lows):
        first, second = table_part(sums, lows, l)
        both = jnp.concatenate([first, second], axis=0)
        ordered = jnp.concatenate(
            [both[4 * j + c : 4 * j + c + 1] for c in range(4) for j in range(3)], axis=0
        )
        out[:, l * LANE : (l + 1) * LANE] = ordered


def call(kernel, ins, outs, scratch, cycles, *args):
    size = sum(a.size * 4 for a in args) + sum(math.prod(o[0]) * 4 for o in outs)
    spaces = {"v": pltpu.VMEM, "h": pl.ANY}
    places = [pl.BlockSpec(memory_space=spaces[p]) for p in ins]
    result = pl.pallas_call(
        kernel,
        out_shape=[jax.ShapeDtypeStruct(*o) for o in outs],
        in_specs=places[: len(args)],
        out_specs=places[len(args) :],
        scratch_shapes=scratch,
        compiler_params=pltpu.CompilerParams(vmem_limit_bytes=56 * 2**20),
        cost_estimate=pl.CostEstimate(flops=cycles, bytes_accessed=size, transcendentals=0),
    )(*args)
    return result[0] if len(outs) == 1 else result


def on_device(
    slave_disp,
    slave_normal,
    gap_zero,
    quad_weight,
    proj_coord,
    multiplier,
    active,
    pair_owner,
    pair_slot,
    master_vol,
    surf_pick,
):
    region_count = lax.axis_size("region")
    dom_count = lax.axis_size("dom")
    owners = region_count * dom_count
    count = slave_disp.shape[1]
    width = master_vol.shape[1]
    lows = width // LANE
    part = width // dom_count
    step = 4096
    blocks = count // LANE
    exchange = functools.partial(lax.all_to_all, split_axis=0, concat_axis=0, tiled=True)
    owner = pair_owner.reshape(1, count)
    flat = (owners, 8, 128)
    everyone = ("region", "dom")
    whole, quad, wide = (1, count), (4, count), (16, count)
    table = pltpu.VMEM((24 * lows, LANE), BF)

    request, place, offset = call(
        functools.partial(request_kernel, step),
        "hhhvvv",
        [(flat, F32), (whole, jnp.int32), ((8, 2 * owners), jnp.int32)],
        [
            pltpu.VMEM(whole, jnp.int32),
            pltpu.VMEM(whole, jnp.int32),
            pltpu.VMEM((3, count), F32),
            pltpu.VMEM((8 * blocks, LANE), F32),
            pltpu.VMEM((owners, count), BF),
            pltpu.VMEM((2 * blocks + 4, 8, 128), F32),
            pltpu.SMEM((8, 2 * owners), jnp.int32),
            pltpu.SemaphoreType.DMA((4,)),
        ],
        10**10,
        owner,
        pair_slot.reshape(1, count),
        slave_normal,
    )
    request, master_vol = lax.optimization_barrier((request, master_vol))
    recv = exchange(request, everyone)
    picked = call(pick_kernel, "vvv", [((dom_count, 12, part), F32)], [table], 10**9, master_vol, surf_pick)
    surf = exchange(picked, "dom")
    toward, back, slave_part = call(
        functools.partial(local_kernel, 512),
        "v" * 8,
        [(wide, F32), (wide, F32), (quad, F32)],
        [],
        10**9,
        slave_disp,
        slave_normal,
        gap_zero,
        quad_weight,
        proj_coord,
    )
    along = call(functools.partial(along_kernel, 32), "vvv", [(flat, F32)], [table], 10**10, surf, recv)
    returned = exchange(along, everyone)
    weighted_gap, multiplier_new, terms = call(
        functools.partial(update_kernel, step),
        "vhhhhhhhhhv",
        [(quad, F32), (quad, F32), (flat, F32)],
        [
            pltpu.SMEM((8, 2 * owners), jnp.int32),
            pltpu.VMEM(whole, jnp.int32),
            pltpu.VMEM(wide, F32),
            pltpu.VMEM(wide, F32),
            pltpu.VMEM(quad, F32),
            pltpu.VMEM(quad, F32),
            pltpu.VMEM(quad, jnp.int32),
            pltpu.VMEM(quad, F32),
            pltpu.VMEM(quad, F32),
            pltpu.VMEM((8 * blocks, LANE), BF),
            pltpu.VMEM((8 * blocks, LANE), F32),
            pltpu.VMEM((2 * blocks + 4, 8, 128), F32),
            pltpu.SemaphoreType.DMA((9,)),
        ],
        2 * 10**10,
        returned,
        offset,
        place,
        toward,
        back,
        slave_part,
        multiplier,
        active,
    )
    factor = exchange(terms, everyone)
    forces = call(
        functools.partial(force_kernel, 32),
        "vvv",
        [((dom_count, 12, part), F32)],
        [pltpu.VMEM((24 * lows, LANE), F32)],
        10**10,
        recv,
        factor,
    )
    moved = exchange(forces, "dom")
    master_force = call(place_kernel, "vvv", [((12, width), F32)], [], 10**9, moved, surf_pick)
    return (weighted_gap, multiplier_new, master_force)


def solution(mesh):
    both = ("region", "dom")
    return jax.shard_map(
        on_device,
        mesh=mesh,
        in_specs=(P(None, both),) * 7 + (P(both, None), P(both), P(None, both), P(both, None)),
        out_specs=(P(None, both),) * 3,
        check_vma=False,
    )
```

```python
import functools
import math

import jax
import jax.numpy as jnp
from jax import lax
from jax.experimental import pallas as pl
from jax.experimental.pallas import tpu as pltpu
from jax.sharding import PartitionSpec as P

gauss_point = 1.0 / math.sqrt(3.0)
node_xs = [-1.0, 1.0, 1.0, -1.0]
node_ys = [-1.0, -1.0, 1.0, 1.0]
point_xs = [-gauss_point, gauss_point, gauss_point, -gauss_point]
point_ys = [-gauss_point, -gauss_point, gauss_point, gauss_point]
slave_table = [
    [(1.0 + node_xs[c] * point_xs[q]) * (1.0 + node_ys[c] * point_ys[q]) * 0.25 for q in range(4)]
    for c in range(4)
]

BF = jnp.bfloat16
F32 = jnp.float32
LANE = 256

NN = (((1,), (0,)), ((), ()))
NT = (((1,), (1,)), ((), ()))


def sub_iota(rows, cols):
    return lax.broadcasted_iota(jnp.int32, (rows, cols), 0)


def split(values):
    high = values.astype(BF)
    return high, (values - high.astype(F32)).astype(BF)


def onehot(index, size):
    n = index.shape[1]
    base = (jnp.broadcast_to(index, (16, n)) - sub_iota(16, n)).astype(F32).astype(BF)
    one, zero = jnp.ones((16, n), BF), jnp.zeros((16, n), BF)
    return jnp.concatenate(
        [jnp.where(base == jnp.asarray(16 * g, BF), one, zero) for g in range(size // 16)], axis=0
    )


def spread(index, values, group, count):
    n = index.shape[1]
    base = (jnp.broadcast_to(index, (16, n)) - sub_iota(16, n) // (16 // group)).astype(F32).astype(BF)
    zero = jnp.zeros((16, n), BF)
    return [
        [jnp.where(base == jnp.asarray(group * g, BF), v, zero) for g in range(count // group)]
        for v in values
    ]


def fill_table(rows, table):
    lows = rows.shape[1] // LANE
    parts = [rows[0:8, l * LANE : (l + 1) * LANE] for l in range(lows)]
    parts += [rows[8:12, l * LANE : (l + 1) * LANE] for l in range(lows)]
    high, low = split(jnp.concatenate(parts, axis=0))
    table[0 : 12 * lows, :] = high
    table[12 * lows :, :] = low


def pick_table(table, index, lows):
    n = index.shape[1]
    grabbed = lax.dot_general(table, onehot(index % LANE, LANE), NN, preferred_element_type=F32)
    total = 12 * lows
    low = jnp.broadcast_to(index // LANE, (8, n))
    pair = low - sub_iota(8, n) // 4
    first = jnp.zeros((8, n), F32)
    for l in range(lows):
        at = 8 * l
        value = grabbed[at : at + 8] + grabbed[total + at : total + at + 8]
        first = jnp.where(low == l, value, first)
    second = jnp.zeros((8, n), F32)
    for l in range(lows // 2):
        at = 8 * lows + 8 * l
        value = grabbed[at : at + 8] + grabbed[total + at : total + at + 8]
        second = jnp.where(pair == 2 * l, value, second)
    return first, second[0:4] + second[4:8]


def add_table(first, second, index, lows):
    high, low = split(first)
    group = jnp.concatenate([high.astype(F32), low.astype(F32)], axis=0).astype(BF)
    wide = spread(index // LANE, [group], 1, lows)[0]
    high, low = split(second)
    high, low = high.astype(F32), low.astype(F32)
    group = jnp.concatenate([high, low, high, low], axis=0).astype(BF)
    narrow = spread(index // LANE, [group], 2, lows)[0]
    stacked = jnp.concatenate(wide + narrow, axis=0)
    return lax.dot_general(
        stacked, onehot(index % LANE, LANE), NT, preferred_element_type=F32
    )


def table_part(total, lows, l):
    first = total[16 * l : 16 * l + 8] + total[16 * l + 8 : 16 * l + 16]
    at = 16 * lows + 8 * l
    return first, total[at : at + 4] + total[at + 4 : at + 8]


def surface_kernel(vol, pick, out, table):
    parts, _, width = vol.shape
    lows = width // LANE
    part = width // parts
    lanes = pl.ds(pl.multiple_of(lax.axis_index("dom") * part, part), part)
    rows = []
    for s in range(parts):
        fill_table(vol[s], table.at[s])
        first, second = pick_table(table[s], pick[s, :, lanes], lows)
        rows.append(jnp.concatenate([first, second], axis=0))
    rows = jnp.concatenate(rows, axis=1)
    order = [rows[3 * c + j : 3 * c + j + 1] for j in range(3) for c in range(4)]
    fill_table(jnp.concatenate(order, axis=0), out)


def lane_iota(rows, cols):
    return lax.broadcasted_iota(jnp.int32, (rows, cols), 1)


def sort_terms(values, place, lows):
    high, low = split(jnp.concatenate([values] * 4, axis=0))
    first, second = spread(place // LANE, [high, low], 4, lows)
    stacked = jnp.concatenate(first + second, axis=0)
    return lax.dot_general(stacked, onehot(place % LANE, LANE), NT, preferred_element_type=F32)


def cut_windows(total, offsets, ordered, out, masked):
    half = total.shape[0] // 2
    sums = total[0:half, :] + total[half:, :]
    top = sub_iota(8, 128) < 4
    groups = half // 8
    left = [sums[8 * g : 8 * g + 8, 0:128] for g in range(groups)]
    right = [sums[8 * g : 8 * g + 8, 128:256] for g in range(groups)]
    turned_left = [pltpu.roll(v, 4, 0) for v in left] + [jnp.zeros((8, 128), F32)]
    turned_right = [pltpu.roll(v, 4, 0) for v in right]
    for g in range(groups):
        ordered[4 * g] = jnp.where(top, left[g], turned_right[g])
        ordered[4 * g + 1] = jnp.where(top, right[g], left[g])
        ordered[4 * g + 2] = jnp.where(top, turned_left[g], right[g])
        ordered[4 * g + 3] = jnp.where(top, turned_right[g], turned_left[g + 1])
    for g in range(4 * groups, ordered.shape[0]):
        ordered[g] = jnp.zeros((8, 128), F32)
    lane = lane_iota(8, 128)
    number = lane + jnp.where(top, 0, 128)

    def window(i, _):
        for u in range(8):
            o = i * 8 + u
            start = offsets[0, o]
            block, shift = start // 128, start % 128
            joined = jnp.where(lane >= shift, ordered[block], ordered[block + 1])
            joined = pltpu.roll(joined, (128 - shift) % 128, 1)
            if masked:
                joined = jnp.where(number < offsets[0, o + 1] - start, joined, 0.0)
            out[o] = joined
        return 0

    lax.fori_loop(0, out.shape[0] // 8, window, 0)


def merge_windows(windows, offsets, merged, table):
    lane = lane_iota(8, 128)
    top = sub_iota(8, 128) < 4

    def window(i, carry):
        for u in range(8):
            o = i * 8 + u
            start, later = offsets[0, o], offsets[0, o + 1]
            block, shift = start // 128, start % 128
            value = pltpu.roll(windows[o], shift, 1)
            turned = pltpu.roll(value, 4, 0)
            one, two = jnp.where(top, value, turned), jnp.where(top, turned, value)
            first = jnp.where(lane >= shift, one, carry)
            second = jnp.where(lane >= shift, two, one)
            merged[block] = first
            merged[block + 1] = second
            merged[block + 2] = two
            ahead = later // 128 - block
            carry = jnp.where(ahead == 0, first, jnp.where(ahead == 1, second, two))
        return carry

    lax.fori_loop(0, windows.shape[0] // 8, window, jnp.zeros((8, 128), F32))
    half = table.shape[0] // 2
    left, right = [], []
    for g in range(half // 8):
        left.append(jnp.where(top, merged[4 * g], merged[4 * g + 2]))
        right.append(jnp.where(top, merged[4 * g + 1], merged[4 * g + 3]))
    both = jnp.concatenate([jnp.concatenate(left, axis=0), jnp.concatenate(right, axis=0)], axis=1)
    high, low = split(both)
    table[0:half, :] = high
    table[half:, :] = low


def request_kernel(step, owner_hbm, slot_hbm, normal_hbm, out, place, offset, owner, slot, normal, total, named, ordered, scalars, sems):
    copies = [
        pltpu.make_async_copy(a, b, sems.at[i])
        for i, (a, b) in enumerate(((owner_hbm, owner), (slot_hbm, slot), (normal_hbm, normal)))
    ]
    for copy in copies:
        copy.start()
    count = owner.shape[1]
    owners = out.shape[0]
    lows = count // LANE
    total[...] = jnp.zeros_like(total)
    copies[0].wait()

    def tally(i, sums):
        for u in range(step // 256):
            lanes = pl.ds(pl.multiple_of(i * step + u * 256, 256), 256)
            value = onehot(owner[:, lanes], owners)
            named[:, lanes] = value
            sums = sums + value
        return sums

    sums = lax.fori_loop(0, count // step, tally, jnp.zeros((owners, 256), BF))
    counts = lax.dot_general(sums, jnp.ones((256, 256), BF), NN, preferred_element_type=F32).astype(BF)
    before = (sub_iota(owners, owners) > lane_iota(owners, owners)).astype(F32).astype(BF)
    base = lax.dot_general(before, counts, NN, preferred_element_type=F32) - 1.0
    counts = lax.dot_general(jnp.ones((16, 256), BF), sums, NT, preferred_element_type=F32).astype(BF)
    before = (sub_iota(owners, 2 * owners) < lane_iota(owners, 2 * owners)).astype(F32).astype(BF)
    offset[...] = lax.dot_general(counts, before, NN, preferred_element_type=F32)[0:8].astype(jnp.int32)
    save = pltpu.make_async_copy(offset, scalars, sems.at[3])
    save.start()
    row, col = sub_iota(256, 512), lane_iota(256, 512)
    upper = ((row <= col) | (col >= 256)).astype(F32).astype(BF)

    def ranks(i, base):
        chunks = []
        for u in range(step // 256):
            chunks.append(named[:, pl.ds(pl.multiple_of(i * step + u * 256, 256), 256)])
        sums = lax.dot_general(jnp.concatenate(chunks, axis=0), upper, NN, preferred_element_type=F32)
        for u in range(step // 256):
            part = sums[u * owners : (u + 1) * owners]
            seen = chunks[u].astype(F32) * (part[:, 0:256] + base)
            lanes = pl.ds(pl.multiple_of(i * step + u * 256, 256), 256)
            place[:, lanes] = jnp.sum(seen, axis=0, keepdims=True).astype(jnp.int32)
            base = base + part[:, 256:512]
        return base

    lax.fori_loop(0, count // step, ranks, base)
    copies[1].wait()
    copies[2].wait()

    def slots(i, _):
        lanes = pl.ds(pl.multiple_of(i * step, step), step)
        values = jnp.concatenate([slot[:, lanes].astype(F32), normal[:, lanes]], axis=0)
        total[...] += sort_terms(values, place[:, lanes], lows)
        return 0

    lax.fori_loop(0, count // step, slots, 0)
    save.wait()
    cut_windows(total, scalars, ordered, out, True)


def along_kernel(group, table, recv, out):
    lows = table.shape[0] // 24

    def step(i, _):
        parts = [recv[i * group + u] for u in range(group)]
        block = jnp.concatenate([p[4 * h : 4 * h + 4] for p in parts for h in range(2)], axis=1)
        index = block[0:1].astype(jnp.int32)
        first, second = pick_table(table[...], index, lows)
        along = first[0:4] * block[1:2] + first[4:8] * block[2:3] + second * block[3:4]
        for u in range(group):
            for h in range(2):
                at = (2 * u + h) * 128
                out[i * group + u, 4 * h : 4 * h + 4, :] = along[:, at : at + 128]
        return 0

    lax.fori_loop(0, recv.shape[0] // group, step, 0)


def signs(xs, inner):
    sub = sub_iota(8, 1)

    def column(number):
        value = jnp.full((8, 1), xs[3], F32)
        for c in range(3):
            value = jnp.where(number == c, xs[c], value)
        return value

    return [column(sub % 4)] * 2 if inner else [column(sub // 4), column(sub // 4 + 2)]


def local_kernel(step, disp, normal, gap, weight, proj, toward, back, part):
    count = disp.shape[1]
    sub4 = sub_iota(4, 1)

    def column(xs):
        value = jnp.full((4, 1), xs[3], F32)
        for a in range(3):
            value = jnp.where(sub4 == a, xs[a], value)
        return value

    def body(i, _):
        lanes = pl.ds(pl.multiple_of(i * step, step), step)
        p, w, d, n, g = proj[:, lanes], weight[:, lanes], disp[:, lanes], normal[:, lanes], gap[:, lanes]
        for inner, out in ((False, toward), (True, back)):
            node_x, node_y = signs(node_xs, inner), signs(node_ys, inner)
            sums = [None, None]
            for q in range(4):
                table = signs([slave_table[a][q] * 0.25 for a in range(4)], not inner)
                first = jnp.broadcast_to(p[2 * q : 2 * q + 1], (8, step))
                second = jnp.broadcast_to(p[2 * q + 1 : 2 * q + 2], (8, step))
                along = jnp.broadcast_to(w[q : q + 1], (8, step))
                for h in range(2):
                    term = (1.0 + node_x[h] * first) * (1.0 + node_y[h] * second) * (along * table[h])
                    sums[h] = term if q == 0 else sums[h] + term
            out[0:8, lanes] = sums[0]
            out[8:16, lanes] = sums[1]
        total = g
        for b in range(4):
            along = n[0:1] * d[3 * b : 3 * b + 1] + n[1:2] * d[3 * b + 1 : 3 * b + 2] + n[2:3] * d[3 * b + 2 : 3 * b + 3]
            total = total + column(slave_table[b]) * along
        points = w * total
        result = column([slave_table[a][0] for a in range(4)]) * points[0:1]
        for q in range(1, 4):
            result = result + column([slave_table[a][q] for a in range(4)]) * points[q : q + 1]
        part[:, lanes] = result
        return 0

    lax.fori_loop(0, count // step, body, 0)


def doubled(values):
    n = values.shape[1]
    rows = [jnp.broadcast_to(values[c : c + 1], (4, n)) for c in range(4)]
    return jnp.concatenate(rows[0:2], axis=0), jnp.concatenate(rows[2:4], axis=0)


def combine(factors, values):
    one, two = doubled(values)
    both = factors[0:8] * one + factors[8:16] * two
    return both[0:4] + both[4:8]


def update_kernel(step, *refs):
    inputs, outputs, out = refs[0:8], refs[8:10], refs[10]
    buffers, results = refs[11:19], refs[19:21]
    table, total, ordered, sems = refs[21:25]
    copies = [pltpu.make_async_copy(inputs[i], buffers[i], sems.at[i]) for i in range(8)]
    for copy in copies:
        copy.start()
    recv, offsets, place, toward, back, part, multiplier, active = buffers
    gap_out, new_out = results
    count = place.shape[1]
    lows = count // LANE
    half = lows * 4
    total[...] = jnp.zeros_like(total)
    for copy in copies[0:2]:
        copy.wait()
    merge_windows(recv, offsets, ordered, table)
    for copy in copies[2:]:
        copy.wait()

    def body(i, _):
        lanes = pl.ds(pl.multiple_of(i * step, step), step)
        places = place[:, lanes]
        grabbed = lax.dot_general(table[...], onehot(places % LANE, LANE), NN, preferred_element_type=F32)
        base = jnp.broadcast_to(places // LANE, (8, step)) - sub_iota(8, step) // 4
        along = jnp.zeros((8, step), F32)
        for g in range(lows // 2):
            value = grabbed[8 * g : 8 * g + 8] + grabbed[half + 8 * g : half + 8 * g + 8]
            along = jnp.where(base == 2 * g, value, along)
        mortar = combine(toward[:, lanes], along[0:4] + along[4:8])
        weighted = part[:, lanes] - mortar
        lagrange = jnp.where(active[:, lanes] == 1, jnp.maximum(multiplier[:, lanes] - weighted, 0.0), 0.0)
        gap_out[:, lanes] = weighted
        new_out[:, lanes] = lagrange
        total[...] += sort_terms(combine(back[:, lanes], lagrange), places, lows)
        return 0

    lax.fori_loop(0, count // step, body, 0)
    saves = [pltpu.make_async_copy(results[i], outputs[i], sems.at[8 + i]) for i in range(2)]
    for save in saves:
        save.start()
    cut_windows(total, offsets, ordered, out, False)
    for save in saves:
        save.wait()


def force_kernel(group, recv, factor, out, total):
    lows = out.shape[0] * out.shape[2] // LANE
    total[...] = jnp.zeros_like(total)

    def step(i, _):
        parts = [recv[i * group + u] for u in range(group)]
        block = jnp.concatenate([p[4 * h : 4 * h + 4] for p in parts for h in range(2)], axis=1)
        parts = [factor[i * group + u] for u in range(group)]
        node = jnp.concatenate([p[4 * h : 4 * h + 4] for p in parts for h in range(2)], axis=1)
        index = block[0:1].astype(jnp.int32)
        first = jnp.concatenate([node * block[1:2], node * block[2:3]], axis=0)
        total[...] += add_table(first, node * block[3:4], index, lows)
        return 0

    lax.fori_loop(0, recv.shape[0] // group, step, 0)
    sums = total[...]
    per = out.shape[2] // LANE
    for l in range(lows):
        first, second = table_part(sums, lows, l)
        lanes = slice(l % per * LANE, (l % per + 1) * LANE)
        out[l // per, 0:8, lanes] = first
        out[l // per, 8:12, lanes] = second


def place_kernel(moved, pick, out):
    lows = out.shape[1] // LANE
    rows = jnp.concatenate([moved[k] for k in range(moved.shape[0])], axis=1)
    sums = add_table(rows[0:8], rows[8:12], pick[...], lows)
    for l in range(lows):
        first, second = table_part(sums, lows, l)
        both = jnp.concatenate([first, second], axis=0)
        ordered = jnp.concatenate(
            [both[4 * j + c : 4 * j + c + 1] for c in range(4) for j in range(3)], axis=0
        )
        out[:, l * LANE : (l + 1) * LANE] = ordered


def call(kernel, ins, outs, scratch, cycles, *args, mebibytes=48):
    size = sum(a.size * 4 for a in args) + sum(math.prod(o[0]) * 4 for o in outs)
    spaces = {"v": pltpu.VMEM, "h": pl.ANY}
    places = [pl.BlockSpec(memory_space=spaces[p]) for p in ins]
    result = pl.pallas_call(
        kernel,
        out_shape=[jax.ShapeDtypeStruct(*o) for o in outs],
        in_specs=places[: len(args)],
        out_specs=places[len(args) :],
        scratch_shapes=scratch,
        compiler_params=pltpu.CompilerParams(vmem_limit_bytes=mebibytes * 2**20),
        cost_estimate=pl.CostEstimate(flops=cycles, bytes_accessed=size, transcendentals=0),
    )(*args)
    return result[0] if len(outs) == 1 else result


def on_device(
    slave_disp,
    slave_normal,
    gap_zero,
    quad_weight,
    proj_coord,
    multiplier,
    active,
    pair_owner,
    pair_slot,
    master_vol,
    surf_pick,
):
    region_count = lax.axis_size("region")
    dom_count = lax.axis_size("dom")
    owners = region_count * dom_count
    count = slave_disp.shape[1]
    width = master_vol.shape[1]
    lows = width // LANE
    part = width // dom_count
    step = 4096
    blocks = count // LANE
    exchange = functools.partial(lax.all_to_all, split_axis=0, concat_axis=0, tiled=True)
    owner = pair_owner.reshape(1, count)
    flat = (owners, 8, 128)
    everyone = ("region", "dom")
    whole, quad, wide = (1, count), (4, count), (16, count)

    volume = lax.all_gather(master_vol, "dom")
    picks = lax.all_gather(surf_pick, "dom")
    request, place, offset = call(
        functools.partial(request_kernel, step),
        "hhhvvv",
        [(flat, F32), (whole, jnp.int32), ((8, 2 * owners), jnp.int32)],
        [
            pltpu.VMEM(whole, jnp.int32),
            pltpu.VMEM(whole, jnp.int32),
            pltpu.VMEM((3, count), F32),
            pltpu.VMEM((8 * blocks, LANE), F32),
            pltpu.VMEM((owners, count), BF),
            pltpu.VMEM((2 * blocks + 4, 8, 128), F32),
            pltpu.SMEM((8, 2 * owners), jnp.int32),
            pltpu.SemaphoreType.DMA((4,)),
        ],
        10**10,
        owner,
        pair_slot.reshape(1, count),
        slave_normal,
        mebibytes=56,
    )
    recv = exchange(request, everyone)
    table = call(
        surface_kernel,
        "vvv",
        [((24 * lows, LANE), BF)],
        [pltpu.VMEM((dom_count, 24 * lows, LANE), BF)],
        10**9,
        volume,
        picks,
    )
    toward, back, slave_part = call(
        functools.partial(local_kernel, 512),
        "v" * 8,
        [(wide, F32), (wide, F32), (quad, F32)],
        [],
        10**9,
        slave_disp,
        slave_normal,
        gap_zero,
        quad_weight,
        proj_coord,
        mebibytes=56,
    )
    along = call(functools.partial(along_kernel, 32), "vvv", [(flat, F32)], [], 10**10, table, recv)
    returned = exchange(along, everyone)
    weighted_gap, multiplier_new, terms = call(
        functools.partial(update_kernel, step),
        "hhhhhhhhhhv",
        [(quad, F32), (quad, F32), (flat, F32)],
        [
            pltpu.VMEM(flat, F32),
            pltpu.SMEM((8, 2 * owners), jnp.int32),
            pltpu.VMEM(whole, jnp.int32),
            pltpu.VMEM(wide, F32),
            pltpu.VMEM(wide, F32),
            pltpu.VMEM(quad, F32),
            pltpu.VMEM(quad, F32),
            pltpu.VMEM(quad, jnp.int32),
            pltpu.VMEM(quad, F32),
            pltpu.VMEM(quad, F32),
            pltpu.VMEM((8 * blocks, LANE), BF),
            pltpu.VMEM((8 * blocks, LANE), F32),
            pltpu.VMEM((2 * blocks + 4, 8, 128), F32),
            pltpu.SemaphoreType.DMA((10,)),
        ],
        2 * 10**10,
        returned,
        offset,
        place,
        toward,
        back,
        slave_part,
        multiplier,
        active,
        mebibytes=56,
    )
    factor = exchange(terms, everyone)
    forces = call(
        functools.partial(force_kernel, 32),
        "vvv",
        [((dom_count, 12, part), F32)],
        [pltpu.VMEM((24 * lows, LANE), F32)],
        10**10,
        recv,
        factor,
    )
    moved = exchange(forces, "dom")
    master_force = call(place_kernel, "vvv", [((12, width), F32)], [], 10**9, moved, surf_pick)
    return (weighted_gap, multiplier_new, master_force)


def solution(mesh):
    both = ("region", "dom")
    return jax.shard_map(
        on_device,
        mesh=mesh,
        in_specs=(P(None, both),) * 7 + (P(both, None), P(both), P(None, both), P(both, None)),
        out_specs=(P(None, both),) * 3,
        check_vma=False,
    )
```

```python
import functools
import math

import jax
import jax.numpy as jnp
from jax import lax
from jax.experimental import pallas as pl
from jax.experimental.pallas import tpu as pltpu
from jax.sharding import PartitionSpec as P

gauss_point = 1.0 / math.sqrt(3.0)
node_xs = [-1.0, 1.0, 1.0, -1.0]
node_ys = [-1.0, -1.0, 1.0, 1.0]
point_xs = [-gauss_point, gauss_point, gauss_point, -gauss_point]
point_ys = [-gauss_point, -gauss_point, gauss_point, gauss_point]
slave_table = [
    [(1.0 + node_xs[c] * point_xs[q]) * (1.0 + node_ys[c] * point_ys[q]) * 0.25 for q in range(4)]
    for c in range(4)
]

BF = jnp.bfloat16
F32 = jnp.float32
LANE = 256

UNROLL = 32
NN = (((1,), (0,)), ((), ()))
NT = (((1,), (1,)), ((), ()))


def sub_iota(rows, cols):
    return lax.broadcasted_iota(jnp.int32, (rows, cols), 0)


def split(values):
    high = values.astype(BF)
    return high, (values - high.astype(F32)).astype(BF)


def onehot(index, size):
    n = index.shape[1]
    base = (jnp.broadcast_to(index, (16, n)) - sub_iota(16, n)).astype(F32).astype(BF)
    one, zero = jnp.ones((16, n), BF), jnp.zeros((16, n), BF)
    return jnp.concatenate(
        [jnp.where(base == jnp.asarray(16 * g, BF), one, zero) for g in range(size // 16)], axis=0
    )


def grab(table, index, apart):
    half = table.shape[0] // 2
    hot = onehot(index, LANE)
    if apart:
        first = lax.dot_general(table[0:half], hot, NN, preferred_element_type=F32)
        return first + lax.dot_general(table[half:], hot, NN, preferred_element_type=F32)
    found = lax.dot_general(table, hot, NN, preferred_element_type=F32)
    return found[0:half] + found[half:]


def spread(index, values, group, count):
    n = index.shape[1]
    base = (jnp.broadcast_to(index, (16, n)) - sub_iota(16, n) // (16 // group)).astype(F32).astype(BF)
    zero = jnp.zeros((16, n), BF)
    return [
        [jnp.where(base == jnp.asarray(group * g, BF), v, zero) for g in range(count // group)]
        for v in values
    ]


def fill_table(rows, table):
    lows = rows.shape[1] // LANE
    parts = [rows[0:8, l * LANE : (l + 1) * LANE] for l in range(lows)]
    parts += [rows[8:12, l * LANE : (l + 1) * LANE] for l in range(lows)]
    high, low = split(jnp.concatenate(parts, axis=0))
    table[0 : 12 * lows, :] = high
    table[12 * lows :, :] = low


def pick_table(table, index, lows):
    n = index.shape[1]
    grabbed = grab(table, index % LANE, False)
    low = jnp.broadcast_to(index // LANE, (8, n))
    pair = low - sub_iota(8, n) // 4
    first = jnp.zeros((8, n), F32)
    for l in range(lows):
        at = 8 * l
        value = grabbed[at : at + 8]
        first = jnp.where(low == l, value, first)
    second = jnp.zeros((8, n), F32)
    for l in range(lows // 2):
        at = 8 * lows + 8 * l
        value = grabbed[at : at + 8]
        second = jnp.where(pair == 2 * l, value, second)
    return first, second[0:4] + second[4:8]


def add_table(first, second, index, lows):
    high, low = split(first)
    group = jnp.concatenate([high.astype(F32), low.astype(F32)], axis=0).astype(BF)
    wide = spread(index // LANE, [group], 1, lows)[0]
    high, low = split(second)
    high, low = high.astype(F32), low.astype(F32)
    group = jnp.concatenate([high, low, high, low], axis=0).astype(BF)
    narrow = spread(index // LANE, [group], 2, lows)[0]
    stacked = jnp.concatenate(wide + narrow, axis=0)
    return lax.dot_general(
        stacked, onehot(index % LANE, LANE), NT, preferred_element_type=F32
    )


def table_part(total, lows, l):
    first = total[16 * l : 16 * l + 8] + total[16 * l + 8 : 16 * l + 16]
    at = 16 * lows + 8 * l
    return first, total[at : at + 4] + total[at + 4 : at + 8]


def pick_kernel(vol, pick, out, table):
    width = vol.shape[1]
    lows = width // LANE
    rows = vol[...]
    fill_table(
        jnp.concatenate([rows[3 * c + j : 3 * c + j + 1] for j in range(3) for c in range(4)], axis=0),
        table,
    )
    count, _, part = out.shape
    for k in range(count):
        first, second = pick_table(table[...], pick[:, k * part : (k + 1) * part], lows)
        out[k, 0:8, :] = first
        out[k, 8:12, :] = second


def lane_iota(rows, cols):
    return lax.broadcasted_iota(jnp.int32, (rows, cols), 1)


def sort_terms(values, place, lows):
    high, low = split(jnp.concatenate([values] * 4, axis=0))
    first, second = spread(place // LANE, [high, low], 4, lows)
    stacked = jnp.concatenate(first + second, axis=0)
    return lax.dot_general(stacked, onehot(place % LANE, LANE), NT, preferred_element_type=F32)


def cut_windows(total, offsets, ordered, out, masked):
    half = total.shape[0] // 2
    sums = total[0:half, :] + total[half:, :]
    top = sub_iota(8, 128) < 4
    groups = half // 8
    left = [sums[8 * g : 8 * g + 8, 0:128] for g in range(groups)]
    right = [sums[8 * g : 8 * g + 8, 128:256] for g in range(groups)]
    turned_left = [pltpu.roll(v, 4, 0) for v in left] + [jnp.zeros((8, 128), F32)]
    turned_right = [pltpu.roll(v, 4, 0) for v in right]
    for g in range(groups):
        ordered[4 * g] = jnp.where(top, left[g], turned_right[g])
        ordered[4 * g + 1] = jnp.where(top, right[g], left[g])
        ordered[4 * g + 2] = jnp.where(top, turned_left[g], right[g])
        ordered[4 * g + 3] = jnp.where(top, turned_right[g], turned_left[g + 1])
    for g in range(4 * groups, ordered.shape[0]):
        ordered[g] = jnp.zeros((8, 128), F32)
    lane = lane_iota(8, 128)
    number = lane + jnp.where(top, 0, 128)

    def window(i, _):
        for u in range(UNROLL):
            o = i * UNROLL + u
            start = offsets[0, o]
            block, shift = start // 128, start % 128
            joined = jnp.where(lane >= shift, ordered[block], ordered[block + 1])
            joined = pltpu.roll(joined, (128 - shift) % 128, 1)
            if masked:
                joined = jnp.where(number < offsets[0, o + 1] - start, joined, 0.0)
            out[o] = joined
        return 0

    lax.fori_loop(0, out.shape[0] // UNROLL, window, 0)


def merge_windows(windows, offsets, merged, table):
    lane = lane_iota(8, 128)
    top = sub_iota(8, 128) < 4

    def window(i, carry):
        for u in range(UNROLL):
            o = i * UNROLL + u
            start, later = offsets[0, o], offsets[0, o + 1]
            block, shift = start // 128, start % 128
            value = pltpu.roll(windows[o], shift, 1)
            turned = pltpu.roll(value, 4, 0)
            one, two = jnp.where(top, value, turned), jnp.where(top, turned, value)
            first = jnp.where(lane >= shift, one, carry)
            second = jnp.where(lane >= shift, two, one)
            merged[block] = first
            merged[block + 1] = second
            merged[block + 2] = two
            ahead = later // 128 - block
            carry = jnp.where(ahead == 0, first, jnp.where(ahead == 1, second, two))
        return carry

    lax.fori_loop(0, windows.shape[0] // UNROLL, window, jnp.zeros((8, 128), F32))
    half = table.shape[0] // 2
    left, right = [], []
    for g in range(half // 8):
        left.append(jnp.where(top, merged[4 * g], merged[4 * g + 2]))
        right.append(jnp.where(top, merged[4 * g + 1], merged[4 * g + 3]))
    both = jnp.concatenate([jnp.concatenate(left, axis=0), jnp.concatenate(right, axis=0)], axis=1)
    high, low = split(both)
    table[0:half, :] = high
    table[half:, :] = low


def request_kernel(step, owner_hbm, slot_hbm, normal_hbm, out, place, offset, owner, slot, normal, total, named, before, ordered, scalars, sems):
    copies = [
        pltpu.make_async_copy(a, b, sems.at[i])
        for i, (a, b) in enumerate(((owner_hbm, owner), (slot_hbm, slot), (normal_hbm, normal)))
    ]
    for copy in copies:
        copy.start()
    count = owner.shape[1]
    owners = out.shape[0]
    lows = count // LANE
    total[...] = jnp.zeros_like(total)
    copies[0].wait()

    groups = owners // 16

    def lookup(names, columns):
        found = names[0:16] * columns[0:16]
        for g in range(1, groups):
            found = found + names[16 * g : 16 * g + 16] * columns[16 * g : 16 * g + 16]
        return jnp.sum(found.astype(F32), axis=0, keepdims=True)

    def tally(i, sums):
        for u in range(step // 256):
            lanes = pl.ds(pl.multiple_of(i * step + u * 256, 256), 256)
            names = onehot(owner[:, lanes], owners)
            named[:, lanes] = names
            before[:, lanes] = lookup(names, sums)
            sums = sums + names
        return sums

    sums = lax.fori_loop(0, count // step, tally, jnp.zeros((owners, 256), BF))
    counts = lax.dot_general(sums, jnp.ones((256, 256), BF), NN, preferred_element_type=F32).astype(BF)
    lower = (sub_iota(owners, owners) > lane_iota(owners, owners)).astype(F32).astype(BF)
    upper = (sub_iota(256, 256) < lane_iota(256, 256)).astype(F32).astype(BF)
    base = lax.dot_general(lower, counts, NN, preferred_element_type=F32)
    high, low = split(base + lax.dot_general(sums, upper, NN, preferred_element_type=F32))
    counts = lax.dot_general(jnp.ones((16, 256), BF), sums, NT, preferred_element_type=F32).astype(BF)
    upper = (sub_iota(owners, 2 * owners) < lane_iota(owners, 2 * owners)).astype(F32).astype(BF)
    offset[...] = lax.dot_general(counts, upper, NN, preferred_element_type=F32)[0:8].astype(jnp.int32)
    save = pltpu.make_async_copy(offset, scalars, sems.at[3])
    save.start()

    def ranks(i, _):
        for u in range(step // 256):
            lanes = pl.ds(pl.multiple_of(i * step + u * 256, 256), 256)
            names = named[:, lanes]
            found = before[:, lanes] + lookup(names, high) + lookup(names, low)
            place[:, lanes] = found.astype(jnp.int32)
        return 0

    lax.fori_loop(0, count // step, ranks, 0)
    copies[1].wait()
    copies[2].wait()

    def slots(i, _):
        lanes = pl.ds(pl.multiple_of(i * step, step), step)
        values = jnp.concatenate([slot[:, lanes].astype(F32), normal[:, lanes]], axis=0)
        total[...] += sort_terms(values, place[:, lanes], lows)
        return 0

    lax.fori_loop(0, count // step, slots, 0)
    save.wait()
    cut_windows(total, scalars, ordered, out, True)


def along_kernel(group, surf, recv, out, table):
    lows = surf.shape[0] * surf.shape[2] // LANE
    fill_table(jnp.concatenate([surf[s] for s in range(surf.shape[0])], axis=1), table)

    def step(i, _):
        parts = [recv[i * group + u] for u in range(group)]
        block = jnp.concatenate([p[4 * h : 4 * h + 4] for p in parts for h in range(2)], axis=1)
        index = block[0:1].astype(jnp.int32)
        first, second = pick_table(table[...], index, lows)
        along = first[0:4] * block[1:2] + first[4:8] * block[2:3] + second * block[3:4]
        for u in range(group):
            for h in range(2):
                at = (2 * u + h) * 128
                out[i * group + u, 4 * h : 4 * h + 4, :] = along[:, at : at + 128]
        return 0

    lax.fori_loop(0, recv.shape[0] // group, step, 0)


def signs(xs, inner):
    sub = sub_iota(8, 1)

    def column(number):
        value = jnp.full((8, 1), xs[3], F32)
        for c in range(3):
            value = jnp.where(number == c, xs[c], value)
        return value

    return [column(sub % 4)] * 2 if inner else [column(sub // 4), column(sub // 4 + 2)]


def local_kernel(step, disp, normal, gap, weight, proj, toward, back, part):
    count = disp.shape[1]
    sub4 = sub_iota(4, 1)

    def column(xs):
        value = jnp.full((4, 1), xs[3], F32)
        for a in range(3):
            value = jnp.where(sub4 == a, xs[a], value)
        return value

    def body(i, _):
        lanes = pl.ds(pl.multiple_of(i * step, step), step)
        p, w, d, n, g = proj[:, lanes], weight[:, lanes], disp[:, lanes], normal[:, lanes], gap[:, lanes]
        for inner, out in ((False, toward), (True, back)):
            node_x, node_y = signs(node_xs, inner), signs(node_ys, inner)
            sums = [None, None]
            for q in range(4):
                table = signs([slave_table[a][q] * 0.25 for a in range(4)], not inner)
                first = jnp.broadcast_to(p[2 * q : 2 * q + 1], (8, step))
                second = jnp.broadcast_to(p[2 * q + 1 : 2 * q + 2], (8, step))
                along = jnp.broadcast_to(w[q : q + 1], (8, step))
                for h in range(2):
                    term = (1.0 + node_x[h] * first) * (1.0 + node_y[h] * second) * (along * table[h])
                    sums[h] = term if q == 0 else sums[h] + term
            out[0:8, lanes] = sums[0]
            out[8:16, lanes] = sums[1]
        total = g
        for b in range(4):
            along = n[0:1] * d[3 * b : 3 * b + 1] + n[1:2] * d[3 * b + 1 : 3 * b + 2] + n[2:3] * d[3 * b + 2 : 3 * b + 3]
            total = total + column(slave_table[b]) * along
        points = w * total
        result = column([slave_table[a][0] for a in range(4)]) * points[0:1]
        for q in range(1, 4):
            result = result + column([slave_table[a][q] for a in range(4)]) * points[q : q + 1]
        part[:, lanes] = result
        return 0

    lax.fori_loop(0, count // step, body, 0)


def doubled(values):
    n = values.shape[1]
    rows = [jnp.broadcast_to(values[c : c + 1], (4, n)) for c in range(4)]
    return jnp.concatenate(rows[0:2], axis=0), jnp.concatenate(rows[2:4], axis=0)


def combine(factors, values):
    one, two = doubled(values)
    both = factors[0:8] * one + factors[8:16] * two
    return both[0:4] + both[4:8]


def update_kernel(step, *refs):
    inputs, outputs, out = refs[0:8], refs[8:10], refs[10]
    buffers, results = refs[11:19], refs[19:21]
    table, total, ordered, sems = refs[21:25]
    copies = [pltpu.make_async_copy(inputs[i], buffers[i], sems.at[i]) for i in range(8)]
    for copy in copies:
        copy.start()
    recv, offsets, place, toward, back, part, multiplier, active = buffers
    gap_out, new_out = results
    count = place.shape[1]
    lows = count // LANE
    total[...] = jnp.zeros_like(total)
    for copy in copies[0:2]:
        copy.wait()
    merge_windows(recv, offsets, ordered, table)
    for copy in copies[2:]:
        copy.wait()

    def body(i, _):
        lanes = pl.ds(pl.multiple_of(i * step, step), step)
        places = place[:, lanes]
        grabbed = grab(table[...], places % LANE, True)
        base = jnp.broadcast_to(places // LANE, (8, step)) - sub_iota(8, step) // 4
        along = jnp.zeros((8, step), F32)
        for g in range(lows // 2):
            along = jnp.where(base == 2 * g, grabbed[8 * g : 8 * g + 8], along)
        mortar = combine(toward[:, lanes], along[0:4] + along[4:8])
        weighted = part[:, lanes] - mortar
        lagrange = jnp.where(active[:, lanes] == 1, jnp.maximum(multiplier[:, lanes] - weighted, 0.0), 0.0)
        gap_out[:, lanes] = weighted
        new_out[:, lanes] = lagrange
        total[...] += sort_terms(combine(back[:, lanes], lagrange), places, lows)
        return 0

    lax.fori_loop(0, count // step, body, 0)
    saves = [pltpu.make_async_copy(results[i], outputs[i], sems.at[8 + i]) for i in range(2)]
    for save in saves:
        save.start()
    cut_windows(total, offsets, ordered, out, False)
    for save in saves:
        save.wait()


def force_kernel(group, recv, factor, out, total):
    lows = out.shape[0] * out.shape[2] // LANE
    total[...] = jnp.zeros_like(total)

    def step(i, _):
        parts = [recv[i * group + u] for u in range(group)]
        block = jnp.concatenate([p[4 * h : 4 * h + 4] for p in parts for h in range(2)], axis=1)
        parts = [factor[i * group + u] for u in range(group)]
        node = jnp.concatenate([p[4 * h : 4 * h + 4] for p in parts for h in range(2)], axis=1)
        index = block[0:1].astype(jnp.int32)
        first = jnp.concatenate([node * block[1:2], node * block[2:3]], axis=0)
        total[...] += add_table(first, node * block[3:4], index, lows)
        return 0

    lax.fori_loop(0, recv.shape[0] // group, step, 0)
    sums = total[...]
    per = out.shape[2] // LANE
    for l in range(lows):
        first, second = table_part(sums, lows, l)
        lanes = slice(l % per * LANE, (l % per + 1) * LANE)
        out[l // per, 0:8, lanes] = first
        out[l // per, 8:12, lanes] = second


def place_kernel(moved, pick, out):
    lows = out.shape[1] // LANE
    rows = jnp.concatenate([moved[k] for k in range(moved.shape[0])], axis=1)
    sums = add_table(rows[0:8], rows[8:12], pick[...], lows)
    for l in range(lows):
        first, second = table_part(sums, lows, l)
        both = jnp.concatenate([first, second], axis=0)
        ordered = jnp.concatenate(
            [both[4 * j + c : 4 * j + c + 1] for c in range(4) for j in range(3)], axis=0
        )
        out[:, l * LANE : (l + 1) * LANE] = ordered


def call(kernel, ins, outs, scratch, cycles, *args, mebibytes=48):
    size = sum(a.size * 4 for a in args) + sum(math.prod(o[0]) * 4 for o in outs)
    spaces = {"v": pltpu.VMEM, "h": pl.ANY}
    places = [pl.BlockSpec(memory_space=spaces[p]) for p in ins]
    result = pl.pallas_call(
        kernel,
        out_shape=[jax.ShapeDtypeStruct(*o) for o in outs],
        in_specs=places[: len(args)],
        out_specs=places[len(args) :],
        scratch_shapes=scratch,
        compiler_params=pltpu.CompilerParams(vmem_limit_bytes=mebibytes * 2**20),
        cost_estimate=pl.CostEstimate(flops=cycles, bytes_accessed=size, transcendentals=0),
    )(*args)
    return result[0] if len(outs) == 1 else result


def on_device(
    slave_disp,
    slave_normal,
    gap_zero,
    quad_weight,
    proj_coord,
    multiplier,
    active,
    pair_owner,
    pair_slot,
    master_vol,
    surf_pick,
):
    region_count = lax.axis_size("region")
    dom_count = lax.axis_size("dom")
    owners = region_count * dom_count
    count = slave_disp.shape[1]
    width = master_vol.shape[1]
    lows = width // LANE
    part = width // dom_count
    step = 4096
    blocks = count // LANE
    exchange = functools.partial(lax.all_to_all, split_axis=0, concat_axis=0, tiled=True)
    owner = pair_owner.reshape(1, count)
    flat = (owners, 8, 128)
    everyone = ("region", "dom")
    whole, quad, wide = (1, count), (4, count), (16, count)

    table = pltpu.VMEM((24 * lows, LANE), BF)
    picked = call(pick_kernel, "vvv", [((dom_count, 12, part), F32)], [table], 10**9, master_vol, surf_pick, mebibytes=60)
    surf = exchange(picked, "dom")
    request, place, offset = call(
        functools.partial(request_kernel, 2 * step),
        "hhhvvv",
        [(flat, F32), (whole, jnp.int32), ((8, 2 * owners), jnp.int32)],
        [
            pltpu.VMEM(whole, jnp.int32),
            pltpu.VMEM(whole, jnp.int32),
            pltpu.VMEM((3, count), F32),
            pltpu.VMEM((8 * blocks, LANE), F32),
            pltpu.VMEM((owners, count), BF),
            pltpu.VMEM(whole, F32),
            pltpu.VMEM((2 * blocks + 4, 8, 128), F32),
            pltpu.SMEM((8, 2 * owners), jnp.int32),
            pltpu.SemaphoreType.DMA((4,)),
        ],
        10**10,
        owner,
        pair_slot.reshape(1, count),
        slave_normal,
        mebibytes=56,
    )
    recv = exchange(request, everyone)
    toward, back, slave_part = call(
        functools.partial(local_kernel, 512),
        "v" * 8,
        [(wide, F32), (wide, F32), (quad, F32)],
        [],
        10**9,
        slave_disp,
        slave_normal,
        gap_zero,
        quad_weight,
        proj_coord,
        mebibytes=56,
    )
    along = call(functools.partial(along_kernel, 32), "vvv", [(flat, F32)], [table], 10**10, surf, recv)
    returned = exchange(along, everyone)
    weighted_gap, multiplier_new, terms = call(
        functools.partial(update_kernel, step),
        "hhhhhhhhhhv",
        [(quad, F32), (quad, F32), (flat, F32)],
        [
            pltpu.VMEM(flat, F32),
            pltpu.SMEM((8, 2 * owners), jnp.int32),
            pltpu.VMEM(whole, jnp.int32),
            pltpu.VMEM(wide, F32),
            pltpu.VMEM(wide, F32),
            pltpu.VMEM(quad, F32),
            pltpu.VMEM(quad, F32),
            pltpu.VMEM(quad, jnp.int32),
            pltpu.VMEM(quad, F32),
            pltpu.VMEM(quad, F32),
            pltpu.VMEM((8 * blocks, LANE), BF),
            pltpu.VMEM((8 * blocks, LANE), F32),
            pltpu.VMEM((2 * blocks + 4, 8, 128), F32),
            pltpu.SemaphoreType.DMA((10,)),
        ],
        2 * 10**10,
        returned,
        offset,
        place,
        toward,
        back,
        slave_part,
        multiplier,
        active,
        mebibytes=56,
    )
    factor = exchange(terms, everyone)
    forces = call(
        functools.partial(force_kernel, 64),
        "vvv",
        [((dom_count, 12, part), F32)],
        [pltpu.VMEM((24 * lows, LANE), F32)],
        10**10,
        recv,
        factor,
    )
    moved = exchange(forces, "dom")
    master_force = call(place_kernel, "vvv", [((12, width), F32)], [], 10**9, moved, surf_pick)
    return (weighted_gap, multiplier_new, master_force)


def solution(mesh):
    both = ("region", "dom")
    return jax.shard_map(
        on_device,
        mesh=mesh,
        in_specs=(P(None, both),) * 7 + (P(both, None), P(both), P(None, both), P(both, None)),
        out_specs=(P(None, both),) * 3,
        check_vma=False,
    )
```

```python
import functools
import math

import jax
import jax.numpy as jnp
from jax import lax
from jax.experimental import pallas as pl
from jax.experimental.pallas import tpu as pltpu
from jax.sharding import PartitionSpec as P

gauss_point = 1.0 / math.sqrt(3.0)
node_xs = [-1.0, 1.0, 1.0, -1.0]
node_ys = [-1.0, -1.0, 1.0, 1.0]
point_xs = [-gauss_point, gauss_point, gauss_point, -gauss_point]
point_ys = [-gauss_point, -gauss_point, gauss_point, gauss_point]
slave_table = [
    [(1.0 + node_xs[c] * point_xs[q]) * (1.0 + node_ys[c] * point_ys[q]) * 0.25 for q in range(4)]
    for c in range(4)
]

BF = jnp.bfloat16
F32 = jnp.float32
LANE = 256

UNROLL = 32
NN = (((1,), (0,)), ((), ()))
NT = (((1,), (1,)), ((), ()))


def sub_iota(rows, cols):
    return lax.broadcasted_iota(jnp.int32, (rows, cols), 0)


def split(values):
    high = values.astype(BF)
    return high, (values - high.astype(F32)).astype(BF)


def onehot(index, size):
    n = index.shape[1]
    base = (jnp.broadcast_to(index, (16, n)) - sub_iota(16, n)).astype(F32).astype(BF)
    one, zero = jnp.ones((16, n), BF), jnp.zeros((16, n), BF)
    return jnp.concatenate(
        [jnp.where(base == jnp.asarray(16 * g, BF), one, zero) for g in range(size // 16)], axis=0
    )


def grab(table, index, apart):
    half = table.shape[0] // 2
    hot = onehot(index, LANE)
    if apart:
        first = lax.dot_general(table[0:half], hot, NN, preferred_element_type=F32)
        return first + lax.dot_general(table[half:], hot, NN, preferred_element_type=F32)
    found = lax.dot_general(table, hot, NN, preferred_element_type=F32)
    return found[0:half] + found[half:]


def spread(index, values, group, count):
    n = index.shape[1]
    base = (jnp.broadcast_to(index, (16, n)) - sub_iota(16, n) // (16 // group)).astype(F32).astype(BF)
    zero = jnp.zeros((16, n), BF)
    return [
        [jnp.where(base == jnp.asarray(group * g, BF), v, zero) for g in range(count // group)]
        for v in values
    ]


def fill_table(rows, table):
    lows = rows.shape[1] // LANE
    parts = [rows[0:8, l * LANE : (l + 1) * LANE] for l in range(lows)]
    parts += [rows[8:12, l * LANE : (l + 1) * LANE] for l in range(lows)]
    high, low = split(jnp.concatenate(parts, axis=0))
    table[0 : 12 * lows, :] = high
    table[12 * lows :, :] = low


def pick_table(table, index, lows):
    n = index.shape[1]
    grabbed = grab(table, index % LANE, False)
    low = jnp.broadcast_to(index // LANE, (8, n))
    pair = low - sub_iota(8, n) // 4
    first = jnp.zeros((8, n), F32)
    for l in range(lows):
        at = 8 * l
        value = grabbed[at : at + 8]
        first = jnp.where(low == l, value, first)
    second = jnp.zeros((8, n), F32)
    for l in range(lows // 2):
        at = 8 * lows + 8 * l
        value = grabbed[at : at + 8]
        second = jnp.where(pair == 2 * l, value, second)
    return first, second[0:4] + second[4:8]


def add_table(first, second, index, lows):
    high, low = split(first)
    group = jnp.concatenate([high.astype(F32), low.astype(F32)], axis=0).astype(BF)
    wide = spread(index // LANE, [group], 1, lows)[0]
    high, low = split(second)
    high, low = high.astype(F32), low.astype(F32)
    group = jnp.concatenate([high, low, high, low], axis=0).astype(BF)
    narrow = spread(index // LANE, [group], 2, lows)[0]
    stacked = jnp.concatenate(wide + narrow, axis=0)
    return lax.dot_general(
        stacked, onehot(index % LANE, LANE), NT, preferred_element_type=F32
    )


def table_part(total, lows, l):
    first = total[16 * l : 16 * l + 8] + total[16 * l + 8 : 16 * l + 16]
    at = 16 * lows + 8 * l
    return first, total[at : at + 4] + total[at + 4 : at + 8]


def pick_kernel(vol, pick, out, table):
    width = vol.shape[1]
    lows = width // LANE
    rows = vol[...]
    fill_table(
        jnp.concatenate([rows[3 * c + j : 3 * c + j + 1] for j in range(3) for c in range(4)], axis=0),
        table,
    )
    count, _, part = out.shape
    for k in range(count):
        first, second = pick_table(table[...], pick[:, k * part : (k + 1) * part], lows)
        out[k, 0:8, :] = first
        out[k, 8:12, :] = second


def lane_iota(rows, cols):
    return lax.broadcasted_iota(jnp.int32, (rows, cols), 1)


def sort_terms(values, place, lows):
    pieces = []
    for value in values:
        pieces += split(jnp.concatenate([value] * 4, axis=0))
    stacked = jnp.concatenate(sum(spread(place // LANE, pieces, 4, lows), []), axis=0)
    return lax.dot_general(stacked, onehot(place % LANE, LANE), NT, preferred_element_type=F32)


def sorted_sums(total, lows):
    rows = 4 * lows
    return [total[i : i + rows] + total[i + rows : i + 2 * rows] for i in range(0, total.shape[0], 2 * rows)]


def cut_windows(sums, offsets, ordered, out, masked):
    top = sub_iota(8, 128) < 4
    groups = sums.shape[0] // 8
    left = [sums[8 * g : 8 * g + 8, 0:128] for g in range(groups)]
    right = [sums[8 * g : 8 * g + 8, 128:256] for g in range(groups)]
    turned_left = [pltpu.roll(v, 4, 0) for v in left] + [jnp.zeros((8, 128), F32)]
    turned_right = [pltpu.roll(v, 4, 0) for v in right]
    for g in range(groups):
        ordered[4 * g] = jnp.where(top, left[g], turned_right[g])
        ordered[4 * g + 1] = jnp.where(top, right[g], left[g])
        ordered[4 * g + 2] = jnp.where(top, turned_left[g], right[g])
        ordered[4 * g + 3] = jnp.where(top, turned_right[g], turned_left[g + 1])
    for g in range(4 * groups, ordered.shape[0]):
        ordered[g] = jnp.zeros((8, 128), F32)
    lane = lane_iota(8, 128)
    number = lane + jnp.where(top, 0, 128)

    def window(i, _):
        for u in range(UNROLL):
            o = i * UNROLL + u
            start = offsets[0, o]
            block, shift = start // 128, start % 128
            joined = jnp.where(lane >= shift, ordered[block], ordered[block + 1])
            joined = pltpu.roll(joined, (128 - shift) % 128, 1)
            if masked:
                joined = jnp.where(number < offsets[0, o + 1] - start, joined, 0.0)
            out[o] = joined
        return 0

    lax.fori_loop(0, out.shape[0] // UNROLL, window, 0)


def merge_windows(windows, offsets, merged, lows):
    lane = lane_iota(8, 128)
    top = sub_iota(8, 128) < 4

    def window(i, carry):
        for u in range(UNROLL):
            o = i * UNROLL + u
            start, later = offsets[0, o], offsets[0, o + 1]
            block, shift = start // 128, start % 128
            value = pltpu.roll(windows[o], shift, 1)
            turned = pltpu.roll(value, 4, 0)
            one, two = jnp.where(top, value, turned), jnp.where(top, turned, value)
            first = jnp.where(lane >= shift, one, carry)
            second = jnp.where(lane >= shift, two, one)
            merged[block] = first
            merged[block + 1] = second
            merged[block + 2] = two
            ahead = later // 128 - block
            carry = jnp.where(ahead == 0, first, jnp.where(ahead == 1, second, two))
        return carry

    lax.fori_loop(0, windows.shape[0] // UNROLL, window, jnp.zeros((8, 128), F32))
    left, right = [], []
    for g in range(lows // 2):
        left.append(jnp.where(top, merged[4 * g], merged[4 * g + 2]))
        right.append(jnp.where(top, merged[4 * g + 1], merged[4 * g + 3]))
    return jnp.concatenate([jnp.concatenate(left, axis=0), jnp.concatenate(right, axis=0)], axis=1)


def request_kernel(step, owner_hbm, slot_hbm, normal_hbm, out, place, offset, owner, slot, normal, total, named, before, ordered, scalars, sems):
    copies = [
        pltpu.make_async_copy(a, b, sems.at[i])
        for i, (a, b) in enumerate(((owner_hbm, owner), (slot_hbm, slot), (normal_hbm, normal)))
    ]
    for copy in copies:
        copy.start()
    count = owner.shape[1]
    owners = out.shape[0]
    lows = count // LANE
    total[...] = jnp.zeros_like(total)
    copies[0].wait()

    groups = owners // 16

    def lookup(names, columns):
        found = names[0:16] * columns[0:16]
        for g in range(1, groups):
            found = found + names[16 * g : 16 * g + 16] * columns[16 * g : 16 * g + 16]
        return jnp.sum(found.astype(F32), axis=0, keepdims=True)

    def tally(i, sums):
        for u in range(step // 256):
            lanes = pl.ds(pl.multiple_of(i * step + u * 256, 256), 256)
            names = onehot(owner[:, lanes], owners)
            named[:, lanes] = names
            before[:, lanes] = lookup(names, sums)
            sums = sums + names
        return sums

    sums = lax.fori_loop(0, count // step, tally, jnp.zeros((owners, 256), BF))
    counts = lax.dot_general(sums, jnp.ones((256, 256), BF), NN, preferred_element_type=F32).astype(BF)
    lower = (sub_iota(owners, owners) > lane_iota(owners, owners)).astype(F32).astype(BF)
    upper = (sub_iota(256, 256) < lane_iota(256, 256)).astype(F32).astype(BF)
    base = lax.dot_general(lower, counts, NN, preferred_element_type=F32)
    high, low = split(base + lax.dot_general(sums, upper, NN, preferred_element_type=F32))
    counts = lax.dot_general(jnp.ones((16, 256), BF), sums, NT, preferred_element_type=F32).astype(BF)
    upper = (sub_iota(owners, 2 * owners) < lane_iota(owners, 2 * owners)).astype(F32).astype(BF)
    offset[...] = lax.dot_general(counts, upper, NN, preferred_element_type=F32)[0:8].astype(jnp.int32)
    save = pltpu.make_async_copy(offset, scalars, sems.at[3])
    save.start()

    def ranks(i, _):
        for u in range(step // 256):
            lanes = pl.ds(pl.multiple_of(i * step + u * 256, 256), 256)
            names = named[:, lanes]
            found = before[:, lanes] + lookup(names, high) + lookup(names, low)
            place[:, lanes] = found.astype(jnp.int32)
        return 0

    lax.fori_loop(0, count // step, ranks, 0)
    copies[1].wait()
    copies[2].wait()

    def slots(i, _):
        lanes = pl.ds(pl.multiple_of(i * step, step), step)
        values = jnp.concatenate([slot[:, lanes].astype(F32), normal[:, lanes]], axis=0)
        total[...] += sort_terms([values], place[:, lanes], lows)
        return 0

    lax.fori_loop(0, count // step, slots, 0)
    save.wait()
    cut_windows(sorted_sums(total, lows)[0], scalars, ordered, out, True)


def along_kernel(group, surf, recv, out, table):
    lows = surf.shape[0] * surf.shape[2] // LANE
    fill_table(jnp.concatenate([surf[s] for s in range(surf.shape[0])], axis=1), table)

    def step(i, _):
        parts = [recv[i * group + u] for u in range(group)]
        block = jnp.concatenate([p[4 * h : 4 * h + 4] for p in parts for h in range(2)], axis=1)
        index = block[0:1].astype(jnp.int32)
        first, second = pick_table(table[...], index, lows)
        along = first[0:4] * block[1:2] + first[4:8] * block[2:3] + second * block[3:4]
        for u in range(group):
            for h in range(2):
                at = (2 * u + h) * 128
                out[i * group + u, 4 * h : 4 * h + 4, :] = along[:, at : at + 128]
        return 0

    lax.fori_loop(0, recv.shape[0] // group, step, 0)


def by_node(values, number):
    result = jnp.full(number.shape, values[3], F32)
    for c in range(3):
        result = jnp.where(number == c, values[c], result)
    return result


def turned(values, by):
    if by % 4 == 0:
        return values
    by = by % 4
    row = lax.broadcasted_iota(jnp.int32, values.shape, 1) % 4
    return jnp.where(row < 4 - by, pltpu.roll(values, 8 - by, 1), pltpu.roll(values, 4 - by, 1))


def sort_kernel(step, place, proj, out, total):
    lows = place.shape[1] // LANE
    total[...] = jnp.zeros_like(total)

    def body(i, _):
        lanes = pl.ds(pl.multiple_of(i * step, step), step)
        p = proj[:, lanes]
        values = [jnp.concatenate([p[2 * q + k : 2 * q + k + 1] for q in range(4)], axis=0) for k in range(2)]
        total[...] += sort_terms(values, place[:, lanes], lows)
        return 0

    lax.fori_loop(0, place.shape[1] // step, body, 0)
    for k, value in enumerate(sorted_sums(total, lows)):
        out[k] = value


def local_kernel(step, place, disp, normal, gap, weight, multiplier, active, proj, part, level, factors, total):
    count = place.shape[1]
    lows = count // LANE
    sub4 = sub_iota(4, 1)
    total[...] = jnp.zeros_like(total)

    def body(i, _):
        lanes = pl.ds(pl.multiple_of(i * step, step), step)
        w, d, n, g = weight[:, lanes], disp[:, lanes], normal[:, lanes], gap[:, lanes]
        points = g
        for b in range(4):
            along = n[0:1] * d[3 * b : 3 * b + 1] + n[1:2] * d[3 * b + 1 : 3 * b + 2] + n[2:3] * d[3 * b + 2 : 3 * b + 3]
            points = points + by_node(slave_table[b], sub4) * along
        points = w * points
        result = by_node([slave_table[a][0] for a in range(4)], sub4) * points[0:1]
        for q in range(1, 4):
            result = result + by_node([slave_table[a][q] for a in range(4)], sub4) * points[q : q + 1]
        part[:, lanes] = result
        start = jnp.where(active[:, lanes] == 1, multiplier[:, lanes] - result, -1e30)
        total[...] += sort_terms([w, start], place[:, lanes], lows)
        return 0

    lax.fori_loop(0, count // step, body, 0)
    w, start = sorted_sums(total, lows)
    level[...] = start
    first, second, w = [v.reshape(-1, 8, LANE) for v in (proj[0], proj[1], w)]
    row = lax.broadcasted_iota(jnp.int32, (1, 8, 1), 1) % 4
    sums = [None] * 4
    for e in range(4):
        x, y = turned(first, e), turned(second, e)
        scaled = turned(w, e) * by_node([slave_table[a][(a + e) % 4] * 0.25 for a in range(4)], row)
        for d in range(4):
            node = (row + d) % 4
            term = (1.0 + by_node(node_xs, node) * x) * (1.0 + by_node(node_ys, node) * y) * scaled
            sums[d] = term if e == 0 else sums[d] + term
    for d in range(4):
        factors[d] = sums[d].reshape(-1, LANE)


def update_kernel(*refs):
    inputs, out, mortar_out = refs[0:4], refs[4], refs[5]
    recv, offsets, level, factors = refs[6:10]
    ordered, sems = refs[10:12]
    copies = [pltpu.make_async_copy(inputs[i], refs[6 + i], sems.at[i]) for i in range(4)]
    for copy in copies:
        copy.start()
    for copy in copies[0:2]:
        copy.wait()
    lows = level.shape[0] // 4
    along = merge_windows(recv, offsets, ordered, lows).reshape(-1, 8, LANE)
    for copy in copies[2:]:
        copy.wait()
    parts = [factors[d].reshape(-1, 8, LANE) for d in range(4)]
    mortar = parts[0] * along
    for d in range(1, 4):
        mortar = mortar + parts[d] * turned(along, d)
    mortar_out[...] = mortar.reshape(-1, LANE)
    lagrange = jnp.maximum(level[...].reshape(-1, 8, LANE) + mortar, 0.0)
    terms = parts[0] * lagrange
    for d in range(1, 4):
        terms = terms + turned(parts[d] * lagrange, 4 - d)
    cut_windows(terms.reshape(-1, LANE), offsets, ordered, out, False)


def restore_kernel(step, mortar, place, part, multiplier, active, gap_out, new_out, table):
    count = place.shape[1]
    lows = count // LANE
    half = table.shape[0] // 2
    high, low = split(mortar[...])
    table[0:half, :] = high
    table[half:, :] = low

    def body(i, _):
        lanes = pl.ds(pl.multiple_of(i * step, step), step)
        places = place[:, lanes]
        grabbed = grab(table[...], places % LANE, True)
        base = jnp.broadcast_to(places // LANE, (8, step)) - sub_iota(8, step) // 4
        found = jnp.zeros((8, step), F32)
        for g in range(lows // 2):
            found = jnp.where(base == 2 * g, grabbed[8 * g : 8 * g + 8], found)
        weighted = part[:, lanes] - (found[0:4] + found[4:8])
        gap_out[:, lanes] = weighted
        new_out[:, lanes] = jnp.where(active[:, lanes] == 1, jnp.maximum(multiplier[:, lanes] - weighted, 0.0), 0.0)
        return 0

    lax.fori_loop(0, count // step, body, 0)


def force_kernel(group, recv, factor, out, total):
    lows = out.shape[0] * out.shape[2] // LANE
    total[...] = jnp.zeros_like(total)

    def step(i, _):
        parts = [recv[i * group + u] for u in range(group)]
        block = jnp.concatenate([p[4 * h : 4 * h + 4] for p in parts for h in range(2)], axis=1)
        parts = [factor[i * group + u] for u in range(group)]
        node = jnp.concatenate([p[4 * h : 4 * h + 4] for p in parts for h in range(2)], axis=1)
        index = block[0:1].astype(jnp.int32)
        first = jnp.concatenate([node * block[1:2], node * block[2:3]], axis=0)
        total[...] += add_table(first, node * block[3:4], index, lows)
        return 0

    lax.fori_loop(0, recv.shape[0] // group, step, 0)
    sums = total[...]
    per = out.shape[2] // LANE
    for l in range(lows):
        first, second = table_part(sums, lows, l)
        lanes = slice(l % per * LANE, (l % per + 1) * LANE)
        out[l // per, 0:8, lanes] = first
        out[l // per, 8:12, lanes] = second


def place_kernel(moved, pick, out):
    lows = out.shape[1] // LANE
    rows = jnp.concatenate([moved[k] for k in range(moved.shape[0])], axis=1)
    sums = add_table(rows[0:8], rows[8:12], pick[...], lows)
    for l in range(lows):
        first, second = table_part(sums, lows, l)
        both = jnp.concatenate([first, second], axis=0)
        ordered = jnp.concatenate(
            [both[4 * j + c : 4 * j + c + 1] for c in range(4) for j in range(3)], axis=0
        )
        out[:, l * LANE : (l + 1) * LANE] = ordered


def call(kernel, ins, outs, scratch, cycles, *args, mebibytes=48):
    size = sum(a.size * 4 for a in args) + sum(math.prod(o[0]) * 4 for o in outs)
    spaces = {"v": pltpu.VMEM, "h": pl.ANY}
    places = [pl.BlockSpec(memory_space=spaces[p]) for p in ins]
    result = pl.pallas_call(
        kernel,
        out_shape=[jax.ShapeDtypeStruct(*o) for o in outs],
        in_specs=places[: len(args)],
        out_specs=places[len(args) :],
        scratch_shapes=scratch,
        compiler_params=pltpu.CompilerParams(vmem_limit_bytes=mebibytes * 2**20),
        cost_estimate=pl.CostEstimate(flops=cycles, bytes_accessed=size, transcendentals=0),
    )(*args)
    return result[0] if len(outs) == 1 else result


def on_device(
    slave_disp,
    slave_normal,
    gap_zero,
    quad_weight,
    proj_coord,
    multiplier,
    active,
    pair_owner,
    pair_slot,
    master_vol,
    surf_pick,
):
    region_count = lax.axis_size("region")
    dom_count = lax.axis_size("dom")
    owners = region_count * dom_count
    count = slave_disp.shape[1]
    width = master_vol.shape[1]
    lows = width // LANE
    part = width // dom_count
    step = 4096
    blocks = count // LANE
    exchange = functools.partial(lax.all_to_all, split_axis=0, concat_axis=0, tiled=True)
    owner = pair_owner.reshape(1, count)
    flat = (owners, 8, 128)
    everyone = ("region", "dom")
    whole, quad = (1, count), (4, count)

    table = pltpu.VMEM((24 * lows, LANE), BF)
    picked = call(pick_kernel, "vvv", [((dom_count, 12, part), F32)], [table], 10**9, master_vol, surf_pick, mebibytes=60)
    surf = exchange(picked, "dom")
    request, place, offset = call(
        functools.partial(request_kernel, 2 * step),
        "hhhvvv",
        [(flat, F32), (whole, jnp.int32), ((8, 2 * owners), jnp.int32)],
        [
            pltpu.VMEM(whole, jnp.int32),
            pltpu.VMEM(whole, jnp.int32),
            pltpu.VMEM((3, count), F32),
            pltpu.VMEM((8 * blocks, LANE), F32),
            pltpu.VMEM((owners, count), BF),
            pltpu.VMEM(whole, F32),
            pltpu.VMEM((2 * blocks + 4, 8, 128), F32),
            pltpu.SMEM((8, 2 * owners), jnp.int32),
            pltpu.SemaphoreType.DMA((4,)),
        ],
        10**10,
        owner,
        pair_slot.reshape(1, count),
        slave_normal,
        mebibytes=56,
    )
    recv = exchange(request, everyone)
    sorted_proj = call(
        functools.partial(sort_kernel, step),
        "vvv",
        [((2, 4 * blocks, LANE), F32)],
        [pltpu.VMEM((16 * blocks, LANE), F32)],
        10**10,
        place,
        proj_coord,
        mebibytes=56,
    )
    surf, sorted_proj = lax.optimization_barrier((surf, sorted_proj))
    along = call(functools.partial(along_kernel, 32), "vvv", [(flat, F32)], [table], 10**10, surf, recv)
    returned = exchange(along, everyone)
    along, sorted_proj = lax.optimization_barrier((along, sorted_proj))
    slave_part, level, factors = call(
        functools.partial(local_kernel, step),
        "v" * 11,
        [(quad, F32), ((4 * blocks, LANE), F32), ((4, 4 * blocks, LANE), F32)],
        [pltpu.VMEM((16 * blocks, LANE), F32)],
        10**10,
        place,
        slave_disp,
        slave_normal,
        gap_zero,
        quad_weight,
        multiplier,
        active,
        sorted_proj,
        mebibytes=56,
    )
    terms, mortar = call(
        update_kernel,
        "hhhhvv",
        [(flat, F32), ((4 * blocks, LANE), F32)],
        [
            pltpu.VMEM(flat, F32),
            pltpu.SMEM((8, 2 * owners), jnp.int32),
            pltpu.VMEM((4 * blocks, LANE), F32),
            pltpu.VMEM((4, 4 * blocks, LANE), F32),
            pltpu.VMEM((2 * blocks + 4, 8, 128), F32),
            pltpu.SemaphoreType.DMA((4,)),
        ],
        10**9,
        returned,
        offset,
        level,
        factors,
        mebibytes=56,
    )
    factor = exchange(terms, everyone)
    weighted_gap, multiplier_new = call(
        functools.partial(restore_kernel, step),
        "v" * 7,
        [(quad, F32), (quad, F32)],
        [pltpu.VMEM((8 * blocks, LANE), BF)],
        10**10,
        mortar,
        place,
        slave_part,
        multiplier,
        active,
        mebibytes=56,
    )
    recv, weighted_gap = lax.optimization_barrier((recv, weighted_gap))
    forces = call(
        functools.partial(force_kernel, 64),
        "vvv",
        [((dom_count, 12, part), F32)],
        [pltpu.VMEM((24 * lows, LANE), F32)],
        10**10,
        recv,
        factor,
    )
    moved = exchange(forces, "dom")
    master_force = call(place_kernel, "vvv", [((12, width), F32)], [], 10**9, moved, surf_pick)
    return (weighted_gap, multiplier_new, master_force)


def solution(mesh):
    both = ("region", "dom")
    return jax.shard_map(
        on_device,
        mesh=mesh,
        in_specs=(P(None, both),) * 7 + (P(both, None), P(both), P(None, both), P(both, None)),
        out_specs=(P(None, both),) * 3,
        check_vma=False,
    )
```

```python
import functools
import math

import jax
import jax.numpy as jnp
from jax import lax
from jax.experimental import pallas as pl
from jax.experimental.pallas import tpu as pltpu
from jax.sharding import PartitionSpec as P

gauss_point = 1.0 / math.sqrt(3.0)
node_xs = [-1.0, 1.0, 1.0, -1.0]
node_ys = [-1.0, -1.0, 1.0, 1.0]
point_xs = [-gauss_point, gauss_point, gauss_point, -gauss_point]
point_ys = [-gauss_point, -gauss_point, gauss_point, gauss_point]
slave_table = [
    [(1.0 + node_xs[c] * point_xs[q]) * (1.0 + node_ys[c] * point_ys[q]) * 0.25 for q in range(4)]
    for c in range(4)
]

BF = jnp.bfloat16
F32 = jnp.float32
LANE = 256

UNROLL = 32
PARTS = 2
NN = (((1,), (0,)), ((), ()))
NT = (((1,), (1,)), ((), ()))


def sub_iota(rows, cols):
    return lax.broadcasted_iota(jnp.int32, (rows, cols), 0)


def quotient(value, by):
    return lax.shift_right_logical(value, jnp.int32(by.bit_length() - 1))


def remainder(value, by):
    return lax.bitwise_and(value, jnp.int32(by - 1))


def split(values):
    high = values.astype(BF)
    return high, (values - high.astype(F32)).astype(BF)


def onehot(index, size):
    n = index.shape[1]
    base = (jnp.broadcast_to(index, (16, n)) - sub_iota(16, n)).astype(F32).astype(BF)
    one, zero = jnp.ones((16, n), BF), jnp.zeros((16, n), BF)
    return jnp.concatenate(
        [jnp.where(base == jnp.asarray(16 * g, BF), one, zero) for g in range(size // 16)], axis=0
    )


def grab(table, index, apart):
    half = table.shape[0] // 2
    hot = onehot(index, LANE)
    if apart:
        first = lax.dot_general(table[0:half], hot, NN, preferred_element_type=F32)
        return first + lax.dot_general(table[half:], hot, NN, preferred_element_type=F32)
    found = lax.dot_general(table, hot, NN, preferred_element_type=F32)
    return found[0:half] + found[half:]


def spread(index, values, group, count):
    n = index.shape[1]
    base = (jnp.broadcast_to(index, (16, n)) - sub_iota(16, n) // (16 // group)).astype(F32).astype(BF)
    zero = jnp.zeros((16, n), BF)
    return [
        [jnp.where(base == jnp.asarray(group * g, BF), v, zero) for g in range(count // group)]
        for v in values
    ]


def fill_table(rows, table):
    lows = rows.shape[1] // LANE
    parts = [rows[0:8, l * LANE : (l + 1) * LANE] for l in range(lows)]
    parts += [rows[8:12, l * LANE : (l + 1) * LANE] for l in range(lows)]
    high, low = split(jnp.concatenate(parts, axis=0))
    table[0 : 12 * lows, :] = high
    table[12 * lows :, :] = low


def pick_table(table, index, lows):
    n = index.shape[1]
    grabbed = grab(table, remainder(index, LANE), False)
    low = jnp.broadcast_to(quotient(index, LANE), (8, n))
    pair = low - sub_iota(8, n) // 4
    first = jnp.zeros((8, n), F32)
    for l in range(lows):
        at = 8 * l
        value = grabbed[at : at + 8]
        first = jnp.where(low == l, value, first)
    second = jnp.zeros((8, n), F32)
    for l in range(lows // 2):
        at = 8 * lows + 8 * l
        value = grabbed[at : at + 8]
        second = jnp.where(pair == 2 * l, value, second)
    return first, second[0:4] + second[4:8]


def add_table(first, second, index, lows):
    high, low = split(first)
    group = jnp.concatenate([high.astype(F32), low.astype(F32)], axis=0).astype(BF)
    wide = spread(quotient(index, LANE), [group], 1, lows)[0]
    high, low = split(second)
    high, low = high.astype(F32), low.astype(F32)
    group = jnp.concatenate([high, low, high, low], axis=0).astype(BF)
    narrow = spread(quotient(index, LANE), [group], 2, lows)[0]
    stacked = jnp.concatenate(wide + narrow, axis=0)
    return lax.dot_general(
        stacked, onehot(remainder(index, LANE), LANE), NT, preferred_element_type=F32
    )


def table_part(total, lows, l):
    first = total[16 * l : 16 * l + 8] + total[16 * l + 8 : 16 * l + 16]
    at = 16 * lows + 8 * l
    return first, total[at : at + 4] + total[at + 4 : at + 8]


def store_tile(out, k, t, first, second):
    tiles = out.shape[1] // 12
    out[k, 8 * t : 8 * t + 8, :] = first
    out[k, 8 * tiles + 4 * t : 8 * tiles + 4 * t + 4, :] = second


def load_tiles(source):
    tiles = source.shape[1] // 12
    rows = []
    for k in range(source.shape[0]):
        for t in range(tiles):
            low = source[k, 8 * tiles + 4 * t : 8 * tiles + 4 * t + 4, :]
            rows.append(jnp.concatenate([source[k, 8 * t : 8 * t + 8, :], low], axis=0))
    return jnp.concatenate(rows, axis=1)


def pick_kernel(vol, pick, out, table):
    width = vol.shape[1]
    lows = width // LANE
    rows = vol[...]
    fill_table(
        jnp.concatenate([rows[3 * c + j : 3 * c + j + 1] for j in range(3) for c in range(4)], axis=0),
        table,
    )
    count, tiles, _ = out.shape
    part = width // count
    for k in range(count):
        first, second = pick_table(table[...], pick[:, k * part : (k + 1) * part], lows)
        for t in range(tiles // 12):
            store_tile(out, k, t, first[:, t * 128 : (t + 1) * 128], second[:, t * 128 : (t + 1) * 128])


def lane_iota(rows, cols):
    return lax.broadcasted_iota(jnp.int32, (rows, cols), 1)


def sort_terms(values, place, lows):
    pieces = []
    for value in values:
        pieces += split(jnp.concatenate([value] * 4, axis=0))
    stacked = jnp.concatenate(sum(spread(quotient(place, LANE), pieces, 4, lows), []), axis=0)
    return lax.dot_general(stacked, onehot(remainder(place, LANE), LANE), NT, preferred_element_type=F32)


def sort_parts(values, place, total):
    per = place.shape[1] // PARTS
    each = total.shape[0] // PARTS

    def body(p, _):
        lanes = pl.ds(pl.multiple_of(p * per, per), per)
        rows = pl.ds(pl.multiple_of(p * each, each), each)
        total[rows, :] = sort_terms(values(lanes), remainder(place[:, lanes], per), per // LANE)
        return 0

    lax.fori_loop(0, PARTS, body, 0)


def sorted_sums(total, lows):
    rows, each = 4 * lows, total.shape[0] // PARTS
    sums = []
    for i in range(0, each, 2 * rows):
        parts = []
        for at in range(i, total.shape[0], each):
            parts.append(total[at : at + rows] + total[at + rows : at + 2 * rows])
        sums.append(jnp.concatenate(parts, axis=0))
    return sums


def cut_windows(sums, offsets, ordered, out, masked):
    top = sub_iota(8, 128) < 4
    groups = sums.shape[0] // 8
    left = [sums[8 * g : 8 * g + 8, 0:128] for g in range(groups)]
    right = [sums[8 * g : 8 * g + 8, 128:256] for g in range(groups)]
    turned_left = [pltpu.roll(v, 4, 0) for v in left] + [jnp.zeros((8, 128), F32)]
    turned_right = [pltpu.roll(v, 4, 0) for v in right]
    for g in range(groups):
        ordered[4 * g] = jnp.where(top, left[g], turned_right[g])
        ordered[4 * g + 1] = jnp.where(top, right[g], left[g])
        ordered[4 * g + 2] = jnp.where(top, turned_left[g], right[g])
        ordered[4 * g + 3] = jnp.where(top, turned_right[g], turned_left[g + 1])
    for g in range(4 * groups, ordered.shape[0]):
        ordered[g] = jnp.zeros((8, 128), F32)
    lane = lane_iota(8, 128)
    number = lane + jnp.where(top, 0, 128)

    def cut(start):
        block, shift = quotient(start, 128), remainder(start, 128)
        joined = jnp.where(lane >= shift, ordered[block], ordered[block + 1])
        return pltpu.roll(joined, remainder(128 - shift, 128), 1)

    def window(i, _):
        for u in range(UNROLL):
            o = i * UNROLL + u
            later = offsets[1, o + 1]
            back = cut(later - 256)
            if masked:
                back = jnp.where(number >= 256 + offsets[1, o] - later, back, 0.0)
            start = offsets[0, o]
            out[o] = jnp.where(number < offsets[0, o + 1] - start, cut(start), back)
        return 0

    lax.fori_loop(0, out.shape[0] // UNROLL, window, 0)


def merge_windows(windows, offsets, merged, lows):
    lane = lane_iota(8, 128)
    top = sub_iota(8, 128) < 4
    owners = windows.shape[0]
    per = 2 * lows // PARTS
    gap = 8

    def shifted(o, shift):
        value = pltpu.roll(windows[o], shift, 1)
        other = pltpu.roll(value, 4, 0)
        return jnp.where(top, value, other), jnp.where(top, other, value)

    def window(i, carry):
        front, back = carry
        for u in range(UNROLL):
            o = i * UNROLL + u
            start, later = offsets[0, o], offsets[0, o + 1]
            block, shift = quotient(start, 128), remainder(start, 128)
            one, two = shifted(o, shift)
            first = jnp.where(lane >= shift, one, front)
            second = jnp.where(lane >= shift, two, one)
            merged[block] = first
            merged[block + 1] = second
            merged[block + 2] = two
            ahead = quotient(later, 128) - block
            front = jnp.where(ahead == 0, first, jnp.where(ahead == 1, second, two))
            o = owners - 1 - o
            start, later = offsets[1, o], offsets[1, o + 1]
            block, shift = quotient(later, 128) + gap, remainder(later, 128)
            one, two = shifted(o, shift)
            second = jnp.where(lane >= shift, two, one)
            third = jnp.where(lane >= shift, back, two)
            merged[block - 2] = one
            merged[block - 1] = second
            merged[block] = third
            behind = block - gap - quotient(start, 128)
            back = jnp.where(behind == 0, third, jnp.where(behind == 1, second, one))
        return front, back

    zero = jnp.zeros((8, 128), F32)
    lax.fori_loop(0, owners // UNROLL, window, (zero, zero))
    left, right = [], []
    for g in range(lows // 2):
        at = 4 * g if 4 * g < per else 4 * g + gap
        left.append(jnp.where(top, merged[at], merged[at + 2]))
        right.append(jnp.where(top, merged[at + 1], merged[at + 3]))
    return jnp.concatenate([jnp.concatenate(left, axis=0), jnp.concatenate(right, axis=0)], axis=1)


def request_kernel(step, owner_hbm, slot_hbm, normal_hbm, out, place, offset, owner, slot, normal, total, named, before, ordered, scalars, sems):
    copies = [
        pltpu.make_async_copy(a, b, sems.at[i])
        for i, (a, b) in enumerate(((owner_hbm, owner), (slot_hbm, slot), (normal_hbm, normal)))
    ]
    for copy in copies:
        copy.start()
    count = owner.shape[1]
    owners = out.shape[0]
    lows = count // PARTS // LANE
    copies[0].wait()

    groups = owners // 16

    def lookup(names, columns):
        found = names[0:16] * columns[0:16]
        for g in range(1, groups):
            found = found + names[16 * g : 16 * g + 16] * columns[16 * g : 16 * g + 16]
        return jnp.sum(found.astype(F32), axis=0, keepdims=True)

    def tally(i, sums):
        for u in range(step // 256):
            lanes = pl.ds(pl.multiple_of(i * step + u * 256, 256), 256)
            names = onehot(owner[:, lanes], owners)
            named[:, lanes] = names
            before[:, lanes] = lookup(names, sums)
            sums = sums + names
        return sums

    lower = (sub_iota(owners, owners) > lane_iota(owners, owners)).astype(F32).astype(BF)
    upper = (sub_iota(256, 256) < lane_iota(256, 256)).astype(F32).astype(BF)
    wide = (sub_iota(owners, 2 * owners) < lane_iota(owners, 2 * owners)).astype(F32).astype(BF)
    per = count // PARTS
    bases, starts = [], []
    for p in range(PARTS):
        sums = lax.fori_loop(p * per // step, (p + 1) * per // step, tally, jnp.zeros((owners, 256), BF))
        counts = lax.dot_general(sums, jnp.ones((256, 256), BF), NN, preferred_element_type=F32).astype(BF)
        base = lax.dot_general(lower, counts, NN, preferred_element_type=F32)
        bases.append(split(base + lax.dot_general(sums, upper, NN, preferred_element_type=F32)))
        counts = lax.dot_general(jnp.ones((16, 256), BF), sums, NT, preferred_element_type=F32).astype(BF)
        starts.append(lax.dot_general(counts, wide, NN, preferred_element_type=F32)[0:8] + 1.0 * p * per)
    offset[...] = jnp.where(sub_iota(8, 2 * owners) == 0, starts[0], starts[1]).astype(jnp.int32)
    save = pltpu.make_async_copy(offset, scalars, sems.at[3])
    save.start()

    for p in range(PARTS):

        def ranks(i, _):
            for u in range(step // 256):
                lanes = pl.ds(pl.multiple_of(i * step + u * 256, 256), 256)
                names = named[:, lanes]
                found = before[:, lanes] + lookup(names, bases[p][0]) + lookup(names, bases[p][1])
                place[:, lanes] = (found + 1.0 * p * per).astype(jnp.int32)
            return 0

        lax.fori_loop(p * per // step, (p + 1) * per // step, ranks, 0)
    copies[1].wait()
    copies[2].wait()

    sort_parts(lambda lanes: [jnp.concatenate([slot[:, lanes].astype(F32), normal[:, lanes]], axis=0)], place, total)
    save.wait()
    cut_windows(sorted_sums(total, lows)[0], scalars, ordered, out, True)


def along_kernel(group, surf, recv, out, table):
    lows = table.shape[0] // 24
    fill_table(load_tiles(surf), table)

    def step(i, _):
        parts = [recv[i * group + u] for u in range(group)]
        block = jnp.concatenate([p[4 * h : 4 * h + 4] for p in parts for h in range(2)], axis=1)
        index = block[0:1].astype(jnp.int32)
        first, second = pick_table(table[...], index, lows)
        along = first[0:4] * block[1:2] + first[4:8] * block[2:3] + second * block[3:4]
        for u in range(group):
            for h in range(2):
                at = (2 * u + h) * 128
                out[i * group + u, 4 * h : 4 * h + 4, :] = along[:, at : at + 128]
        return 0

    lax.fori_loop(0, recv.shape[0] // group, step, 0)


def by_node(values, number):
    result = jnp.full(number.shape, values[3], F32)
    for c in range(3):
        result = jnp.where(number == c, values[c], result)
    return result


def turned(values, by):
    if by % 4 == 0:
        return values
    by = by % 4
    row = lax.broadcasted_iota(jnp.int32, values.shape, 1) % 4
    return jnp.where(row < 4 - by, pltpu.roll(values, 8 - by, 1), pltpu.roll(values, 4 - by, 1))


def sort_kernel(place, proj, out, total):
    def values(lanes):
        p = proj[:, lanes]
        return [jnp.concatenate([p[2 * q + k : 2 * q + k + 1] for q in range(4)], axis=0) for k in range(2)]

    sort_parts(values, place, total)
    for k, value in enumerate(sorted_sums(total, place.shape[1] // PARTS // LANE)):
        out[k] = value


def local_kernel(place, disp, normal, gap, weight, multiplier, active, proj, part, factors, total):
    sub4 = sub_iota(4, 1)

    def values(lanes):
        w, d, n, g = weight[:, lanes], disp[:, lanes], normal[:, lanes], gap[:, lanes]
        points = g
        for b in range(4):
            along = n[0:1] * d[3 * b : 3 * b + 1] + n[1:2] * d[3 * b + 1 : 3 * b + 2] + n[2:3] * d[3 * b + 2 : 3 * b + 3]
            points = points + by_node(slave_table[b], sub4) * along
        points = w * points
        result = by_node([slave_table[a][0] for a in range(4)], sub4) * points[0:1]
        for q in range(1, 4):
            result = result + by_node([slave_table[a][q] for a in range(4)], sub4) * points[q : q + 1]
        part[:, lanes] = result
        start = jnp.where(active[:, lanes] == 1, multiplier[:, lanes] - result, -1e30)
        return [w, start]

    sort_parts(values, place, total)
    w, start = sorted_sums(total, place.shape[1] // PARTS // LANE)
    factors[4] = start
    first, second, w = [v.reshape(-1, 8, LANE) for v in (proj[0], proj[1], w)]
    row = lax.broadcasted_iota(jnp.int32, (1, 8, 1), 1) % 4
    sums = [None] * 4
    for e in range(4):
        x, y = turned(first, e), turned(second, e)
        scaled = turned(w, e) * by_node([slave_table[a][(a + e) % 4] * 0.25 for a in range(4)], row)
        for d in range(4):
            node = (row + d) % 4
            term = (1.0 + by_node(node_xs, node) * x) * (1.0 + by_node(node_ys, node) * y) * scaled
            sums[d] = term if e == 0 else sums[d] + term
    for d in range(4):
        factors[d] = sums[d].reshape(-1, LANE)


def update_kernel(recv, offsets_hbm, factors_hbm, out, mortar_out, offsets, factors, ordered, sems):
    copies = [
        pltpu.make_async_copy(a, b, sems.at[i])
        for i, (a, b) in enumerate(((offsets_hbm, offsets), (factors_hbm, factors)))
    ]
    for copy in copies:
        copy.start()
    copies[0].wait()
    lows = factors.shape[1] // 4
    along = merge_windows(recv, offsets, ordered, lows).reshape(-1, 8, LANE)
    copies[1].wait()
    parts = [factors[d].reshape(-1, 8, LANE) for d in range(4)]
    mortar = parts[0] * along
    for d in range(1, 4):
        mortar = mortar + parts[d] * turned(along, d)
    mortar_out[...] = mortar.reshape(-1, LANE)
    lagrange = jnp.maximum(factors[4].reshape(-1, 8, LANE) + mortar, 0.0)
    terms = parts[0] * lagrange
    for d in range(1, 4):
        terms = terms + turned(parts[d] * lagrange, 4 - d)
    cut_windows(terms.reshape(-1, LANE), offsets, ordered, out, False)


def restore_kernel(mortar, place, part, multiplier, active, gap_out, new_out, table):
    per = place.shape[1] // PARTS
    lows = per // LANE
    rows = 4 * lows
    for p in range(PARTS):
        high, low = split(mortar[p * rows : (p + 1) * rows])
        table[p, 0:rows, :] = high
        table[p, rows:, :] = low

    def body(p, _):
        lanes = pl.ds(pl.multiple_of(p * per, per), per)
        places = remainder(place[:, lanes], per)
        grabbed = grab(table[p], remainder(places, LANE), True)
        base = jnp.broadcast_to(quotient(places, LANE), (8, per)) - sub_iota(8, per) // 4
        found = jnp.zeros((8, per), F32)
        for g in range(lows // 2):
            found = jnp.where(base == 2 * g, grabbed[8 * g : 8 * g + 8], found)
        weighted = part[:, lanes] - (found[0:4] + found[4:8])
        gap_out[:, lanes] = weighted
        new_out[:, lanes] = jnp.where(active[:, lanes] == 1, jnp.maximum(multiplier[:, lanes] - weighted, 0.0), 0.0)
        return 0

    lax.fori_loop(0, PARTS, body, 0)


def force_kernel(group, recv, factor, out, total):
    lows = total.shape[0] // 24
    total[...] = jnp.zeros_like(total)

    def step(i, _):
        parts = [recv[i * group + u] for u in range(group)]
        block = jnp.concatenate([p[4 * h : 4 * h + 4] for p in parts for h in range(2)], axis=1)
        parts = [factor[i * group + u] for u in range(group)]
        node = jnp.concatenate([p[4 * h : 4 * h + 4] for p in parts for h in range(2)], axis=1)
        index = block[0:1].astype(jnp.int32)
        first = jnp.concatenate([node * block[1:2], node * block[2:3]], axis=0)
        total[...] += add_table(first, node * block[3:4], index, lows)
        return 0

    lax.fori_loop(0, recv.shape[0] // group, step, 0)
    sums = total[...]
    per = lows // out.shape[0]
    for l in range(lows):
        first, second = table_part(sums, lows, l)
        for t in range(LANE // 128):
            lanes = slice(t * 128, (t + 1) * 128)
            store_tile(out, l // per, l % per * (LANE // 128) + t, first[:, lanes], second[:, lanes])


def place_kernel(moved, pick, out):
    lows = out.shape[1] // LANE
    rows = load_tiles(moved)
    sums = add_table(rows[0:8], rows[8:12], pick[...], lows)
    for l in range(lows):
        first, second = table_part(sums, lows, l)
        both = jnp.concatenate([first, second], axis=0)
        ordered = jnp.concatenate(
            [both[4 * j + c : 4 * j + c + 1] for c in range(4) for j in range(3)], axis=0
        )
        out[:, l * LANE : (l + 1) * LANE] = ordered


def call(kernel, ins, outs, scratch, cycles, *args, mebibytes=48):
    size = sum(a.size * 4 for a in args) + sum(math.prod(o[0]) * 4 for o in outs)
    spaces = {"v": pltpu.VMEM, "h": pl.ANY}
    places = [pl.BlockSpec(memory_space=spaces[p]) for p in ins]
    result = pl.pallas_call(
        kernel,
        out_shape=[jax.ShapeDtypeStruct(*o) for o in outs],
        in_specs=places[: len(args)],
        out_specs=places[len(args) :],
        scratch_shapes=scratch,
        compiler_params=pltpu.CompilerParams(vmem_limit_bytes=mebibytes * 2**20),
        cost_estimate=pl.CostEstimate(flops=cycles, bytes_accessed=size, transcendentals=0),
    )(*args)
    return result[0] if len(outs) == 1 else result


def on_device(
    slave_disp,
    slave_normal,
    gap_zero,
    quad_weight,
    proj_coord,
    multiplier,
    active,
    pair_owner,
    pair_slot,
    master_vol,
    surf_pick,
):
    region_count = lax.axis_size("region")
    dom_count = lax.axis_size("dom")
    owners = region_count * dom_count
    count = slave_disp.shape[1]
    width = master_vol.shape[1]
    lows = width // LANE
    part = width // dom_count
    step = 4096
    blocks = count // LANE
    exchange = functools.partial(lax.all_to_all, split_axis=0, concat_axis=0, tiled=True)
    owner = pair_owner.reshape(1, count)
    flat = (owners, 8, 128)
    everyone = ("region", "dom")
    whole, quad = (1, count), (4, count)

    table = pltpu.VMEM((24 * lows, LANE), BF)
    picked = call(pick_kernel, "vvv", [((dom_count, 12 * part // 128, 128), F32)], [table], 10**9, master_vol, surf_pick, mebibytes=60)
    surf = exchange(picked, "dom")
    request, place, offset = call(
        functools.partial(request_kernel, 2 * step),
        "hhhvvv",
        [(flat, F32), (whole, jnp.int32), ((8, 2 * owners), jnp.int32)],
        [
            pltpu.VMEM(whole, jnp.int32),
            pltpu.VMEM(whole, jnp.int32),
            pltpu.VMEM((3, count), F32),
            pltpu.VMEM((8 * blocks, LANE), F32),
            pltpu.VMEM((owners, count), BF),
            pltpu.VMEM(whole, F32),
            pltpu.VMEM((2 * blocks + 4, 8, 128), F32),
            pltpu.SMEM((8, 2 * owners), jnp.int32),
            pltpu.SemaphoreType.DMA((4,)),
        ],
        10**10,
        owner,
        pair_slot.reshape(1, count),
        slave_normal,
        mebibytes=56,
    )
    recv = exchange(request, everyone)
    sorted_proj = call(
        sort_kernel,
        "vvv",
        [((2, 4 * blocks, LANE), F32)],
        [pltpu.VMEM((16 * blocks, LANE), F32)],
        10**10,
        place,
        proj_coord,
        mebibytes=56,
    )
    surf, sorted_proj = lax.optimization_barrier((surf, sorted_proj))
    along = call(functools.partial(along_kernel, 64), "vvv", [(flat, F32)], [table], 10**10, surf, recv)
    returned = exchange(along, everyone)
    along, sorted_proj = lax.optimization_barrier((along, sorted_proj))
    slave_part, factors = call(
        local_kernel,
        "v" * 10,
        [(quad, F32), ((5, 4 * blocks, LANE), F32)],
        [pltpu.VMEM((16 * blocks, LANE), F32)],
        10**10,
        place,
        slave_disp,
        slave_normal,
        gap_zero,
        quad_weight,
        multiplier,
        active,
        sorted_proj,
        mebibytes=56,
    )
    terms, mortar = call(
        update_kernel,
        "vhhvv",
        [(flat, F32), ((4 * blocks, LANE), F32)],
        [
            pltpu.SMEM((8, 2 * owners), jnp.int32),
            pltpu.VMEM((5, 4 * blocks, LANE), F32),
            pltpu.VMEM((2 * blocks + 12, 8, 128), F32),
            pltpu.SemaphoreType.DMA((2,)),
        ],
        10**9,
        returned,
        offset,
        factors,
        mebibytes=52,
    )
    factor = exchange(terms, everyone)
    weighted_gap, multiplier_new = call(
        restore_kernel,
        "v" * 7,
        [(quad, F32), (quad, F32)],
        [pltpu.VMEM((PARTS, 8 * blocks // PARTS, LANE), BF)],
        10**10,
        mortar,
        place,
        slave_part,
        multiplier,
        active,
        mebibytes=56,
    )
    recv, weighted_gap = lax.optimization_barrier((recv, weighted_gap))
    forces = call(
        functools.partial(force_kernel, 128),
        "vvv",
        [((dom_count, 12 * part // 128, 128), F32)],
        [pltpu.VMEM((24 * lows, LANE), F32)],
        10**10,
        recv,
        factor,
    )
    moved = exchange(forces, "dom")
    master_force = call(place_kernel, "vvv", [((12, width), F32)], [], 10**9, moved, surf_pick)
    return (weighted_gap, multiplier_new, master_force)


def solution(mesh):
    both = ("region", "dom")
    return jax.shard_map(
        on_device,
        mesh=mesh,
        in_specs=(P(None, both),) * 7 + (P(both, None), P(both), P(None, both), P(both, None)),
        out_specs=(P(None, both),) * 3,
        check_vma=False,
    )
```

```python
import functools
import math

import jax
import jax.numpy as jnp
from jax import lax
from jax.experimental import pallas as pl
from jax.experimental.pallas import tpu as pltpu
from jax.sharding import PartitionSpec as P

gauss_point = 1.0 / math.sqrt(3.0)
node_xs = [-1.0, 1.0, 1.0, -1.0]
node_ys = [-1.0, -1.0, 1.0, 1.0]
point_xs = [-gauss_point, gauss_point, gauss_point, -gauss_point]
point_ys = [-gauss_point, -gauss_point, gauss_point, gauss_point]
slave_table = [
    [(1.0 + node_xs[c] * point_xs[q]) * (1.0 + node_ys[c] * point_ys[q]) * 0.25 for q in range(4)]
    for c in range(4)
]

BF = jnp.bfloat16
F32 = jnp.float32
LANE = 256

UNROLL = 32
PARTS = 2
NN = (((1,), (0,)), ((), ()))
NT = (((1,), (1,)), ((), ()))


def sub_iota(rows, cols):
    return lax.broadcasted_iota(jnp.int32, (rows, cols), 0)


def quotient(value, by):
    return lax.shift_right_logical(value, jnp.int32(by.bit_length() - 1))


def remainder(value, by):
    return lax.bitwise_and(value, jnp.int32(by - 1))


def split(values):
    high = values.astype(BF)
    return high, (values - high.astype(F32)).astype(BF)


def onehot(index, size):
    n = index.shape[1]
    base = (jnp.broadcast_to(index, (16, n)) - sub_iota(16, n)).astype(F32).astype(BF)
    one, zero = jnp.ones((16, n), BF), jnp.zeros((16, n), BF)
    return jnp.concatenate(
        [jnp.where(base == jnp.asarray(16 * g, BF), one, zero) for g in range(size // 16)], axis=0
    )


def grab(table, index, apart):
    half = table.shape[0] // 2
    hot = onehot(index, LANE)
    if apart:
        first = lax.dot_general(table[0:half], hot, NN, preferred_element_type=F32)
        return first + lax.dot_general(table[half:], hot, NN, preferred_element_type=F32)
    found = lax.dot_general(table, hot, NN, preferred_element_type=F32)
    return found[0:half] + found[half:]


def spread(index, values, group, count):
    n = index.shape[1]
    base = (jnp.broadcast_to(index, (16, n)) - sub_iota(16, n) // (16 // group)).astype(F32).astype(BF)
    zero = jnp.zeros((16, n), BF)
    return [
        [jnp.where(base == jnp.asarray(group * g, BF), v, zero) for g in range(count // group)]
        for v in values
    ]


def fill_table(rows, table):
    lows = rows.shape[1] // LANE
    parts = [rows[0:8, l * LANE : (l + 1) * LANE] for l in range(lows)]
    parts += [rows[8:12, l * LANE : (l + 1) * LANE] for l in range(lows)]
    high, low = split(jnp.concatenate(parts, axis=0))
    table[0 : 12 * lows, :] = high
    table[12 * lows :, :] = low


def pick_table(table, index, lows):
    n = index.shape[1]
    grabbed = grab(table, remainder(index, LANE), False)
    low = jnp.broadcast_to(quotient(index, LANE), (8, n))
    pair = low - sub_iota(8, n) // 4
    first = jnp.zeros((8, n), F32)
    for l in range(lows):
        at = 8 * l
        value = grabbed[at : at + 8]
        first = jnp.where(low == l, value, first)
    second = jnp.zeros((8, n), F32)
    for l in range(lows // 2):
        at = 8 * lows + 8 * l
        value = grabbed[at : at + 8]
        second = jnp.where(pair == 2 * l, value, second)
    return first, second[0:4] + second[4:8]


def add_table(first, second, index, lows):
    high, low = split(first)
    group = jnp.concatenate([high.astype(F32), low.astype(F32)], axis=0).astype(BF)
    wide = spread(quotient(index, LANE), [group], 1, lows)[0]
    high, low = split(second)
    high, low = high.astype(F32), low.astype(F32)
    group = jnp.concatenate([high, low, high, low], axis=0).astype(BF)
    narrow = spread(quotient(index, LANE), [group], 2, lows)[0]
    stacked = jnp.concatenate(wide + narrow, axis=0)
    return lax.dot_general(
        stacked, onehot(remainder(index, LANE), LANE), NT, preferred_element_type=F32
    )


def table_part(total, lows, l):
    first = total[16 * l : 16 * l + 8] + total[16 * l + 8 : 16 * l + 16]
    at = 16 * lows + 8 * l
    return first, total[at : at + 4] + total[at + 4 : at + 8]


def store_tile(out, k, t, first, second):
    tiles = out.shape[1] // 12
    out[k, 8 * t : 8 * t + 8, :] = first
    out[k, 8 * tiles + 4 * t : 8 * tiles + 4 * t + 4, :] = second


def load_tiles(source):
    tiles = source.shape[1] // 12
    rows = []
    for k in range(source.shape[0]):
        for t in range(tiles):
            low = source[k, 8 * tiles + 4 * t : 8 * tiles + 4 * t + 4, :]
            rows.append(jnp.concatenate([source[k, 8 * t : 8 * t + 8, :], low], axis=0))
    return jnp.concatenate(rows, axis=1)


def pick_kernel(vol, pick, out, table):
    width = vol.shape[1]
    lows = width // LANE
    rows = vol[...]
    fill_table(
        jnp.concatenate([rows[3 * c + j : 3 * c + j + 1] for j in range(3) for c in range(4)], axis=0),
        table,
    )
    count, tiles, _ = out.shape
    part = width // count
    for k in range(count):
        first, second = pick_table(table[...], pick[:, k * part : (k + 1) * part], lows)
        for t in range(tiles // 12):
            store_tile(out, k, t, first[:, t * 128 : (t + 1) * 128], second[:, t * 128 : (t + 1) * 128])


def lane_iota(rows, cols):
    return lax.broadcasted_iota(jnp.int32, (rows, cols), 1)


def sort_terms(values, place, lows):
    pieces = []
    for value in values:
        pieces += split(jnp.concatenate([value] * 4, axis=0))
    stacked = jnp.concatenate(sum(spread(quotient(place, LANE), pieces, 4, lows), []), axis=0)
    return lax.dot_general(stacked, onehot(remainder(place, LANE), LANE), NT, preferred_element_type=F32)


def sort_parts(values, place, total):
    per = place.shape[1] // PARTS
    each = total.shape[0] // PARTS

    def body(p, _):
        lanes = pl.ds(pl.multiple_of(p * per, per), per)
        rows = pl.ds(pl.multiple_of(p * each, each), each)
        total[rows, :] = sort_terms(values(lanes), remainder(place[:, lanes], per), per // LANE)
        return 0

    lax.fori_loop(0, PARTS, body, 0)


def sorted_sums(total, lows):
    rows, each = 4 * lows, total.shape[0] // PARTS
    sums = []
    for i in range(0, each, 2 * rows):
        parts = []
        for at in range(i, total.shape[0], each):
            parts.append(total[at : at + rows] + total[at + rows : at + 2 * rows])
        sums.append(jnp.concatenate(parts, axis=0))
    return sums


def cut_windows(sums, offsets, ordered, out, masked):
    top = sub_iota(8, 128) < 4
    groups = sums.shape[0] // 8
    left = [sums[8 * g : 8 * g + 8, 0:128] for g in range(groups)]
    right = [sums[8 * g : 8 * g + 8, 128:256] for g in range(groups)]
    turned_left = [pltpu.roll(v, 4, 0) for v in left] + [jnp.zeros((8, 128), F32)]
    turned_right = [pltpu.roll(v, 4, 0) for v in right]
    for g in range(groups):
        ordered[4 * g] = jnp.where(top, left[g], turned_right[g])
        ordered[4 * g + 1] = jnp.where(top, right[g], left[g])
        ordered[4 * g + 2] = jnp.where(top, turned_left[g], right[g])
        ordered[4 * g + 3] = jnp.where(top, turned_right[g], turned_left[g + 1])
    for g in range(4 * groups, ordered.shape[0]):
        ordered[g] = jnp.zeros((8, 128), F32)
    lane = lane_iota(8, 128)
    number = lane + jnp.where(top, 0, 128)

    def cut(start):
        block, shift = quotient(start, 128), remainder(start, 128)
        joined = jnp.where(lane >= shift, ordered[block], ordered[block + 1])
        return pltpu.roll(joined, remainder(128 - shift, 128), 1)

    def window(i, _):
        for u in range(UNROLL):
            o = i * UNROLL + u
            later = offsets[1, o + 1]
            back = cut(later - 256)
            if masked:
                back = jnp.where(number >= 256 + offsets[1, o] - later, back, 0.0)
            start = offsets[0, o]
            out[o] = jnp.where(number < offsets[0, o + 1] - start, cut(start), back)
        return 0

    lax.fori_loop(0, out.shape[0] // UNROLL, window, 0)


def merge_windows(windows, offsets, merged, lows):
    lane = lane_iota(8, 128)
    top = sub_iota(8, 128) < 4
    owners = windows.shape[0]
    per = 2 * lows // PARTS
    gap = 8

    def shifted(o, shift):
        value = pltpu.roll(windows[o], shift, 1)
        other = pltpu.roll(value, 4, 0)
        return jnp.where(top, value, other), jnp.where(top, other, value)

    def window(i, carry):
        front, back = carry
        for u in range(UNROLL):
            o = i * UNROLL + u
            start, later = offsets[0, o], offsets[0, o + 1]
            block, shift = quotient(start, 128), remainder(start, 128)
            one, two = shifted(o, shift)
            first = jnp.where(lane >= shift, one, front)
            second = jnp.where(lane >= shift, two, one)
            merged[block] = first
            merged[block + 1] = second
            merged[block + 2] = two
            ahead = quotient(later, 128) - block
            front = jnp.where(ahead == 0, first, jnp.where(ahead == 1, second, two))
            o = owners - 1 - o
            start, later = offsets[1, o], offsets[1, o + 1]
            block, shift = quotient(later, 128) + gap, remainder(later, 128)
            one, two = shifted(o, shift)
            second = jnp.where(lane >= shift, two, one)
            third = jnp.where(lane >= shift, back, two)
            merged[block - 2] = one
            merged[block - 1] = second
            merged[block] = third
            behind = block - gap - quotient(start, 128)
            back = jnp.where(behind == 0, third, jnp.where(behind == 1, second, one))
        return front, back

    zero = jnp.zeros((8, 128), F32)
    lax.fori_loop(0, owners // UNROLL, window, (zero, zero))
    left, right = [], []
    for g in range(lows // 2):
        at = 4 * g if 4 * g < per else 4 * g + gap
        left.append(jnp.where(top, merged[at], merged[at + 2]))
        right.append(jnp.where(top, merged[at + 1], merged[at + 3]))
    return jnp.concatenate([jnp.concatenate(left, axis=0), jnp.concatenate(right, axis=0)], axis=1)


def request_kernel(step, owner, slot, normal, out, place, offset, total, named, before, ordered, scalars, sem):
    count = owner.shape[1]
    owners = out.shape[0]
    lows = count // PARTS // LANE
    groups = owners // 16

    def lookup(names, columns):
        found = names[0:16] * columns[0:16]
        for g in range(1, groups):
            found = found + names[16 * g : 16 * g + 16] * columns[16 * g : 16 * g + 16]
        return jnp.sum(found.astype(F32), axis=0, keepdims=True)

    def tally(i, sums):
        for u in range(step // 256):
            lanes = pl.ds(pl.multiple_of(i * step + u * 256, 256), 256)
            names = onehot(owner[:, lanes], owners)
            named[:, lanes] = names
            before[:, lanes] = lookup(names, sums)
            sums = sums + names
        return sums

    lower = (sub_iota(owners, owners) > lane_iota(owners, owners)).astype(F32).astype(BF)
    upper = (sub_iota(256, 256) < lane_iota(256, 256)).astype(F32).astype(BF)
    wide = (sub_iota(owners, 2 * owners) < lane_iota(owners, 2 * owners)).astype(F32).astype(BF)
    per = count // PARTS
    bases, starts = [], []
    for p in range(PARTS):
        sums = lax.fori_loop(p * per // step, (p + 1) * per // step, tally, jnp.zeros((owners, 256), BF))
        counts = lax.dot_general(sums, jnp.ones((256, 256), BF), NN, preferred_element_type=F32).astype(BF)
        base = lax.dot_general(lower, counts, NN, preferred_element_type=F32)
        bases.append(split(base + lax.dot_general(sums, upper, NN, preferred_element_type=F32)))
        counts = lax.dot_general(jnp.ones((16, 256), BF), sums, NT, preferred_element_type=F32).astype(BF)
        starts.append(lax.dot_general(counts, wide, NN, preferred_element_type=F32)[0:8] + 1.0 * p * per)
    offset[...] = jnp.where(sub_iota(8, 2 * owners) == 0, starts[0], starts[1]).astype(jnp.int32)
    save = pltpu.make_async_copy(offset, scalars, sem)
    save.start()

    for p in range(PARTS):

        def ranks(i, _):
            for u in range(step // 256):
                lanes = pl.ds(pl.multiple_of(i * step + u * 256, 256), 256)
                names = named[:, lanes]
                found = before[:, lanes] + lookup(names, bases[p][0]) + lookup(names, bases[p][1])
                place[:, lanes] = (found + 1.0 * p * per).astype(jnp.int32)
            return 0

        lax.fori_loop(p * per // step, (p + 1) * per // step, ranks, 0)

    sort_parts(lambda lanes: [jnp.concatenate([slot[:, lanes].astype(F32), normal[:, lanes]], axis=0)], place, total)
    save.wait()
    cut_windows(sorted_sums(total, lows)[0], scalars, ordered, out, True)


def along_kernel(group, surf, recv, out, table):
    lows = table.shape[0] // 24
    fill_table(load_tiles(surf), table)

    def step(i, _):
        parts = [recv[i * group + u] for u in range(group)]
        block = jnp.concatenate([p[4 * h : 4 * h + 4] for p in parts for h in range(2)], axis=1)
        index = block[0:1].astype(jnp.int32)
        first, second = pick_table(table[...], index, lows)
        along = first[0:4] * block[1:2] + first[4:8] * block[2:3] + second * block[3:4]
        for u in range(group):
            for h in range(2):
                at = (2 * u + h) * 128
                out[i * group + u, 4 * h : 4 * h + 4, :] = along[:, at : at + 128]
        return 0

    lax.fori_loop(0, recv.shape[0] // group, step, 0)


def by_node(values, number):
    result = jnp.full(number.shape, values[3], F32)
    for c in range(3):
        result = jnp.where(number == c, values[c], result)
    return result


def turned(values, by):
    if by % 4 == 0:
        return values
    by = by % 4
    row = lax.broadcasted_iota(jnp.int32, values.shape, 1) % 4
    return jnp.where(row < 4 - by, pltpu.roll(values, 8 - by, 1), pltpu.roll(values, 4 - by, 1))


def sort_kernel(place, proj, out, total):
    def values(lanes):
        p = proj[:, lanes]
        return [jnp.concatenate([p[2 * q + k : 2 * q + k + 1] for q in range(4)], axis=0) for k in range(2)]

    sort_parts(values, place, total)
    for k, value in enumerate(sorted_sums(total, place.shape[1] // PARTS // LANE)):
        out[k] = value


def local_kernel(place, disp, normal, gap, weight, multiplier, active, proj, part, factors, total):
    sub4 = sub_iota(4, 1)

    def values(lanes):
        w, d, n, g = weight[:, lanes], disp[:, lanes], normal[:, lanes], gap[:, lanes]
        points = g
        for b in range(4):
            along = n[0:1] * d[3 * b : 3 * b + 1] + n[1:2] * d[3 * b + 1 : 3 * b + 2] + n[2:3] * d[3 * b + 2 : 3 * b + 3]
            points = points + by_node(slave_table[b], sub4) * along
        points = w * points
        result = by_node([slave_table[a][0] for a in range(4)], sub4) * points[0:1]
        for q in range(1, 4):
            result = result + by_node([slave_table[a][q] for a in range(4)], sub4) * points[q : q + 1]
        part[:, lanes] = result
        start = jnp.where(active[:, lanes] == 1, multiplier[:, lanes] - result, -1e30)
        return [w, start]

    sort_parts(values, place, total)
    w, start = sorted_sums(total, place.shape[1] // PARTS // LANE)
    factors[4] = start
    first, second, w = [v.reshape(-1, 8, LANE) for v in (proj[0], proj[1], w)]
    row = lax.broadcasted_iota(jnp.int32, (1, 8, 1), 1) % 4
    sums = [None] * 4
    for e in range(4):
        x, y = turned(first, e), turned(second, e)
        scaled = turned(w, e) * by_node([slave_table[a][(a + e) % 4] * 0.25 for a in range(4)], row)
        for d in range(4):
            node = (row + d) % 4
            term = (1.0 + by_node(node_xs, node) * x) * (1.0 + by_node(node_ys, node) * y) * scaled
            sums[d] = term if e == 0 else sums[d] + term
    for d in range(4):
        factors[d] = sums[d].reshape(-1, LANE)


def update_kernel(recv, offsets_hbm, factors_hbm, out, mortar_out, offsets, factors, ordered, sems):
    copies = [
        pltpu.make_async_copy(a, b, sems.at[i])
        for i, (a, b) in enumerate(((offsets_hbm, offsets), (factors_hbm, factors)))
    ]
    for copy in copies:
        copy.start()
    copies[0].wait()
    lows = factors.shape[1] // 4
    along = merge_windows(recv, offsets, ordered, lows).reshape(-1, 8, LANE)
    copies[1].wait()
    parts = [factors[d].reshape(-1, 8, LANE) for d in range(4)]
    mortar = parts[0] * along
    for d in range(1, 4):
        mortar = mortar + parts[d] * turned(along, d)
    mortar_out[...] = mortar.reshape(-1, LANE)
    lagrange = jnp.maximum(factors[4].reshape(-1, 8, LANE) + mortar, 0.0)
    terms = parts[0] * lagrange
    for d in range(1, 4):
        terms = terms + turned(parts[d] * lagrange, 4 - d)
    cut_windows(terms.reshape(-1, LANE), offsets, ordered, out, False)


def restore_kernel(mortar, place, part, multiplier, active, gap_out, new_out, table):
    per = place.shape[1] // PARTS
    lows = per // LANE
    rows = 4 * lows
    for p in range(PARTS):
        high, low = split(mortar[p * rows : (p + 1) * rows])
        table[p, 0:rows, :] = high
        table[p, rows:, :] = low

    def body(p, _):
        lanes = pl.ds(pl.multiple_of(p * per, per), per)
        places = remainder(place[:, lanes], per)
        grabbed = grab(table[p], remainder(places, LANE), True)
        base = jnp.broadcast_to(quotient(places, LANE), (8, per)) - sub_iota(8, per) // 4
        found = jnp.zeros((8, per), F32)
        for g in range(lows // 2):
            found = jnp.where(base == 2 * g, grabbed[8 * g : 8 * g + 8], found)
        weighted = part[:, lanes] - (found[0:4] + found[4:8])
        gap_out[:, lanes] = weighted
        new_out[:, lanes] = jnp.where(active[:, lanes] == 1, jnp.maximum(multiplier[:, lanes] - weighted, 0.0), 0.0)
        return 0

    lax.fori_loop(0, PARTS, body, 0)


def force_kernel(group, recv, factor, out, total):
    lows = total.shape[0] // 24
    total[...] = jnp.zeros_like(total)

    def step(i, _):
        parts = [recv[i * group + u] for u in range(group)]
        block = jnp.concatenate([p[4 * h : 4 * h + 4] for p in parts for h in range(2)], axis=1)
        parts = [factor[i * group + u] for u in range(group)]
        node = jnp.concatenate([p[4 * h : 4 * h + 4] for p in parts for h in range(2)], axis=1)
        index = block[0:1].astype(jnp.int32)
        first = jnp.concatenate([node * block[1:2], node * block[2:3]], axis=0)
        total[...] += add_table(first, node * block[3:4], index, lows)
        return 0

    lax.fori_loop(0, recv.shape[0] // group, step, 0)
    sums = total[...]
    per = lows // out.shape[0]
    for l in range(lows):
        first, second = table_part(sums, lows, l)
        for t in range(LANE // 128):
            lanes = slice(t * 128, (t + 1) * 128)
            store_tile(out, l // per, l % per * (LANE // 128) + t, first[:, lanes], second[:, lanes])


def place_kernel(moved, pick, out):
    lows = out.shape[1] // LANE
    rows = load_tiles(moved)
    sums = add_table(rows[0:8], rows[8:12], pick[...], lows)
    for l in range(lows):
        first, second = table_part(sums, lows, l)
        both = jnp.concatenate([first, second], axis=0)
        ordered = jnp.concatenate(
            [both[4 * j + c : 4 * j + c + 1] for c in range(4) for j in range(3)], axis=0
        )
        out[:, l * LANE : (l + 1) * LANE] = ordered


def call(kernel, ins, outs, scratch, cycles, *args, mebibytes=48):
    size = sum(a.size * 4 for a in args) + sum(math.prod(o[0]) * 4 for o in outs)
    spaces = {"v": pltpu.VMEM, "h": pl.ANY}
    places = [pl.BlockSpec(memory_space=spaces[p]) for p in ins]
    result = pl.pallas_call(
        kernel,
        out_shape=[jax.ShapeDtypeStruct(*o) for o in outs],
        in_specs=places[: len(args)],
        out_specs=places[len(args) :],
        scratch_shapes=scratch,
        compiler_params=pltpu.CompilerParams(vmem_limit_bytes=mebibytes * 2**20),
        cost_estimate=pl.CostEstimate(flops=cycles, bytes_accessed=size, transcendentals=0),
    )(*args)
    return result[0] if len(outs) == 1 else result


def on_device(
    slave_disp,
    slave_normal,
    gap_zero,
    quad_weight,
    proj_coord,
    multiplier,
    active,
    pair_owner,
    pair_slot,
    master_vol,
    surf_pick,
):
    region_count = lax.axis_size("region")
    dom_count = lax.axis_size("dom")
    owners = region_count * dom_count
    count = slave_disp.shape[1]
    width = master_vol.shape[1]
    lows = width // LANE
    part = width // dom_count
    step = 4096
    blocks = count // LANE
    exchange = functools.partial(lax.all_to_all, split_axis=0, concat_axis=0, tiled=True)
    owner = pair_owner.reshape(1, count)
    flat = (owners, 8, 128)
    everyone = ("region", "dom")
    whole, quad = (1, count), (4, count)

    table = pltpu.VMEM((24 * lows, LANE), BF)
    picked = call(pick_kernel, "vvv", [((dom_count, 12 * part // 128, 128), F32)], [table], 10**9, master_vol, surf_pick, mebibytes=60)
    surf = exchange(picked, "dom")
    request, place, offset = call(
        functools.partial(request_kernel, 2 * step),
        "vvvvvv",
        [(flat, F32), (whole, jnp.int32), ((8, 2 * owners), jnp.int32)],
        [
            pltpu.VMEM((8 * blocks, LANE), F32),
            pltpu.VMEM((owners, count), BF),
            pltpu.VMEM(whole, F32),
            pltpu.VMEM((2 * blocks + 4, 8, 128), F32),
            pltpu.SMEM((8, 2 * owners), jnp.int32),
            pltpu.SemaphoreType.DMA,
        ],
        10**10,
        owner,
        pair_slot.reshape(1, count),
        slave_normal,
    )
    recv = exchange(request, everyone)
    sorted_proj = call(
        sort_kernel,
        "vvv",
        [((2, 4 * blocks, LANE), F32)],
        [pltpu.VMEM((16 * blocks, LANE), F32)],
        10**10,
        place,
        proj_coord,
        mebibytes=56,
    )
    surf, sorted_proj = lax.optimization_barrier((surf, sorted_proj))
    along = call(functools.partial(along_kernel, 64), "vvv", [(flat, F32)], [table], 10**10, surf, recv)
    returned = exchange(along, everyone)
    along, sorted_proj = lax.optimization_barrier((along, sorted_proj))
    slave_part, factors = call(
        local_kernel,
        "v" * 10,
        [(quad, F32), ((5, 4 * blocks, LANE), F32)],
        [pltpu.VMEM((16 * blocks, LANE), F32)],
        10**10,
        place,
        slave_disp,
        slave_normal,
        gap_zero,
        quad_weight,
        multiplier,
        active,
        sorted_proj,
        mebibytes=56,
    )
    terms, mortar = call(
        update_kernel,
        "vhhvv",
        [(flat, F32), ((4 * blocks, LANE), F32)],
        [
            pltpu.SMEM((8, 2 * owners), jnp.int32),
            pltpu.VMEM((5, 4 * blocks, LANE), F32),
            pltpu.VMEM((2 * blocks + 12, 8, 128), F32),
            pltpu.SemaphoreType.DMA((2,)),
        ],
        10**9,
        returned,
        offset,
        factors,
        mebibytes=52,
    )
    factor = exchange(terms, everyone)
    weighted_gap, multiplier_new = call(
        restore_kernel,
        "v" * 7,
        [(quad, F32), (quad, F32)],
        [pltpu.VMEM((PARTS, 8 * blocks // PARTS, LANE), BF)],
        10**10,
        mortar,
        place,
        slave_part,
        multiplier,
        active,
        mebibytes=48,
    )
    recv, weighted_gap = lax.optimization_barrier((recv, weighted_gap))
    forces = call(
        functools.partial(force_kernel, 128),
        "vvv",
        [((dom_count, 12 * part // 128, 128), F32)],
        [pltpu.VMEM((24 * lows, LANE), F32)],
        10**10,
        recv,
        factor,
    )
    moved = exchange(forces, "dom")
    master_force = call(place_kernel, "vvv", [((12, width), F32)], [], 10**9, moved, surf_pick)
    return (weighted_gap, multiplier_new, master_force)


def solution(mesh):
    both = ("region", "dom")
    return jax.shard_map(
        on_device,
        mesh=mesh,
        in_specs=(P(None, both),) * 7 + (P(both, None), P(both), P(None, both), P(both, None)),
        out_specs=(P(None, both),) * 3,
        check_vma=False,
    )
```

```python
import functools
import math

import jax
import jax.numpy as jnp
from jax import lax
from jax.experimental import pallas as pl
from jax.experimental.pallas import tpu as pltpu
from jax.sharding import PartitionSpec as P

gauss_point = 1.0 / math.sqrt(3.0)
node_xs = [-1.0, 1.0, 1.0, -1.0]
node_ys = [-1.0, -1.0, 1.0, 1.0]
point_xs = [-gauss_point, gauss_point, gauss_point, -gauss_point]
point_ys = [-gauss_point, -gauss_point, gauss_point, gauss_point]
slave_table = [
    [(1.0 + node_xs[c] * point_xs[q]) * (1.0 + node_ys[c] * point_ys[q]) * 0.25 for q in range(4)]
    for c in range(4)
]

BF = jnp.bfloat16
F32 = jnp.float32
LANE = 256

UNROLL = 64
PARTS = 2
NN = (((1,), (0,)), ((), ()))
NT = (((1,), (1,)), ((), ()))


def sub_iota(rows, cols):
    return lax.broadcasted_iota(jnp.int32, (rows, cols), 0)


def quotient(value, by):
    return lax.shift_right_logical(value, jnp.int32(by.bit_length() - 1))


def remainder(value, by):
    return lax.bitwise_and(value, jnp.int32(by - 1))


def split(values):
    high = values.astype(BF)
    return high, (values - high.astype(F32)).astype(BF)


def onehot(index, size):
    n = index.shape[1]
    base = (jnp.broadcast_to(index, (16, n)) - sub_iota(16, n)).astype(F32).astype(BF)
    one, zero = jnp.ones((16, n), BF), jnp.zeros((16, n), BF)
    return jnp.concatenate(
        [jnp.where(base == jnp.asarray(16 * g, BF), one, zero) for g in range(size // 16)], axis=0
    )


def grab(table, index, apart):
    half = table.shape[0] // 2
    hot = onehot(index, LANE)
    if apart:
        first = lax.dot_general(table[0:half], hot, NN, preferred_element_type=F32)
        return first + lax.dot_general(table[half:], hot, NN, preferred_element_type=F32)
    found = lax.dot_general(table, hot, NN, preferred_element_type=F32)
    return found[0:half] + found[half:]


def spread(index, values, group, count):
    n = index.shape[1]
    base = (jnp.broadcast_to(index, (16, n)) - sub_iota(16, n) // (16 // group)).astype(F32).astype(BF)
    zero = jnp.zeros((16, n), BF)
    return [
        [jnp.where(base == jnp.asarray(group * g, BF), v, zero) for g in range(count // group)]
        for v in values
    ]


def fill_table(rows, table):
    lows = rows.shape[1] // LANE
    parts = [rows[0:8, l * LANE : (l + 1) * LANE] for l in range(lows)]
    parts += [rows[8:12, l * LANE : (l + 1) * LANE] for l in range(lows)]
    high, low = split(jnp.concatenate(parts, axis=0))
    table[0 : 12 * lows, :] = high
    table[12 * lows :, :] = low


def pick_table(table, index, lows):
    n = index.shape[1]
    grabbed = grab(table, remainder(index, LANE), False)
    low = jnp.broadcast_to(quotient(index, LANE), (8, n))
    pair = low - sub_iota(8, n) // 4
    first = jnp.zeros((8, n), F32)
    for l in range(lows):
        at = 8 * l
        value = grabbed[at : at + 8]
        first = jnp.where(low == l, value, first)
    second = jnp.zeros((8, n), F32)
    for l in range(lows // 2):
        at = 8 * lows + 8 * l
        value = grabbed[at : at + 8]
        second = jnp.where(pair == 2 * l, value, second)
    return first, second[0:4] + second[4:8]


def add_table(first, second, index, lows):
    high, low = split(first)
    group = jnp.concatenate([high.astype(F32), low.astype(F32)], axis=0).astype(BF)
    wide = spread(quotient(index, LANE), [group], 1, lows)[0]
    high, low = split(second)
    high, low = high.astype(F32), low.astype(F32)
    group = jnp.concatenate([high, low, high, low], axis=0).astype(BF)
    narrow = spread(quotient(index, LANE), [group], 2, lows)[0]
    stacked = jnp.concatenate(wide + narrow, axis=0)
    return lax.dot_general(
        stacked, onehot(remainder(index, LANE), LANE), NT, preferred_element_type=F32
    )


def table_part(total, lows, l):
    first = total[16 * l : 16 * l + 8] + total[16 * l + 8 : 16 * l + 16]
    at = 16 * lows + 8 * l
    return first, total[at : at + 4] + total[at + 4 : at + 8]


def store_tile(out, k, t, first, second):
    tiles = out.shape[1] // 12
    out[k, 8 * t : 8 * t + 8, :] = first
    out[k, 8 * tiles + 4 * t : 8 * tiles + 4 * t + 4, :] = second


def load_tiles(source):
    tiles = source.shape[1] // 12
    rows = []
    for k in range(source.shape[0]):
        for t in range(tiles):
            low = source[k, 8 * tiles + 4 * t : 8 * tiles + 4 * t + 4, :]
            rows.append(jnp.concatenate([source[k, 8 * t : 8 * t + 8, :], low], axis=0))
    return jnp.concatenate(rows, axis=1)


def pick_kernel(vol, pick, out, table):
    width = vol.shape[1]
    lows = width // LANE
    rows = vol[...]
    fill_table(
        jnp.concatenate([rows[3 * c + j : 3 * c + j + 1] for j in range(3) for c in range(4)], axis=0),
        table,
    )
    count, tiles, _ = out.shape
    part = width // count
    for k in range(count):
        first, second = pick_table(table[...], pick[:, k * part : (k + 1) * part], lows)
        for t in range(tiles // 12):
            store_tile(out, k, t, first[:, t * 128 : (t + 1) * 128], second[:, t * 128 : (t + 1) * 128])


def lane_iota(rows, cols):
    return lax.broadcasted_iota(jnp.int32, (rows, cols), 1)


def sort_terms(values, place, lows):
    pieces = []
    for value in values:
        pieces += split(jnp.concatenate([value] * 4, axis=0))
    stacked = jnp.concatenate(sum(spread(quotient(place, LANE), pieces, 4, lows), []), axis=0)
    return lax.dot_general(stacked, onehot(remainder(place, LANE), LANE), NT, preferred_element_type=F32)


def sort_parts(values, place, total):
    per = place.shape[1] // PARTS
    each = total.shape[0] // PARTS

    def body(p, _):
        lanes = pl.ds(pl.multiple_of(p * per, per), per)
        rows = pl.ds(pl.multiple_of(p * each, each), each)
        total[rows, :] = sort_terms(values(lanes), remainder(place[:, lanes], per), per // LANE)
        return 0

    lax.fori_loop(0, PARTS, body, 0)


def sorted_sums(total, lows):
    rows, each = 4 * lows, total.shape[0] // PARTS
    sums = []
    for i in range(0, each, 2 * rows):
        parts = []
        for at in range(i, total.shape[0], each):
            parts.append(total[at : at + rows] + total[at + rows : at + 2 * rows])
        sums.append(jnp.concatenate(parts, axis=0))
    return sums


def cut_windows(sums, offsets, ordered, out, masked):
    top = sub_iota(8, 128) < 4
    groups = sums.shape[0] // 8
    left = [sums[8 * g : 8 * g + 8, 0:128] for g in range(groups)]
    right = [sums[8 * g : 8 * g + 8, 128:256] for g in range(groups)]
    turned_left = [pltpu.roll(v, 4, 0) for v in left] + [jnp.zeros((8, 128), F32)]
    turned_right = [pltpu.roll(v, 4, 0) for v in right]
    for g in range(groups):
        ordered[4 * g] = jnp.where(top, left[g], turned_right[g])
        ordered[4 * g + 1] = jnp.where(top, right[g], left[g])
        ordered[4 * g + 2] = jnp.where(top, turned_left[g], right[g])
        ordered[4 * g + 3] = jnp.where(top, turned_right[g], turned_left[g + 1])
    for g in range(4 * groups, ordered.shape[0]):
        ordered[g] = jnp.zeros((8, 128), F32)
    lane = lane_iota(8, 128)
    number = lane + jnp.where(top, 0, 128)

    def cut(start):
        block, shift = quotient(start, 128), remainder(start, 128)
        joined = jnp.where(lane >= shift, ordered[block], ordered[block + 1])
        return pltpu.roll(joined, remainder(128 - shift, 128), 1)

    for o in range(out.shape[0]):
        later = offsets[1, o + 1]
        back = cut(later - 256)
        if masked:
            back = jnp.where(number >= 256 + offsets[1, o] - later, back, 0.0)
        start = offsets[0, o]
        out[o] = jnp.where(number < offsets[0, o + 1] - start, cut(start), back)


def merge_windows(windows, offsets, merged, lows):
    lane = lane_iota(8, 128)
    top = sub_iota(8, 128) < 4
    owners = windows.shape[0]
    per = 2 * lows // PARTS
    gap = 8

    def shifted(o, shift):
        value = pltpu.roll(windows[o], shift, 1)
        other = pltpu.roll(value, 4, 0)
        return jnp.where(top, value, other), jnp.where(top, other, value)

    def window(i, carry):
        front, back = carry
        for u in range(UNROLL):
            o = i * UNROLL + u
            start, later = offsets[0, o], offsets[0, o + 1]
            block, shift = quotient(start, 128), remainder(start, 128)
            one, two = shifted(o, shift)
            first = jnp.where(lane >= shift, one, front)
            second = jnp.where(lane >= shift, two, one)
            merged[block] = first
            merged[block + 1] = second
            merged[block + 2] = two
            ahead = quotient(later, 128) - block
            front = jnp.where(ahead == 0, first, jnp.where(ahead == 1, second, two))
            o = owners - 1 - o
            start, later = offsets[1, o], offsets[1, o + 1]
            block, shift = quotient(later, 128) + gap, remainder(later, 128)
            one, two = shifted(o, shift)
            second = jnp.where(lane >= shift, two, one)
            third = jnp.where(lane >= shift, back, two)
            merged[block - 2] = one
            merged[block - 1] = second
            merged[block] = third
            behind = block - gap - quotient(start, 128)
            back = jnp.where(behind == 0, third, jnp.where(behind == 1, second, one))
        return front, back

    zero = jnp.zeros((8, 128), F32)
    lax.fori_loop(0, owners // UNROLL, window, (zero, zero))
    left, right = [], []
    for g in range(lows // 2):
        at = 4 * g if 4 * g < per else 4 * g + gap
        left.append(jnp.where(top, merged[at], merged[at + 2]))
        right.append(jnp.where(top, merged[at + 1], merged[at + 3]))
    return jnp.concatenate([jnp.concatenate(left, axis=0), jnp.concatenate(right, axis=0)], axis=1)


def request_kernel(step, owner, slot, normal, out, place, offset, total, named, before, ordered, scalars, sem):
    count = owner.shape[1]
    owners = out.shape[0]
    lows = count // PARTS // LANE
    groups = owners // 16

    def lookup(names, columns):
        found = names[0:16] * columns[0:16]
        for g in range(1, groups):
            found = found + names[16 * g : 16 * g + 16] * columns[16 * g : 16 * g + 16]
        return jnp.sum(found.astype(F32), axis=0, keepdims=True)

    def tally(i, sums):
        for u in range(step // 256):
            lanes = pl.ds(pl.multiple_of(i * step + u * 256, 256), 256)
            names = onehot(owner[:, lanes], owners)
            named[:, lanes] = names
            before[:, lanes] = lookup(names, sums)
            sums = sums + names
        return sums

    lower = (sub_iota(owners, owners) > lane_iota(owners, owners)).astype(F32).astype(BF)
    upper = (sub_iota(256, 256) < lane_iota(256, 256)).astype(F32).astype(BF)
    wide = (sub_iota(owners, 2 * owners) < lane_iota(owners, 2 * owners)).astype(F32).astype(BF)
    per = count // PARTS
    bases, starts = [], []
    for p in range(PARTS):
        sums = lax.fori_loop(p * per // step, (p + 1) * per // step, tally, jnp.zeros((owners, 256), BF))
        counts = lax.dot_general(sums, jnp.ones((256, 256), BF), NN, preferred_element_type=F32).astype(BF)
        base = lax.dot_general(lower, counts, NN, preferred_element_type=F32)
        bases.append(split(base + lax.dot_general(sums, upper, NN, preferred_element_type=F32)))
        counts = lax.dot_general(jnp.ones((16, 256), BF), sums, NT, preferred_element_type=F32).astype(BF)
        starts.append(lax.dot_general(counts, wide, NN, preferred_element_type=F32)[0:8] + 1.0 * p * per)
    offset[...] = jnp.where(sub_iota(8, 2 * owners) == 0, starts[0], starts[1]).astype(jnp.int32)
    save = pltpu.make_async_copy(offset, scalars, sem)
    save.start()

    for p in range(PARTS):

        def ranks(i, _):
            for u in range(step // 256):
                lanes = pl.ds(pl.multiple_of(i * step + u * 256, 256), 256)
                names = named[:, lanes]
                found = before[:, lanes] + lookup(names, bases[p][0]) + lookup(names, bases[p][1])
                place[:, lanes] = (found + 1.0 * p * per).astype(jnp.int32)
            return 0

        lax.fori_loop(p * per // step, (p + 1) * per // step, ranks, 0)

    sort_parts(lambda lanes: [jnp.concatenate([slot[:, lanes].astype(F32), normal[:, lanes]], axis=0)], place, total)
    save.wait()
    cut_windows(sorted_sums(total, lows)[0], scalars, ordered, out, True)


def along_kernel(group, surf, recv, out, table):
    lows = table.shape[0] // 24
    fill_table(load_tiles(surf), table)

    def step(i, _):
        parts = [recv[i * group + u] for u in range(group)]
        block = jnp.concatenate([p[4 * h : 4 * h + 4] for p in parts for h in range(2)], axis=1)
        index = block[0:1].astype(jnp.int32)
        first, second = pick_table(table[...], index, lows)
        along = first[0:4] * block[1:2] + first[4:8] * block[2:3] + second * block[3:4]
        for u in range(group):
            for h in range(2):
                at = (2 * u + h) * 128
                out[i * group + u, 4 * h : 4 * h + 4, :] = along[:, at : at + 128]
        return 0

    lax.fori_loop(0, recv.shape[0] // group, step, 0)


def by_node(values, number):
    result = jnp.full(number.shape, values[3], F32)
    for c in range(3):
        result = jnp.where(number == c, values[c], result)
    return result


def turned(values, by):
    if by % 4 == 0:
        return values
    by = by % 4
    row = lax.broadcasted_iota(jnp.int32, values.shape, 1) % 4
    return jnp.where(row < 4 - by, pltpu.roll(values, 8 - by, 1), pltpu.roll(values, 4 - by, 1))


def sort_kernel(place, proj, out, total):
    def values(lanes):
        p = proj[:, lanes]
        return [jnp.concatenate([p[2 * q + k : 2 * q + k + 1] for q in range(4)], axis=0) for k in range(2)]

    sort_parts(values, place, total)
    for k, value in enumerate(sorted_sums(total, place.shape[1] // PARTS // LANE)):
        out[k] = value


def local_kernel(place, disp, normal, gap, weight, multiplier, active, proj, part, factors, total):
    sub4 = sub_iota(4, 1)

    def values(lanes):
        w, d, n, g = weight[:, lanes], disp[:, lanes], normal[:, lanes], gap[:, lanes]
        points = g
        for b in range(4):
            along = n[0:1] * d[3 * b : 3 * b + 1] + n[1:2] * d[3 * b + 1 : 3 * b + 2] + n[2:3] * d[3 * b + 2 : 3 * b + 3]
            points = points + by_node(slave_table[b], sub4) * along
        points = w * points
        result = by_node([slave_table[a][0] for a in range(4)], sub4) * points[0:1]
        for q in range(1, 4):
            result = result + by_node([slave_table[a][q] for a in range(4)], sub4) * points[q : q + 1]
        part[:, lanes] = result
        start = jnp.where(active[:, lanes] == 1, multiplier[:, lanes] - result, -1e30)
        return [w, start]

    sort_parts(values, place, total)
    w, start = sorted_sums(total, place.shape[1] // PARTS // LANE)
    factors[4] = start
    first, second, w = [v.reshape(-1, 8, LANE) for v in (proj[0], proj[1], w)]
    row = lax.broadcasted_iota(jnp.int32, (1, 8, 1), 1) % 4
    sums = [None] * 4
    for e in range(4):
        x, y = turned(first, e), turned(second, e)
        scaled = turned(w, e) * by_node([slave_table[a][(a + e) % 4] * 0.25 for a in range(4)], row)
        for d in range(4):
            node = (row + d) % 4
            term = (1.0 + by_node(node_xs, node) * x) * (1.0 + by_node(node_ys, node) * y) * scaled
            sums[d] = term if e == 0 else sums[d] + term
    for d in range(4):
        factors[d] = sums[d].reshape(-1, LANE)


def update_kernel(recv, offsets_hbm, factors_hbm, out, mortar_out, offsets, factors, ordered, sems):
    copies = [
        pltpu.make_async_copy(a, b, sems.at[i])
        for i, (a, b) in enumerate(((offsets_hbm, offsets), (factors_hbm, factors)))
    ]
    for copy in copies:
        copy.start()
    copies[0].wait()
    lows = factors.shape[1] // 4
    along = merge_windows(recv, offsets, ordered, lows).reshape(-1, 8, LANE)
    copies[1].wait()
    parts = [factors[d].reshape(-1, 8, LANE) for d in range(4)]
    mortar = parts[0] * along
    for d in range(1, 4):
        mortar = mortar + parts[d] * turned(along, d)
    mortar_out[...] = mortar.reshape(-1, LANE)
    lagrange = jnp.maximum(factors[4].reshape(-1, 8, LANE) + mortar, 0.0)
    terms = parts[0] * lagrange
    for d in range(1, 4):
        terms = terms + turned(parts[d] * lagrange, 4 - d)
    cut_windows(terms.reshape(-1, LANE), offsets, ordered, out, False)


def restore_kernel(mortar, place, part, multiplier, active, gap_out, new_out, table):
    per = place.shape[1] // PARTS
    lows = per // LANE
    rows = 4 * lows
    for p in range(PARTS):
        high, low = split(mortar[p * rows : (p + 1) * rows])
        table[p, 0:rows, :] = high
        table[p, rows:, :] = low

    def body(p, _):
        lanes = pl.ds(pl.multiple_of(p * per, per), per)
        places = remainder(place[:, lanes], per)
        grabbed = grab(table[p], remainder(places, LANE), True)
        base = jnp.broadcast_to(quotient(places, LANE), (8, per)) - sub_iota(8, per) // 4
        found = jnp.zeros((8, per), F32)
        for g in range(lows // 2):
            found = jnp.where(base == 2 * g, grabbed[8 * g : 8 * g + 8], found)
        weighted = part[:, lanes] - (found[0:4] + found[4:8])
        gap_out[:, lanes] = weighted
        new_out[:, lanes] = jnp.where(active[:, lanes] == 1, jnp.maximum(multiplier[:, lanes] - weighted, 0.0), 0.0)
        return 0

    lax.fori_loop(0, PARTS, body, 0)


def force_kernel(group, recv, factor, out, total):
    lows = total.shape[0] // 24
    total[...] = jnp.zeros_like(total)

    def step(i, _):
        parts = [recv[i * group + u] for u in range(group)]
        block = jnp.concatenate([p[4 * h : 4 * h + 4] for p in parts for h in range(2)], axis=1)
        parts = [factor[i * group + u] for u in range(group)]
        node = jnp.concatenate([p[4 * h : 4 * h + 4] for p in parts for h in range(2)], axis=1)
        index = block[0:1].astype(jnp.int32)
        first = jnp.concatenate([node * block[1:2], node * block[2:3]], axis=0)
        total[...] += add_table(first, node * block[3:4], index, lows)
        return 0

    lax.fori_loop(0, recv.shape[0] // group, step, 0)
    sums = total[...]
    per = lows // out.shape[0]
    for l in range(lows):
        first, second = table_part(sums, lows, l)
        for t in range(LANE // 128):
            lanes = slice(t * 128, (t + 1) * 128)
            store_tile(out, l // per, l % per * (LANE // 128) + t, first[:, lanes], second[:, lanes])


def place_kernel(moved, pick, out):
    lows = out.shape[1] // LANE
    rows = load_tiles(moved)
    sums = add_table(rows[0:8], rows[8:12], pick[...], lows)
    for l in range(lows):
        first, second = table_part(sums, lows, l)
        both = jnp.concatenate([first, second], axis=0)
        ordered = jnp.concatenate(
            [both[4 * j + c : 4 * j + c + 1] for c in range(4) for j in range(3)], axis=0
        )
        out[:, l * LANE : (l + 1) * LANE] = ordered


def call(kernel, ins, outs, scratch, cycles, *args, mebibytes=48):
    size = sum(a.size * 4 for a in args) + sum(math.prod(o[0]) * 4 for o in outs)
    spaces = {"v": pltpu.VMEM, "h": pl.ANY}
    places = [pl.BlockSpec(memory_space=spaces[p]) for p in ins]
    result = pl.pallas_call(
        kernel,
        out_shape=[jax.ShapeDtypeStruct(*o) for o in outs],
        in_specs=places[: len(args)],
        out_specs=places[len(args) :],
        scratch_shapes=scratch,
        compiler_params=pltpu.CompilerParams(vmem_limit_bytes=mebibytes * 2**20),
        cost_estimate=pl.CostEstimate(flops=cycles, bytes_accessed=size, transcendentals=0),
    )(*args)
    return result[0] if len(outs) == 1 else result


def on_device(
    slave_disp,
    slave_normal,
    gap_zero,
    quad_weight,
    proj_coord,
    multiplier,
    active,
    pair_owner,
    pair_slot,
    master_vol,
    surf_pick,
):
    region_count = lax.axis_size("region")
    dom_count = lax.axis_size("dom")
    owners = region_count * dom_count
    count = slave_disp.shape[1]
    width = master_vol.shape[1]
    lows = width // LANE
    part = width // dom_count
    step = 4096
    blocks = count // LANE
    exchange = functools.partial(lax.all_to_all, split_axis=0, concat_axis=0, tiled=True)
    owner = pair_owner.reshape(1, count)
    flat = (owners, 8, 128)
    everyone = ("region", "dom")
    whole, quad = (1, count), (4, count)

    table = pltpu.VMEM((24 * lows, LANE), BF)
    picked = call(pick_kernel, "vvv", [((dom_count, 12 * part // 128, 128), F32)], [table], 10**9, master_vol, surf_pick, mebibytes=60)
    surf = exchange(picked, "dom")
    request, place, offset = call(
        functools.partial(request_kernel, 2 * step),
        "vvvvvv",
        [(flat, F32), (whole, jnp.int32), ((8, 2 * owners), jnp.int32)],
        [
            pltpu.VMEM((8 * blocks, LANE), F32),
            pltpu.VMEM((owners, count), BF),
            pltpu.VMEM(whole, F32),
            pltpu.VMEM((2 * blocks + 4, 8, 128), F32),
            pltpu.SMEM((8, 2 * owners), jnp.int32),
            pltpu.SemaphoreType.DMA,
        ],
        10**10,
        owner,
        pair_slot.reshape(1, count),
        slave_normal,
    )
    recv = exchange(request, everyone)
    sorted_proj = call(
        sort_kernel,
        "vvv",
        [((2, 4 * blocks, LANE), F32)],
        [pltpu.VMEM((16 * blocks, LANE), F32)],
        10**10,
        place,
        proj_coord,
        mebibytes=56,
    )
    surf, sorted_proj = lax.optimization_barrier((surf, sorted_proj))
    along = call(functools.partial(along_kernel, 64), "vvv", [(flat, F32)], [table], 10**10, surf, recv)
    returned = exchange(along, everyone)
    along, sorted_proj = lax.optimization_barrier((along, sorted_proj))
    slave_part, factors = call(
        local_kernel,
        "v" * 10,
        [(quad, F32), ((5, 4 * blocks, LANE), F32)],
        [pltpu.VMEM((16 * blocks, LANE), F32)],
        10**10,
        place,
        slave_disp,
        slave_normal,
        gap_zero,
        quad_weight,
        multiplier,
        active,
        sorted_proj,
        mebibytes=56,
    )
    terms, mortar = call(
        update_kernel,
        "vhhvv",
        [(flat, F32), ((4 * blocks, LANE), F32)],
        [
            pltpu.SMEM((8, 2 * owners), jnp.int32),
            pltpu.VMEM((5, 4 * blocks, LANE), F32),
            pltpu.VMEM((2 * blocks + 12, 8, 128), F32),
            pltpu.SemaphoreType.DMA((2,)),
        ],
        10**9,
        returned,
        offset,
        factors,
        mebibytes=52,
    )
    factor = exchange(terms, everyone)
    weighted_gap, multiplier_new = call(
        restore_kernel,
        "v" * 7,
        [(quad, F32), (quad, F32)],
        [pltpu.VMEM((PARTS, 8 * blocks // PARTS, LANE), BF)],
        10**10,
        mortar,
        place,
        slave_part,
        multiplier,
        active,
        mebibytes=48,
    )
    recv, weighted_gap = lax.optimization_barrier((recv, weighted_gap))
    forces = call(
        functools.partial(force_kernel, 128),
        "vvv",
        [((dom_count, 12 * part // 128, 128), F32)],
        [pltpu.VMEM((24 * lows, LANE), F32)],
        10**10,
        recv,
        factor,
    )
    moved = exchange(forces, "dom")
    master_force = call(place_kernel, "vvv", [((12, width), F32)], [], 10**9, moved, surf_pick)
    return (weighted_gap, multiplier_new, master_force)


def solution(mesh):
    both = ("region", "dom")
    return jax.shard_map(
        on_device,
        mesh=mesh,
        in_specs=(P(None, both),) * 7 + (P(both, None), P(both), P(None, both), P(both, None)),
        out_specs=(P(None, both),) * 3,
        check_vma=False,
    )
```

```python
import functools
import math

import jax
import jax.numpy as jnp
from jax import lax
from jax.experimental import pallas as pl
from jax.experimental.pallas import tpu as pltpu
from jax.sharding import PartitionSpec as P

gauss_point = 1.0 / math.sqrt(3.0)
node_xs = [-1.0, 1.0, 1.0, -1.0]
node_ys = [-1.0, -1.0, 1.0, 1.0]
point_xs = [-gauss_point, gauss_point, gauss_point, -gauss_point]
point_ys = [-gauss_point, -gauss_point, gauss_point, gauss_point]
slave_table = [
    [(1.0 + node_xs[c] * point_xs[q]) * (1.0 + node_ys[c] * point_ys[q]) * 0.25 for q in range(4)]
    for c in range(4)
]

BF = jnp.bfloat16
F32 = jnp.float32
LANE = 256

UNROLL = 64
PARTS = 2
NN = (((1,), (0,)), ((), ()))
NT = (((1,), (1,)), ((), ()))


def sub_iota(rows, cols):
    return lax.broadcasted_iota(jnp.int32, (rows, cols), 0)


def quotient(value, by):
    return lax.shift_right_logical(value, jnp.int32(by.bit_length() - 1))


def remainder(value, by):
    return lax.bitwise_and(value, jnp.int32(by - 1))


def split(values):
    high = values.astype(BF)
    return high, (values - high.astype(F32)).astype(BF)


def onehot(index, size):
    n = index.shape[1]
    base = (jnp.broadcast_to(index, (16, n)) - sub_iota(16, n)).astype(F32).astype(BF)
    one, zero = jnp.ones((16, n), BF), jnp.zeros((16, n), BF)
    return jnp.concatenate(
        [jnp.where(base == jnp.asarray(16 * g, BF), one, zero) for g in range(size // 16)], axis=0
    )


def grab(table, index, apart):
    half = table.shape[0] // 2
    hot = onehot(index, LANE)
    if apart:
        first = lax.dot_general(table[0:half], hot, NN, preferred_element_type=F32)
        return first + lax.dot_general(table[half:], hot, NN, preferred_element_type=F32)
    found = lax.dot_general(table, hot, NN, preferred_element_type=F32)
    return found[0:half] + found[half:]


def spread(index, values, group, count):
    n = index.shape[1]
    base = (jnp.broadcast_to(index, (16, n)) - sub_iota(16, n) // (16 // group)).astype(F32).astype(BF)
    zero = jnp.zeros((16, n), BF)
    return [
        [jnp.where(base == jnp.asarray(group * g, BF), v, zero) for g in range(count // group)]
        for v in values
    ]


def fill_table(rows, table):
    lows = rows.shape[1] // LANE
    parts = [rows[0:8, l * LANE : (l + 1) * LANE] for l in range(lows)]
    parts += [rows[8:12, l * LANE : (l + 1) * LANE] for l in range(lows)]
    high, low = split(jnp.concatenate(parts, axis=0))
    table[0 : 12 * lows, :] = high
    table[12 * lows :, :] = low


def pick_table(table, index, lows):
    n = index.shape[1]
    grabbed = grab(table, remainder(index, LANE), False)
    low = jnp.broadcast_to(quotient(index, LANE), (8, n))
    pair = low - sub_iota(8, n) // 4
    first = jnp.zeros((8, n), F32)
    for l in range(lows):
        at = 8 * l
        value = grabbed[at : at + 8]
        first = jnp.where(low == l, value, first)
    second = jnp.zeros((8, n), F32)
    for l in range(lows // 2):
        at = 8 * lows + 8 * l
        value = grabbed[at : at + 8]
        second = jnp.where(pair == 2 * l, value, second)
    return first, second[0:4] + second[4:8]


def add_table(first, second, index, lows):
    high, low = split(first)
    group = jnp.concatenate([high.astype(F32), low.astype(F32)], axis=0).astype(BF)
    wide = spread(quotient(index, LANE), [group], 1, lows)[0]
    high, low = split(second)
    high, low = high.astype(F32), low.astype(F32)
    group = jnp.concatenate([high, low, high, low], axis=0).astype(BF)
    narrow = spread(quotient(index, LANE), [group], 2, lows)[0]
    stacked = jnp.concatenate(wide + narrow, axis=0)
    return lax.dot_general(
        stacked, onehot(remainder(index, LANE), LANE), NT, preferred_element_type=F32
    )


def table_part(total, lows, l):
    first = total[16 * l : 16 * l + 8] + total[16 * l + 8 : 16 * l + 16]
    at = 16 * lows + 8 * l
    return first, total[at : at + 4] + total[at + 4 : at + 8]


def store_tile(out, k, t, first, second):
    tiles = out.shape[1] // 12
    out[k, 8 * t : 8 * t + 8, :] = first
    out[k, 8 * tiles + 4 * t : 8 * tiles + 4 * t + 4, :] = second


def load_tiles(source):
    tiles = source.shape[1] // 12
    rows = []
    for k in range(source.shape[0]):
        for t in range(tiles):
            low = source[k, 8 * tiles + 4 * t : 8 * tiles + 4 * t + 4, :]
            rows.append(jnp.concatenate([source[k, 8 * t : 8 * t + 8, :], low], axis=0))
    return jnp.concatenate(rows, axis=1)


def pick_kernel(vol, pick, out, table):
    width = vol.shape[1]
    lows = width // LANE
    rows = vol[...]
    fill_table(
        jnp.concatenate([rows[3 * c + j : 3 * c + j + 1] for j in range(3) for c in range(4)], axis=0),
        table,
    )
    count, tiles, _ = out.shape
    part = width // count
    for k in range(count):
        first, second = pick_table(table[...], pick[:, k * part : (k + 1) * part], lows)
        for t in range(tiles // 12):
            store_tile(out, k, t, first[:, t * 128 : (t + 1) * 128], second[:, t * 128 : (t + 1) * 128])


def lane_iota(rows, cols):
    return lax.broadcasted_iota(jnp.int32, (rows, cols), 1)


def sort_terms(values, place, lows):
    pieces = []
    for value in values:
        pieces += split(jnp.concatenate([value] * 4, axis=0))
    stacked = jnp.concatenate(sum(spread(quotient(place, LANE), pieces, 4, lows), []), axis=0)
    return lax.dot_general(stacked, onehot(remainder(place, LANE), LANE), NT, preferred_element_type=F32)


def sort_parts(values, place, total):
    per = place.shape[1] // PARTS
    each = total.shape[0] // PARTS

    def body(p, _):
        lanes = pl.ds(pl.multiple_of(p * per, per), per)
        rows = pl.ds(pl.multiple_of(p * each, each), each)
        total[rows, :] = sort_terms(values(lanes), remainder(place[:, lanes], per), per // LANE)
        return 0

    lax.fori_loop(0, PARTS, body, 0)


def sorted_sums(total, lows):
    rows, each = 4 * lows, total.shape[0] // PARTS
    sums = []
    for i in range(0, each, 2 * rows):
        parts = []
        for at in range(i, total.shape[0], each):
            parts.append(total[at : at + rows] + total[at + rows : at + 2 * rows])
        sums.append(jnp.concatenate(parts, axis=0))
    return sums


def cut_windows(sums, offsets, ordered, out, masked):
    top = sub_iota(8, 128) < 4
    groups = sums.shape[0] // 8
    left = [sums[8 * g : 8 * g + 8, 0:128] for g in range(groups)]
    right = [sums[8 * g : 8 * g + 8, 128:256] for g in range(groups)]
    turned_left = [pltpu.roll(v, 4, 0) for v in left] + [jnp.zeros((8, 128), F32)]
    turned_right = [pltpu.roll(v, 4, 0) for v in right]
    for g in range(groups):
        ordered[4 * g] = jnp.where(top, left[g], turned_right[g])
        ordered[4 * g + 1] = jnp.where(top, right[g], left[g])
        ordered[4 * g + 2] = jnp.where(top, turned_left[g], right[g])
        ordered[4 * g + 3] = jnp.where(top, turned_right[g], turned_left[g + 1])
    for g in range(4 * groups, ordered.shape[0]):
        ordered[g] = jnp.zeros((8, 128), F32)
    lane = lane_iota(8, 128)
    number = lane + jnp.where(top, 0, 128)

    def cut(start):
        block, shift = quotient(start, 128), remainder(start, 128)
        joined = jnp.where(lane >= shift, ordered[block], ordered[block + 1])
        return pltpu.roll(joined, remainder(128 - shift, 128), 1)

    for o in range(out.shape[0]):
        later = offsets[1, o + 1]
        back = cut(later - 256)
        if masked:
            back = jnp.where(number >= 256 + offsets[1, o] - later, back, 0.0)
        start = offsets[0, o]
        out[o] = jnp.where(number < offsets[0, o + 1] - start, cut(start), back)


def merge_windows(windows, offsets, merged, lows):
    lane = lane_iota(8, 128)
    top = sub_iota(8, 128) < 4
    owners = windows.shape[0]
    per = 2 * lows // PARTS
    gap = 8

    def shifted(o, shift):
        value = pltpu.roll(windows[o], shift, 1)
        other = pltpu.roll(value, 4, 0)
        return jnp.where(top, value, other), jnp.where(top, other, value)

    def window(i, carry):
        front, back = carry
        for u in range(UNROLL):
            o = i * UNROLL + u
            start, later = offsets[0, o], offsets[0, o + 1]
            block, shift = quotient(start, 128), remainder(start, 128)
            one, two = shifted(o, shift)
            first = jnp.where(lane >= shift, one, front)
            second = jnp.where(lane >= shift, two, one)
            merged[block] = first
            merged[block + 1] = second
            merged[block + 2] = two
            ahead = quotient(later, 128) - block
            front = jnp.where(ahead == 0, first, jnp.where(ahead == 1, second, two))
            o = owners - 1 - o
            start, later = offsets[1, o], offsets[1, o + 1]
            block, shift = quotient(later, 128) + gap, remainder(later, 128)
            one, two = shifted(o, shift)
            second = jnp.where(lane >= shift, two, one)
            third = jnp.where(lane >= shift, back, two)
            merged[block - 2] = one
            merged[block - 1] = second
            merged[block] = third
            behind = block - gap - quotient(start, 128)
            back = jnp.where(behind == 0, third, jnp.where(behind == 1, second, one))
        return front, back

    zero = jnp.zeros((8, 128), F32)
    lax.fori_loop(0, owners // UNROLL, window, (zero, zero))
    left, right = [], []
    for g in range(lows // 2):
        at = 4 * g if 4 * g < per else 4 * g + gap
        left.append(jnp.where(top, merged[at], merged[at + 2]))
        right.append(jnp.where(top, merged[at + 1], merged[at + 3]))
    return jnp.concatenate([jnp.concatenate(left, axis=0), jnp.concatenate(right, axis=0)], axis=1)


def request_kernel(step, owner, slot, normal, out, place, offset, total, named, before, ordered, scalars, sem):
    count = owner.shape[1]
    owners = out.shape[0]
    lows = count // PARTS // LANE
    groups = owners // 16

    def lookup(names, columns):
        found = names[0:16] * columns[0:16]
        for g in range(1, groups):
            found = found + names[16 * g : 16 * g + 16] * columns[16 * g : 16 * g + 16]
        return found

    def tally(i, sums):
        for u in range(step // 256):
            lanes = pl.ds(pl.multiple_of(i * step + u * 256, 256), 256)
            names = onehot(owner[:, lanes], owners)
            named[:, lanes] = names
            before[:, lanes] = lookup(names, sums)
            sums = sums + names
        return sums

    lower = (sub_iota(owners, owners) > lane_iota(owners, owners)).astype(F32).astype(BF)
    upper = (sub_iota(256, 256) < lane_iota(256, 256)).astype(F32).astype(BF)
    wide = (sub_iota(owners, 2 * owners) < lane_iota(owners, 2 * owners)).astype(F32).astype(BF)
    per = count // PARTS
    bases, starts = [], []
    for p in range(PARTS):
        sums = lax.fori_loop(p * per // step, (p + 1) * per // step, tally, jnp.zeros((owners, 256), BF))
        counts = lax.dot_general(sums, jnp.ones((256, 256), BF), NN, preferred_element_type=F32).astype(BF)
        base = lax.dot_general(lower, counts, NN, preferred_element_type=F32)
        bases.append(split(base + lax.dot_general(sums, upper, NN, preferred_element_type=F32)))
        counts = lax.dot_general(jnp.ones((16, 256), BF), sums, NT, preferred_element_type=F32).astype(BF)
        starts.append(lax.dot_general(counts, wide, NN, preferred_element_type=F32)[0:8] + 1.0 * p * per)
    offset[...] = jnp.where(sub_iota(8, 2 * owners) == 0, starts[0], starts[1]).astype(jnp.int32)
    save = pltpu.make_async_copy(offset, scalars, sem)
    save.start()

    for p in range(PARTS):

        def ranks(i, _):
            for u in range(step // 256):
                lanes = pl.ds(pl.multiple_of(i * step + u * 256, 256), 256)
                names = named[:, lanes]
                found = lookup(names, bases[p][0]).astype(F32)
                found = found + (before[:, lanes] + lookup(names, bases[p][1])).astype(F32)
                found = jnp.sum(found, axis=0, keepdims=True) + 1.0 * p * per
                place[:, lanes] = found.astype(jnp.int32)
            return 0

        lax.fori_loop(p * per // step, (p + 1) * per // step, ranks, 0)

    sort_parts(lambda lanes: [jnp.concatenate([slot[:, lanes].astype(F32), normal[:, lanes]], axis=0)], place, total)
    save.wait()
    cut_windows(sorted_sums(total, lows)[0], scalars, ordered, out, True)


def along_kernel(group, surf, recv, out, table):
    lows = table.shape[0] // 24
    fill_table(load_tiles(surf), table)

    def step(i, _):
        parts = [recv[i * group + u] for u in range(group)]
        block = jnp.concatenate([p[4 * h : 4 * h + 4] for p in parts for h in range(2)], axis=1)
        index = block[0:1].astype(jnp.int32)
        first, second = pick_table(table[...], index, lows)
        along = first[0:4] * block[1:2] + first[4:8] * block[2:3] + second * block[3:4]
        for u in range(group):
            for h in range(2):
                at = (2 * u + h) * 128
                out[i * group + u, 4 * h : 4 * h + 4, :] = along[:, at : at + 128]
        return 0

    lax.fori_loop(0, recv.shape[0] // group, step, 0)


def by_node(values, number):
    result = jnp.full(number.shape, values[3], F32)
    for c in range(3):
        result = jnp.where(number == c, values[c], result)
    return result


def turned(values, by):
    if by % 4 == 0:
        return values
    by = by % 4
    row = lax.broadcasted_iota(jnp.int32, values.shape, 1) % 4
    return jnp.where(row < 4 - by, pltpu.roll(values, 8 - by, 1), pltpu.roll(values, 4 - by, 1))


def sort_kernel(place, proj, out, total):
    def values(lanes):
        p = proj[:, lanes]
        return [jnp.concatenate([p[2 * q + k : 2 * q + k + 1] for q in range(4)], axis=0) for k in range(2)]

    sort_parts(values, place, total)
    for k, value in enumerate(sorted_sums(total, place.shape[1] // PARTS // LANE)):
        out[k] = value


def local_kernel(place, disp, normal, gap, weight, multiplier, active, proj, part, factors, total):
    sub4 = sub_iota(4, 1)

    def values(lanes):
        w, d, n, g = weight[:, lanes], disp[:, lanes], normal[:, lanes], gap[:, lanes]
        points = g
        for b in range(4):
            along = n[0:1] * d[3 * b : 3 * b + 1] + n[1:2] * d[3 * b + 1 : 3 * b + 2] + n[2:3] * d[3 * b + 2 : 3 * b + 3]
            points = points + by_node(slave_table[b], sub4) * along
        points = w * points
        result = by_node([slave_table[a][0] for a in range(4)], sub4) * points[0:1]
        for q in range(1, 4):
            result = result + by_node([slave_table[a][q] for a in range(4)], sub4) * points[q : q + 1]
        part[:, lanes] = result
        start = jnp.where(active[:, lanes] == 1, multiplier[:, lanes] - result, -1e30)
        return [w, start]

    sort_parts(values, place, total)
    w, start = sorted_sums(total, place.shape[1] // PARTS // LANE)
    factors[4] = start
    first, second, w = [v.reshape(-1, 8, LANE) for v in (proj[0], proj[1], w)]
    row = lax.broadcasted_iota(jnp.int32, (1, 8, 1), 1) % 4
    sums = [None] * 4
    for e in range(4):
        x, y = turned(first, e), turned(second, e)
        scaled = turned(w, e) * by_node([slave_table[a][(a + e) % 4] * 0.25 for a in range(4)], row)
        for d in range(4):
            node = (row + d) % 4
            term = (1.0 + by_node(node_xs, node) * x) * (1.0 + by_node(node_ys, node) * y) * scaled
            sums[d] = term if e == 0 else sums[d] + term
    for d in range(4):
        factors[d] = sums[d].reshape(-1, LANE)


def update_kernel(recv, offsets_hbm, factors_hbm, out, mortar_out, offsets, factors, ordered, sems):
    copies = [
        pltpu.make_async_copy(a, b, sems.at[i])
        for i, (a, b) in enumerate(((offsets_hbm, offsets), (factors_hbm, factors)))
    ]
    for copy in copies:
        copy.start()
    copies[0].wait()
    lows = factors.shape[1] // 4
    along = merge_windows(recv, offsets, ordered, lows).reshape(-1, 8, LANE)
    copies[1].wait()
    parts = [factors[d].reshape(-1, 8, LANE) for d in range(4)]
    mortar = parts[0] * along
    for d in range(1, 4):
        mortar = mortar + parts[d] * turned(along, d)
    mortar_out[...] = mortar.reshape(-1, LANE)
    lagrange = jnp.maximum(factors[4].reshape(-1, 8, LANE) + mortar, 0.0)
    terms = parts[0] * lagrange
    for d in range(1, 4):
        terms = terms + turned(parts[d] * lagrange, 4 - d)
    cut_windows(terms.reshape(-1, LANE), offsets, ordered, out, False)


def restore_kernel(mortar, place, part, multiplier, active, gap_out, new_out, table):
    per = place.shape[1] // PARTS
    lows = per // LANE
    rows = 4 * lows
    for p in range(PARTS):
        high, low = split(mortar[p * rows : (p + 1) * rows])
        table[p, 0:rows, :] = high
        table[p, rows:, :] = low

    def body(p, _):
        lanes = pl.ds(pl.multiple_of(p * per, per), per)
        places = remainder(place[:, lanes], per)
        grabbed = grab(table[p], remainder(places, LANE), True)
        base = jnp.broadcast_to(quotient(places, LANE), (8, per)) - sub_iota(8, per) // 4
        found = jnp.zeros((8, per), F32)
        for g in range(lows // 2):
            found = jnp.where(base == 2 * g, grabbed[8 * g : 8 * g + 8], found)
        weighted = part[:, lanes] - (found[0:4] + found[4:8])
        gap_out[:, lanes] = weighted
        new_out[:, lanes] = jnp.where(active[:, lanes] == 1, jnp.maximum(multiplier[:, lanes] - weighted, 0.0), 0.0)
        return 0

    lax.fori_loop(0, PARTS, body, 0)


def force_kernel(group, recv, factor, out, total):
    lows = total.shape[0] // 24
    total[...] = jnp.zeros_like(total)

    def step(i, _):
        parts = [recv[i * group + u] for u in range(group)]
        block = jnp.concatenate([p[4 * h : 4 * h + 4] for p in parts for h in range(2)], axis=1)
        parts = [factor[i * group + u] for u in range(group)]
        node = jnp.concatenate([p[4 * h : 4 * h + 4] for p in parts for h in range(2)], axis=1)
        index = block[0:1].astype(jnp.int32)
        first = jnp.concatenate([node * block[1:2], node * block[2:3]], axis=0)
        total[...] += add_table(first, node * block[3:4], index, lows)
        return 0

    lax.fori_loop(0, recv.shape[0] // group, step, 0)
    sums = total[...]
    per = lows // out.shape[0]
    for l in range(lows):
        first, second = table_part(sums, lows, l)
        for t in range(LANE // 128):
            lanes = slice(t * 128, (t + 1) * 128)
            store_tile(out, l // per, l % per * (LANE // 128) + t, first[:, lanes], second[:, lanes])


def place_kernel(moved, pick, out):
    lows = out.shape[1] // LANE
    rows = load_tiles(moved)
    sums = add_table(rows[0:8], rows[8:12], pick[...], lows)
    for l in range(lows):
        first, second = table_part(sums, lows, l)
        both = jnp.concatenate([first, second], axis=0)
        ordered = jnp.concatenate(
            [both[4 * j + c : 4 * j + c + 1] for c in range(4) for j in range(3)], axis=0
        )
        out[:, l * LANE : (l + 1) * LANE] = ordered


def call(kernel, ins, outs, scratch, cycles, *args, mebibytes=48):
    size = sum(a.size * 4 for a in args) + sum(math.prod(o[0]) * 4 for o in outs)
    spaces = {"v": pltpu.VMEM, "h": pl.ANY}
    places = [pl.BlockSpec(memory_space=spaces[p]) for p in ins]
    result = pl.pallas_call(
        kernel,
        out_shape=[jax.ShapeDtypeStruct(*o) for o in outs],
        in_specs=places[: len(args)],
        out_specs=places[len(args) :],
        scratch_shapes=scratch,
        compiler_params=pltpu.CompilerParams(vmem_limit_bytes=mebibytes * 2**20),
        cost_estimate=pl.CostEstimate(flops=cycles, bytes_accessed=size, transcendentals=0),
    )(*args)
    return result[0] if len(outs) == 1 else result


def on_device(
    slave_disp,
    slave_normal,
    gap_zero,
    quad_weight,
    proj_coord,
    multiplier,
    active,
    pair_owner,
    pair_slot,
    master_vol,
    surf_pick,
):
    region_count = lax.axis_size("region")
    dom_count = lax.axis_size("dom")
    owners = region_count * dom_count
    count = slave_disp.shape[1]
    width = master_vol.shape[1]
    lows = width // LANE
    part = width // dom_count
    step = 4096
    blocks = count // LANE
    exchange = functools.partial(lax.all_to_all, split_axis=0, concat_axis=0, tiled=True)
    owner = pair_owner.reshape(1, count)
    flat = (owners, 8, 128)
    everyone = ("region", "dom")
    whole, quad = (1, count), (4, count)

    table = pltpu.VMEM((24 * lows, LANE), BF)
    picked = call(pick_kernel, "vvv", [((dom_count, 12 * part // 128, 128), F32)], [table], 10**9, master_vol, surf_pick, mebibytes=60)
    surf = exchange(picked, "dom")
    request, place, offset = call(
        functools.partial(request_kernel, 2 * step),
        "vvvvvv",
        [(flat, F32), (whole, jnp.int32), ((8, 2 * owners), jnp.int32)],
        [
            pltpu.VMEM((8 * blocks, LANE), F32),
            pltpu.VMEM((owners, count), BF),
            pltpu.VMEM((16, count), BF),
            pltpu.VMEM((2 * blocks + 4, 8, 128), F32),
            pltpu.SMEM((8, 2 * owners), jnp.int32),
            pltpu.SemaphoreType.DMA,
        ],
        10**10,
        owner,
        pair_slot.reshape(1, count),
        slave_normal,
    )
    recv = exchange(request, everyone)
    sorted_proj = call(
        sort_kernel,
        "vvv",
        [((2, 4 * blocks, LANE), F32)],
        [pltpu.VMEM((16 * blocks, LANE), F32)],
        10**10,
        place,
        proj_coord,
        mebibytes=56,
    )
    surf, sorted_proj = lax.optimization_barrier((surf, sorted_proj))
    along = call(functools.partial(along_kernel, 64), "vvv", [(flat, F32)], [table], 10**10, surf, recv)
    returned = exchange(along, everyone)
    along, sorted_proj = lax.optimization_barrier((along, sorted_proj))
    slave_part, factors = call(
        local_kernel,
        "v" * 10,
        [(quad, F32), ((5, 4 * blocks, LANE), F32)],
        [pltpu.VMEM((16 * blocks, LANE), F32)],
        10**10,
        place,
        slave_disp,
        slave_normal,
        gap_zero,
        quad_weight,
        multiplier,
        active,
        sorted_proj,
        mebibytes=56,
    )
    terms, mortar = call(
        update_kernel,
        "vhhvv",
        [(flat, F32), ((4 * blocks, LANE), F32)],
        [
            pltpu.SMEM((8, 2 * owners), jnp.int32),
            pltpu.VMEM((5, 4 * blocks, LANE), F32),
            pltpu.VMEM((2 * blocks + 12, 8, 128), F32),
            pltpu.SemaphoreType.DMA((2,)),
        ],
        10**9,
        returned,
        offset,
        factors,
        mebibytes=52,
    )
    factor = exchange(terms, everyone)
    weighted_gap, multiplier_new = call(
        restore_kernel,
        "v" * 7,
        [(quad, F32), (quad, F32)],
        [pltpu.VMEM((PARTS, 8 * blocks // PARTS, LANE), BF)],
        10**10,
        mortar,
        place,
        slave_part,
        multiplier,
        active,
        mebibytes=48,
    )
    recv, weighted_gap = lax.optimization_barrier((recv, weighted_gap))
    forces = call(
        functools.partial(force_kernel, 128),
        "vvv",
        [((dom_count, 12 * part // 128, 128), F32)],
        [pltpu.VMEM((24 * lows, LANE), F32)],
        10**10,
        recv,
        factor,
    )
    moved = exchange(forces, "dom")
    master_force = call(place_kernel, "vvv", [((12, width), F32)], [], 10**9, moved, surf_pick)
    return (weighted_gap, multiplier_new, master_force)


def solution(mesh):
    both = ("region", "dom")
    return jax.shard_map(
        on_device,
        mesh=mesh,
        in_specs=(P(None, both),) * 7 + (P(both, None), P(both), P(None, both), P(both, None)),
        out_specs=(P(None, both),) * 3,
        check_vma=False,
    )
```

```python
import functools
import math

import jax
import jax.numpy as jnp
from jax import lax
from jax.experimental import pallas as pl
from jax.experimental.pallas import tpu as pltpu
from jax.sharding import PartitionSpec as P

gauss_point = 1.0 / math.sqrt(3.0)
node_xs = [-1.0, 1.0, 1.0, -1.0]
node_ys = [-1.0, -1.0, 1.0, 1.0]
point_xs = [-gauss_point, gauss_point, gauss_point, -gauss_point]
point_ys = [-gauss_point, -gauss_point, gauss_point, gauss_point]
slave_table = [
    [(1.0 + node_xs[c] * point_xs[q]) * (1.0 + node_ys[c] * point_ys[q]) * 0.25 for q in range(4)]
    for c in range(4)
]

BF = jnp.bfloat16
F32 = jnp.float32
LANE = 256

UNROLL = 128
PARTS = 2
NN = (((1,), (0,)), ((), ()))
NT = (((1,), (1,)), ((), ()))


def sub_iota(rows, cols):
    return lax.broadcasted_iota(jnp.int32, (rows, cols), 0)


def quotient(value, by):
    return lax.shift_right_logical(value, jnp.int32(by.bit_length() - 1))


def remainder(value, by):
    return lax.bitwise_and(value, jnp.int32(by - 1))


def split(values):
    high = values.astype(BF)
    return high, (values - high.astype(F32)).astype(BF)


def onehot(index, size):
    n = index.shape[1]
    base = (jnp.broadcast_to(index, (16, n)) - sub_iota(16, n)).astype(F32).astype(BF)
    one, zero = jnp.ones((16, n), BF), jnp.zeros((16, n), BF)
    return jnp.concatenate(
        [jnp.where(base == jnp.asarray(16 * g, BF), one, zero) for g in range(size // 16)], axis=0
    )


def grab(table, index, apart):
    half = table.shape[0] // 2
    hot = onehot(index, LANE)
    if apart:
        first = lax.dot_general(table[0:half], hot, NN, preferred_element_type=F32)
        return first + lax.dot_general(table[half:], hot, NN, preferred_element_type=F32)
    found = lax.dot_general(table, hot, NN, preferred_element_type=F32)
    return found[0:half] + found[half:]


def spread(index, values, group, count):
    n = index.shape[1]
    base = (jnp.broadcast_to(index, (16, n)) - sub_iota(16, n) // (16 // group)).astype(F32).astype(BF)
    zero = jnp.zeros((16, n), BF)
    return [
        [jnp.where(base == jnp.asarray(group * g, BF), v, zero) for g in range(count // group)]
        for v in values
    ]


def fill_table(rows, table):
    lows = rows.shape[1] // LANE
    parts = [rows[0:8, l * LANE : (l + 1) * LANE] for l in range(lows)]
    parts += [rows[8:12, l * LANE : (l + 1) * LANE] for l in range(lows)]
    high, low = split(jnp.concatenate(parts, axis=0))
    table[0 : 12 * lows, :] = high
    table[12 * lows :, :] = low


def pick_table(table, index, lows):
    n = index.shape[1]
    grabbed = grab(table, remainder(index, LANE), False)
    low = jnp.broadcast_to(quotient(index, LANE), (8, n))
    pair = low - sub_iota(8, n) // 4
    first = jnp.zeros((8, n), F32)
    for l in range(lows):
        at = 8 * l
        value = grabbed[at : at + 8]
        first = jnp.where(low == l, value, first)
    second = jnp.zeros((8, n), F32)
    for l in range(lows // 2):
        at = 8 * lows + 8 * l
        value = grabbed[at : at + 8]
        second = jnp.where(pair == 2 * l, value, second)
    return first, second[0:4] + second[4:8]


def add_table(first, second, index, lows):
    high, low = split(first)
    group = jnp.concatenate([high.astype(F32), low.astype(F32)], axis=0).astype(BF)
    wide = spread(quotient(index, LANE), [group], 1, lows)[0]
    high, low = split(second)
    high, low = high.astype(F32), low.astype(F32)
    group = jnp.concatenate([high, low, high, low], axis=0).astype(BF)
    narrow = spread(quotient(index, LANE), [group], 2, lows)[0]
    stacked = jnp.concatenate(wide + narrow, axis=0)
    return lax.dot_general(
        stacked, onehot(remainder(index, LANE), LANE), NT, preferred_element_type=F32
    )


def table_part(total, lows, l):
    first = total[16 * l : 16 * l + 8] + total[16 * l + 8 : 16 * l + 16]
    at = 16 * lows + 8 * l
    return first, total[at : at + 4] + total[at + 4 : at + 8]


def store_tile(out, k, t, first, second):
    tiles = out.shape[1] // 12
    out[k, 8 * t : 8 * t + 8, :] = first
    out[k, 8 * tiles + 4 * t : 8 * tiles + 4 * t + 4, :] = second


def load_tiles(source):
    tiles = source.shape[1] // 12
    rows = []
    for k in range(source.shape[0]):
        for t in range(tiles):
            low = source[k, 8 * tiles + 4 * t : 8 * tiles + 4 * t + 4, :]
            rows.append(jnp.concatenate([source[k, 8 * t : 8 * t + 8, :], low], axis=0))
    return jnp.concatenate(rows, axis=1)


def pick_kernel(vol, pick, out, table):
    width = vol.shape[1]
    lows = width // LANE
    rows = vol[...]
    fill_table(
        jnp.concatenate([rows[3 * c + j : 3 * c + j + 1] for j in range(3) for c in range(4)], axis=0),
        table,
    )
    count, tiles, _ = out.shape
    part = width // count
    for k in range(count):
        first, second = pick_table(table[...], pick[:, k * part : (k + 1) * part], lows)
        for t in range(tiles // 12):
            store_tile(out, k, t, first[:, t * 128 : (t + 1) * 128], second[:, t * 128 : (t + 1) * 128])


def lane_iota(rows, cols):
    return lax.broadcasted_iota(jnp.int32, (rows, cols), 1)


def sort_terms(values, place, lows):
    pieces = []
    for value in values:
        pieces += split(jnp.concatenate([value] * 4, axis=0))
    stacked = jnp.concatenate(sum(spread(quotient(place, LANE), pieces, 4, lows), []), axis=0)
    return lax.dot_general(stacked, onehot(remainder(place, LANE), LANE), NT, preferred_element_type=F32)


def sort_parts(values, place, total):
    per = place.shape[1] // PARTS
    each = total.shape[0] // PARTS

    def body(p, _):
        lanes = pl.ds(pl.multiple_of(p * per, per), per)
        rows = pl.ds(pl.multiple_of(p * each, each), each)
        total[rows, :] = sort_terms(values(lanes), remainder(place[:, lanes], per), per // LANE)
        return 0

    lax.fori_loop(0, PARTS, body, 0)


def sorted_sums(total, lows):
    rows, each = 4 * lows, total.shape[0] // PARTS
    sums = []
    for i in range(0, each, 2 * rows):
        parts = []
        for at in range(i, total.shape[0], each):
            parts.append(total[at : at + rows] + total[at + rows : at + 2 * rows])
        sums.append(jnp.concatenate(parts, axis=0))
    return sums


def cut_windows(sums, offsets, ordered, out, masked):
    top = sub_iota(8, 128) < 4
    groups = sums.shape[0] // 8
    left = [sums[8 * g : 8 * g + 8, 0:128] for g in range(groups)]
    right = [sums[8 * g : 8 * g + 8, 128:256] for g in range(groups)]
    turned_left = [pltpu.roll(v, 4, 0) for v in left] + [jnp.zeros((8, 128), F32)]
    turned_right = [pltpu.roll(v, 4, 0) for v in right]
    for g in range(groups):
        ordered[4 * g] = jnp.where(top, left[g], turned_right[g])
        ordered[4 * g + 1] = jnp.where(top, right[g], left[g])
        ordered[4 * g + 2] = jnp.where(top, turned_left[g], right[g])
        ordered[4 * g + 3] = jnp.where(top, turned_right[g], turned_left[g + 1])
    for g in range(4 * groups, ordered.shape[0]):
        ordered[g] = jnp.zeros((8, 128), F32)
    lane = lane_iota(8, 128)
    number = lane + jnp.where(top, 0, 128)

    def cut(start):
        block, shift = quotient(start, 128), remainder(start, 128)
        joined = jnp.where(lane >= shift, ordered[block], ordered[block + 1])
        return pltpu.roll(joined, remainder(128 - shift, 128), 1)

    for o in range(out.shape[0]):
        later = offsets[1, o + 1]
        back = cut(later - 256)
        if masked:
            back = jnp.where(number >= 256 + offsets[1, o] - later, back, 0.0)
        start = offsets[0, o]
        out[o] = jnp.where(number < offsets[0, o + 1] - start, cut(start), back)


def merge_windows(windows, offsets, merged, lows):
    lane = lane_iota(8, 128)
    top = sub_iota(8, 128) < 4
    owners = windows.shape[0]
    per = 2 * lows // PARTS
    gap = 8

    def shifted(o, shift):
        value = pltpu.roll(windows[o], shift, 1)
        other = pltpu.roll(value, 4, 0)
        return jnp.where(top, value, other), jnp.where(top, other, value)

    def window(i, carry):
        front, back = carry
        for u in range(UNROLL):
            o = i * UNROLL + u
            start, later = offsets[0, o], offsets[0, o + 1]
            block, shift = quotient(start, 128), remainder(start, 128)
            one, two = shifted(o, shift)
            first = jnp.where(lane >= shift, one, front)
            second = jnp.where(lane >= shift, two, one)
            merged[block] = first
            merged[block + 1] = second
            merged[block + 2] = two
            ahead = quotient(later, 128) - block
            front = jnp.where(ahead == 0, first, jnp.where(ahead == 1, second, two))
            o = owners - 1 - o
            start, later = offsets[1, o], offsets[1, o + 1]
            block, shift = quotient(later, 128) + gap, remainder(later, 128)
            one, two = shifted(o, shift)
            second = jnp.where(lane >= shift, two, one)
            third = jnp.where(lane >= shift, back, two)
            merged[block - 2] = one
            merged[block - 1] = second
            merged[block] = third
            behind = block - gap - quotient(start, 128)
            back = jnp.where(behind == 0, third, jnp.where(behind == 1, second, one))
        return front, back

    zero = jnp.zeros((8, 128), F32)
    lax.fori_loop(0, owners // UNROLL, window, (zero, zero))
    left, right = [], []
    for g in range(lows // 2):
        at = 4 * g if 4 * g < per else 4 * g + gap
        left.append(jnp.where(top, merged[at], merged[at + 2]))
        right.append(jnp.where(top, merged[at + 1], merged[at + 3]))
    return jnp.concatenate([jnp.concatenate(left, axis=0), jnp.concatenate(right, axis=0)], axis=1)


def request_kernel(step, owner, slot, normal, out, place, offset, total, named, before, ordered, scalars, sem):
    count = owner.shape[1]
    owners = out.shape[0]
    lows = count // PARTS // LANE
    groups = owners // 16

    def lookup(names, columns):
        found = names[0:16] * columns[0:16]
        for g in range(1, groups):
            found = found + names[16 * g : 16 * g + 16] * columns[16 * g : 16 * g + 16]
        return found

    def tally(i, sums):
        for u in range(step // 256):
            lanes = pl.ds(pl.multiple_of(i * step + u * 256, 256), 256)
            names = onehot(owner[:, lanes], owners)
            named[:, lanes] = names
            before[:, lanes] = lookup(names, sums)
            sums = sums + names
        return sums

    lower = (sub_iota(owners, owners) > lane_iota(owners, owners)).astype(F32).astype(BF)
    upper = (sub_iota(256, 256) < lane_iota(256, 256)).astype(F32).astype(BF)
    wide = (sub_iota(owners, 2 * owners) < lane_iota(owners, 2 * owners)).astype(F32).astype(BF)
    per = count // PARTS
    bases, starts = [], []
    for p in range(PARTS):
        sums = lax.fori_loop(p * per // step, (p + 1) * per // step, tally, jnp.zeros((owners, 256), BF))
        counts = lax.dot_general(sums, jnp.ones((256, 256), BF), NN, preferred_element_type=F32).astype(BF)
        base = lax.dot_general(lower, counts, NN, preferred_element_type=F32)
        bases.append(split(base + lax.dot_general(sums, upper, NN, preferred_element_type=F32)))
        counts = lax.dot_general(jnp.ones((16, 256), BF), sums, NT, preferred_element_type=F32).astype(BF)
        starts.append(lax.dot_general(counts, wide, NN, preferred_element_type=F32)[0:8] + 1.0 * p * per)
    offset[...] = jnp.where(sub_iota(8, 2 * owners) == 0, starts[0], starts[1]).astype(jnp.int32)
    save = pltpu.make_async_copy(offset, scalars, sem)
    save.start()

    for p in range(PARTS):

        def ranks(i, _):
            for u in range(step // 256):
                lanes = pl.ds(pl.multiple_of(i * step + u * 256, 256), 256)
                names = named[:, lanes]
                found = lookup(names, bases[p][0]).astype(F32)
                found = found + (before[:, lanes] + lookup(names, bases[p][1])).astype(F32)
                found = jnp.sum(found, axis=0, keepdims=True) + 1.0 * p * per
                place[:, lanes] = found.astype(jnp.int32)
            return 0

        lax.fori_loop(p * per // step, (p + 1) * per // step, ranks, 0)

    sort_parts(lambda lanes: [jnp.concatenate([slot[:, lanes].astype(F32), normal[:, lanes]], axis=0)], place, total)
    save.wait()
    cut_windows(sorted_sums(total, lows)[0], scalars, ordered, out, True)


def along_kernel(group, surf, recv, out, table):
    lows = table.shape[0] // 24
    fill_table(load_tiles(surf), table)

    def step(i, _):
        parts = [recv[i * group + u] for u in range(group)]
        block = jnp.concatenate([p[4 * h : 4 * h + 4] for p in parts for h in range(2)], axis=1)
        index = block[0:1].astype(jnp.int32)
        first, second = pick_table(table[...], index, lows)
        along = first[0:4] * block[1:2] + first[4:8] * block[2:3] + second * block[3:4]
        for u in range(group):
            for h in range(2):
                at = (2 * u + h) * 128
                out[i * group + u, 4 * h : 4 * h + 4, :] = along[:, at : at + 128]
        return 0

    lax.fori_loop(0, recv.shape[0] // group, step, 0)


def by_node(values, number):
    result = jnp.full(number.shape, values[3], F32)
    for c in range(3):
        result = jnp.where(number == c, values[c], result)
    return result


def turned(values, by):
    if by % 4 == 0:
        return values
    by = by % 4
    row = lax.broadcasted_iota(jnp.int32, values.shape, 1) % 4
    return jnp.where(row < 4 - by, pltpu.roll(values, 8 - by, 1), pltpu.roll(values, 4 - by, 1))


def sort_kernel(place, proj, out, total):
    def values(lanes):
        p = proj[:, lanes]
        return [jnp.concatenate([p[2 * q + k : 2 * q + k + 1] for q in range(4)], axis=0) for k in range(2)]

    sort_parts(values, place, total)
    for k, value in enumerate(sorted_sums(total, place.shape[1] // PARTS // LANE)):
        out[k] = value


def local_kernel(place, disp, normal, gap, weight, multiplier, active, proj, part, factors, total):
    sub4 = sub_iota(4, 1)

    def values(lanes):
        w, d, n, g = weight[:, lanes], disp[:, lanes], normal[:, lanes], gap[:, lanes]
        points = g
        for b in range(4):
            along = n[0:1] * d[3 * b : 3 * b + 1] + n[1:2] * d[3 * b + 1 : 3 * b + 2] + n[2:3] * d[3 * b + 2 : 3 * b + 3]
            points = points + by_node(slave_table[b], sub4) * along
        points = w * points
        result = by_node([slave_table[a][0] for a in range(4)], sub4) * points[0:1]
        for q in range(1, 4):
            result = result + by_node([slave_table[a][q] for a in range(4)], sub4) * points[q : q + 1]
        part[:, lanes] = result
        start = jnp.where(active[:, lanes] == 1, multiplier[:, lanes] - result, -1e30)
        return [w, start]

    sort_parts(values, place, total)
    w, start = sorted_sums(total, place.shape[1] // PARTS // LANE)
    factors[4] = start
    first, second, w = [v.reshape(-1, 8, LANE) for v in (proj[0], proj[1], w)]
    row = lax.broadcasted_iota(jnp.int32, (1, 8, 1), 1) % 4
    sums = [None] * 4
    for e in range(4):
        x, y = turned(first, e), turned(second, e)
        scaled = turned(w, e) * by_node([slave_table[a][(a + e) % 4] * 0.25 for a in range(4)], row)
        for d in range(4):
            node = (row + d) % 4
            term = (1.0 + by_node(node_xs, node) * x) * (1.0 + by_node(node_ys, node) * y) * scaled
            sums[d] = term if e == 0 else sums[d] + term
    for d in range(4):
        factors[d] = sums[d].reshape(-1, LANE)


def update_kernel(recv, offsets_hbm, factors_hbm, out, mortar_out, offsets, factors, ordered, sems):
    copies = [
        pltpu.make_async_copy(a, b, sems.at[i])
        for i, (a, b) in enumerate(((offsets_hbm, offsets), (factors_hbm, factors)))
    ]
    for copy in copies:
        copy.start()
    copies[0].wait()
    lows = factors.shape[1] // 4
    along = merge_windows(recv, offsets, ordered, lows).reshape(-1, 8, LANE)
    copies[1].wait()
    parts = [factors[d].reshape(-1, 8, LANE) for d in range(4)]
    mortar = parts[0] * along
    for d in range(1, 4):
        mortar = mortar + parts[d] * turned(along, d)
    mortar_out[...] = mortar.reshape(-1, LANE)
    lagrange = jnp.maximum(factors[4].reshape(-1, 8, LANE) + mortar, 0.0)
    terms = parts[0] * lagrange
    for d in range(1, 4):
        terms = terms + turned(parts[d] * lagrange, 4 - d)
    cut_windows(terms.reshape(-1, LANE), offsets, ordered, out, False)


def restore_kernel(mortar, place, part, multiplier, active, gap_out, new_out, table):
    per = place.shape[1] // PARTS
    lows = per // LANE
    rows = 4 * lows
    for p in range(PARTS):
        high, low = split(mortar[p * rows : (p + 1) * rows])
        table[p, 0:rows, :] = high
        table[p, rows:, :] = low

    def body(p, _):
        lanes = pl.ds(pl.multiple_of(p * per, per), per)
        places = remainder(place[:, lanes], per)
        grabbed = grab(table[p], remainder(places, LANE), True)
        base = jnp.broadcast_to(quotient(places, LANE), (8, per)) - sub_iota(8, per) // 4
        found = jnp.zeros((8, per), F32)
        for g in range(lows // 2):
            found = jnp.where(base == 2 * g, grabbed[8 * g : 8 * g + 8], found)
        weighted = part[:, lanes] - (found[0:4] + found[4:8])
        gap_out[:, lanes] = weighted
        new_out[:, lanes] = jnp.where(active[:, lanes] == 1, jnp.maximum(multiplier[:, lanes] - weighted, 0.0), 0.0)
        return 0

    lax.fori_loop(0, PARTS, body, 0)


def force_kernel(group, recv, factor, out, total):
    lows = total.shape[0] // 24
    total[...] = jnp.zeros_like(total)

    def step(i, _):
        parts = [recv[i * group + u] for u in range(group)]
        block = jnp.concatenate([p[4 * h : 4 * h + 4] for p in parts for h in range(2)], axis=1)
        parts = [factor[i * group + u] for u in range(group)]
        node = jnp.concatenate([p[4 * h : 4 * h + 4] for p in parts for h in range(2)], axis=1)
        index = block[0:1].astype(jnp.int32)
        first = jnp.concatenate([node * block[1:2], node * block[2:3]], axis=0)
        total[...] += add_table(first, node * block[3:4], index, lows)
        return 0

    lax.fori_loop(0, recv.shape[0] // group, step, 0)
    sums = total[...]
    per = lows // out.shape[0]
    for l in range(lows):
        first, second = table_part(sums, lows, l)
        for t in range(LANE // 128):
            lanes = slice(t * 128, (t + 1) * 128)
            store_tile(out, l // per, l % per * (LANE // 128) + t, first[:, lanes], second[:, lanes])


def place_kernel(moved, pick, out):
    lows = out.shape[1] // LANE
    rows = load_tiles(moved)
    sums = add_table(rows[0:8], rows[8:12], pick[...], lows)
    for l in range(lows):
        first, second = table_part(sums, lows, l)
        both = jnp.concatenate([first, second], axis=0)
        ordered = jnp.concatenate(
            [both[4 * j + c : 4 * j + c + 1] for c in range(4) for j in range(3)], axis=0
        )
        out[:, l * LANE : (l + 1) * LANE] = ordered


def call(kernel, ins, outs, scratch, cycles, *args, mebibytes=48):
    size = sum(a.size * 4 for a in args) + sum(math.prod(o[0]) * 4 for o in outs)
    spaces = {"v": pltpu.VMEM, "h": pl.ANY}
    places = [pl.BlockSpec(memory_space=spaces[p]) for p in ins]
    result = pl.pallas_call(
        kernel,
        out_shape=[jax.ShapeDtypeStruct(*o) for o in outs],
        in_specs=places[: len(args)],
        out_specs=places[len(args) :],
        scratch_shapes=scratch,
        compiler_params=pltpu.CompilerParams(vmem_limit_bytes=mebibytes * 2**20),
        cost_estimate=pl.CostEstimate(flops=cycles, bytes_accessed=size, transcendentals=0),
    )(*args)
    return result[0] if len(outs) == 1 else result


def on_device(
    slave_disp,
    slave_normal,
    gap_zero,
    quad_weight,
    proj_coord,
    multiplier,
    active,
    pair_owner,
    pair_slot,
    master_vol,
    surf_pick,
):
    region_count = lax.axis_size("region")
    dom_count = lax.axis_size("dom")
    owners = region_count * dom_count
    count = slave_disp.shape[1]
    width = master_vol.shape[1]
    lows = width // LANE
    part = width // dom_count
    step = 4096
    blocks = count // LANE
    exchange = functools.partial(lax.all_to_all, split_axis=0, concat_axis=0, tiled=True)
    owner = pair_owner.reshape(1, count)
    flat = (owners, 8, 128)
    everyone = ("region", "dom")
    whole, quad = (1, count), (4, count)

    table = pltpu.VMEM((24 * lows, LANE), BF)
    picked = call(pick_kernel, "vvv", [((dom_count, 12 * part // 128, 128), F32)], [table], 10**9, master_vol, surf_pick, mebibytes=60)
    surf = exchange(picked, "dom")
    request, place, offset = call(
        functools.partial(request_kernel, 2 * step),
        "vvvvvv",
        [(flat, F32), (whole, jnp.int32), ((8, 2 * owners), jnp.int32)],
        [
            pltpu.VMEM((8 * blocks, LANE), F32),
            pltpu.VMEM((owners, count), BF),
            pltpu.VMEM((16, count), BF),
            pltpu.VMEM((2 * blocks + 4, 8, 128), F32),
            pltpu.SMEM((8, 2 * owners), jnp.int32),
            pltpu.SemaphoreType.DMA,
        ],
        10**10,
        owner,
        pair_slot.reshape(1, count),
        slave_normal,
    )
    recv = exchange(request, everyone)
    sorted_proj = call(
        sort_kernel,
        "vvv",
        [((2, 4 * blocks, LANE), F32)],
        [pltpu.VMEM((16 * blocks, LANE), F32)],
        10**10,
        place,
        proj_coord,
        mebibytes=56,
    )
    surf, sorted_proj = lax.optimization_barrier((surf, sorted_proj))
    along = call(functools.partial(along_kernel, 64), "vvv", [(flat, F32)], [table], 10**10, surf, recv)
    returned = exchange(along, everyone)
    along, sorted_proj = lax.optimization_barrier((along, sorted_proj))
    slave_part, factors = call(
        local_kernel,
        "v" * 10,
        [(quad, F32), ((5, 4 * blocks, LANE), F32)],
        [pltpu.VMEM((16 * blocks, LANE), F32)],
        10**10,
        place,
        slave_disp,
        slave_normal,
        gap_zero,
        quad_weight,
        multiplier,
        active,
        sorted_proj,
        mebibytes=56,
    )
    terms, mortar = call(
        update_kernel,
        "vhhvv",
        [(flat, F32), ((4 * blocks, LANE), F32)],
        [
            pltpu.SMEM((8, 2 * owners), jnp.int32),
            pltpu.VMEM((5, 4 * blocks, LANE), F32),
            pltpu.VMEM((2 * blocks + 12, 8, 128), F32),
            pltpu.SemaphoreType.DMA((2,)),
        ],
        10**9,
        returned,
        offset,
        factors,
        mebibytes=52,
    )
    factor = exchange(terms, everyone)
    weighted_gap, multiplier_new = call(
        restore_kernel,
        "v" * 7,
        [(quad, F32), (quad, F32)],
        [pltpu.VMEM((PARTS, 8 * blocks // PARTS, LANE), BF)],
        10**10,
        mortar,
        place,
        slave_part,
        multiplier,
        active,
        mebibytes=48,
    )
    recv, weighted_gap = lax.optimization_barrier((recv, weighted_gap))
    forces = call(
        functools.partial(force_kernel, 128),
        "vvv",
        [((dom_count, 12 * part // 128, 128), F32)],
        [pltpu.VMEM((24 * lows, LANE), F32)],
        10**10,
        recv,
        factor,
    )
    moved = exchange(forces, "dom")
    master_force = call(place_kernel, "vvv", [((12, width), F32)], [], 10**9, moved, surf_pick)
    return (weighted_gap, multiplier_new, master_force)


def solution(mesh):
    both = ("region", "dom")
    return jax.shard_map(
        on_device,
        mesh=mesh,
        in_specs=(P(None, both),) * 7 + (P(both, None), P(both), P(None, both), P(both, None)),
        out_specs=(P(None, both),) * 3,
        check_vma=False,
    )
```
